128 devices in a mesh: gx: 16 (over z_lo, x, core), gy: 8 (over y, z_hi).
Axes of the slice: x: 4, y: 4, z: 4 (z_hi: 2, z_lo: 2; z = z_hi * 2 + z_lo), core: 2. Of those that a mesh axis runs over, the one named last changes fastest.
Arguments:
- tokens: bfloat16 [4096, 8192], P('gy', 'gx'), may hold values from -6 to 6
- norm_gain: float32 [8192], replicated, may hold values from 0.1 to 1.9
- query_weight: bfloat16 [8192, 8192], P('gy', 'gx')
- kv_weight: bfloat16 [8192, 2048], P('gy')
- out_weight: bfloat16 [8192, 8192], P('gx', 'gy'), may hold values from -0.0625 to 0.0625
- lengths: int32 [8], P('gy'), may hold values from 1 to 512, as said below
Outputs:
- mixed: bfloat16 [4096, 8192], P('gy', 'gx')
The draws below stay inside these ranges and needn't reach their ends.
Inputs may be any that keep to these rules, and one draw needn't show every extreme that they name: `lengths`: some transcript has all 512 slots valid in every draw.
All inputs are finite; a program needn't handle non-finite values.
Results may differ from the reference program's by a relative error of at most 0.039.
Values may be sent and summed in bfloat16 or wider, within the bound.
No kernel may reach another device: no remote copies, remote signals or barrier semaphores. Data moves between devices by JAX's collectives and lax.ppermute only.
A program may use at most 128 MiB of HBM per device.

```python
import jax
import jax.numpy as jnp
from jax import lax

MODEL_WIDTH = 8192
QUERY_HEADS = 64
KEY_VALUE_HEADS = 8
HEAD_SIZE = 128
TRANSCRIPT_SLOTS = 512
TRANSCRIPT_COUNT = 8
TOKEN_SLOTS = 4096
N_GX = 16


def shared_keys(key):
    key_portion = jax.random.fold_in(key, 101)
    return jax.random.normal(key_portion, (MODEL_WIDTH, KEY_VALUE_HEADS * HEAD_SIZE), jnp.float32) * MODEL_WIDTH ** (-0.5)


def draw_kv_weight(key, part):
    key_matrix = shared_keys(key)
    key = jax.random.fold_in(key, 2)
    value_matrix = jax.random.normal(key, (MODEL_WIDTH, KEY_VALUE_HEADS * HEAD_SIZE), jnp.float32) * MODEL_WIDTH ** (-0.5)
    joined_heads = jnp.stack([key_matrix.reshape(MODEL_WIDTH, KEY_VALUE_HEADS, HEAD_SIZE), value_matrix.reshape(MODEL_WIDTH, KEY_VALUE_HEADS, HEAD_SIZE)], axis=2)
    return joined_heads.reshape(MODEL_WIDTH, 2 * KEY_VALUE_HEADS * HEAD_SIZE).astype(jnp.bfloat16)


def draw_query_weight(key, part):
    key = jax.random.fold_in(key, 3)
    own_part = jax.random.normal(key, (MODEL_WIDTH, QUERY_HEADS * HEAD_SIZE), jnp.float32) * MODEL_WIDTH ** (-0.5)
    return own_part.astype(jnp.bfloat16)


def draw_lengths(key, part):
    key = jax.random.fold_in(key, 5)
    drawn = jax.random.randint(key, (TRANSCRIPT_COUNT,), 1, TRANSCRIPT_SLOTS + 1, dtype=jnp.int32)
    full_spot = jax.random.randint(jax.random.fold_in(key, 6), (), 0, TRANSCRIPT_COUNT, dtype=jnp.int32)
    return jnp.where(jnp.arange(TRANSCRIPT_COUNT, dtype=jnp.int32) == full_spot, TRANSCRIPT_SLOTS, drawn).astype(jnp.int32)


def block_scale(own_key, extent, pieces, low, high):
    level = 1.0
    for position, parts in pieces:
        heights = jax.random.uniform(jax.random.fold_in(jax.random.fold_in(own_key, 6), position), (parts,), jnp.float32, low / len(pieces), high / len(pieces))
        level = level * jnp.repeat(jnp.exp(heights), extent[position] // parts).reshape((-1,) + (1,) * (len(extent) - 1 - position))
    return level


def noise(rng, dims, scale, limit, cuts=(), held_as=jnp.bfloat16):
    gain = block_scale(rng, dims, cuts, -0.22, 0.18) if cuts else 1.0
    entries = jax.random.normal(rng, dims, jnp.float32) * scale * gain
    return jnp.minimum(jnp.maximum(entries, -limit), limit).astype(held_as)


def setup_inputs(seed: int = 0) -> dict:
    seeds = jax.random.split(jax.random.key(seed), 7)
    tokens = noise(seeds[0], (TOKEN_SLOTS, MODEL_WIDTH), 1.0, 6.0, ((0, 8), (1, 16)))
    norm_gain = jnp.clip(1.0 + 0.18 * jax.random.normal(seeds[1], (MODEL_WIDTH,), jnp.float32), 0.1, 1.9)
    query_weight = draw_query_weight(jax.random.fold_in(seeds[6], 71), 0)
    kv_weight = draw_kv_weight(jax.random.fold_in(seeds[6], 71), 0)
    out_weight = noise(seeds[4], (QUERY_HEADS * HEAD_SIZE, MODEL_WIDTH), (QUERY_HEADS * HEAD_SIZE) ** -0.5, 0.0625, ((0, 16), (1, 8)))
    lengths = draw_lengths(jax.random.fold_in(seeds[6], 71), 0)
    return dict(tokens=tokens, norm_gain=norm_gain, query_weight=query_weight, kv_weight=kv_weight, out_weight=out_weight, lengths=lengths)


rope_base = 500000.0
norm_eps = 1e-05

def apply_rope(vectors, positions):
    half_dim = vectors.shape[-1] // 2
    steps_up = jnp.arange(0, half_dim, dtype=jnp.float32) * (2.0 / vectors.shape[-1])
    inverse = jnp.power(jnp.float32(rope_base), -steps_up)
    angles = positions.astype(jnp.float32)[:, None] * inverse[None, :]
    cosine = jnp.cos(angles)[:, None, :]
    sine_part = jnp.sin(angles)[:, None, :]
    low_half = vectors[..., :half_dim]
    high_half = vectors[..., half_dim:]
    return jnp.concatenate([low_half * cosine - high_half * sine_part, high_half * cosine + low_half * sine_part], axis=-1)

def reference(tokens, norm_gain, query_weight, kv_weight, out_weight, lengths):
    wide_rows = tokens.astype(jnp.float32)
    square_mean = lax.optimization_barrier(jnp.mean(wide_rows * wide_rows, axis=-1, keepdims=True))
    normed = (wide_rows * lax.rsqrt(square_mean + norm_eps) * norm_gain[None, :]).astype(jnp.bfloat16)
    projected = jnp.dot(normed, query_weight, preferred_element_type=jnp.float32)
    key_value_projected = jnp.dot(normed, kv_weight, preferred_element_type=jnp.float32)
    positions = jnp.arange(TOKEN_SLOTS, dtype=jnp.int32) % TRANSCRIPT_SLOTS
    query_rows = apply_rope(projected.reshape(TOKEN_SLOTS, QUERY_HEADS, HEAD_SIZE), positions).astype(jnp.bfloat16)
    key_value_divided = key_value_projected.reshape(TOKEN_SLOTS, KEY_VALUE_HEADS, 2, HEAD_SIZE)
    key_row_stack = apply_rope(key_value_divided[:, :, 0, :], positions).astype(jnp.bfloat16)
    value_row_stack = key_value_divided[:, :, 1, :].astype(jnp.bfloat16)
    query_group_count = QUERY_HEADS // KEY_VALUE_HEADS

    def transcript_wise(operands):
        query_block, key_block, value_block, valid = operands
        scores = jnp.einsum('qhgd,khd->hgqk', query_block.astype(jnp.float32), key_block.astype(jnp.float32)) / jnp.sqrt(jnp.float32(HEAD_SIZE))
        slot_q = jnp.arange(TRANSCRIPT_SLOTS, dtype=jnp.int32)[:, None]
        slot_k = jnp.arange(TRANSCRIPT_SLOTS, dtype=jnp.int32)[None, :]
        allowed_mask = (slot_k <= slot_q) & (slot_k < valid)
        scores = jnp.where(allowed_mask[None, None], scores, -jnp.inf)
        top_score = lax.optimization_barrier(jnp.max(scores, axis=-1, keepdims=True))
        expd = jnp.exp(scores - top_score)
        probs = (expd / lax.optimization_barrier(jnp.sum(expd, axis=-1, keepdims=True))).astype(jnp.bfloat16)
        attended_output = jnp.einsum('hgqk,khd->qhgd', probs.astype(jnp.float32), value_block.astype(jnp.float32))
        return attended_output.astype(jnp.bfloat16).reshape(TRANSCRIPT_SLOTS, QUERY_HEADS * HEAD_SIZE)
    attended_output = lax.map(transcript_wise, (query_rows.reshape(TRANSCRIPT_COUNT, TRANSCRIPT_SLOTS, KEY_VALUE_HEADS, query_group_count, HEAD_SIZE), key_row_stack.reshape(TRANSCRIPT_COUNT, TRANSCRIPT_SLOTS, KEY_VALUE_HEADS, HEAD_SIZE), value_row_stack.reshape(TRANSCRIPT_COUNT, TRANSCRIPT_SLOTS, KEY_VALUE_HEADS, HEAD_SIZE), lengths))
    attended_output = attended_output.reshape(TOKEN_SLOTS, QUERY_HEADS * HEAD_SIZE)
    group_width = QUERY_HEADS * HEAD_SIZE // N_GX

    def add_group(running, group_index):
        first_col = (group_index * group_width).astype(jnp.int32)
        attn_part = lax.dynamic_slice_in_dim(attended_output, first_col, group_width, 1)
        weight_part = lax.dynamic_slice_in_dim(out_weight, first_col, group_width, 0)
        partial_g = lax.optimization_barrier(jnp.dot(attn_part, weight_part, preferred_element_type=jnp.float32).astype(jnp.bfloat16))
        return (running + partial_g.astype(jnp.float32), None)
    summed, _ = lax.scan(add_group, jnp.zeros((TOKEN_SLOTS, MODEL_WIDTH), jnp.float32), jnp.arange(N_GX, dtype=jnp.int32))
    return (wide_rows + summed).astype(jnp.bfloat16)
```

```python
import jax
import jax.numpy as jnp
from jax import lax
from jax.sharding import Mesh, PartitionSpec as P

HEAD_SIZE = 128
SLOTS = 512
HALF = 256
AXES = ("zl", "x", "core", "y", "zh")
SIZES = (2, 4, 2, 4, 2)

rope_base = 500000.0
norm_eps = 1e-05


def coords(i):
    out = {}
    for name, size in zip(AXES[::-1], SIZES[::-1]):
        i, out[name] = divmod(i, size)
    return out


def index(c):
    i = 0
    for name, size in zip(AXES, SIZES):
        i = i * size + c[name] % size
    return i


def pairs(change):
    out = []
    for i in range(128):
        c = coords(i)
        out.append((i, index({**c, **change(c)})))
    return out


def send(value, change):
    return lax.ppermute(value, AXES, pairs(change))


def core_swap(value):
    return send(value, lambda c: dict(core=1 - c["core"]))


def zh_swap(value):
    return send(value, lambda c: dict(zh=1 - c["zh"]))


def y_shift(value, k):
    return send(value, lambda c: dict(y=c["y"] + k))


def to_slice(flip):
    def change(c):
        return dict(
            y=2 * c["zl"] + c["x"] // 2,
            zl=c["y"] // 2,
            x=(c["y"] % 2) * 2 + c["x"] % 2,
            core=c["core"] ^ flip,
        )

    return change


def rope_tables(positions):
    half_dim = HEAD_SIZE // 2
    steps_up = jnp.arange(0, half_dim, dtype=jnp.float32) * (2.0 / HEAD_SIZE)
    inverse = jnp.power(jnp.float32(rope_base), -steps_up)
    angles = positions.astype(jnp.float32)[:, None] * inverse[None, :]
    return jnp.cos(angles)[:, None, :], jnp.sin(angles)[:, None, :]


def apply_rope(vectors, tables):
    cosine, sine = tables
    half_dim = HEAD_SIZE // 2
    low = vectors[..., :half_dim]
    high = vectors[..., half_dim:]
    return jnp.concatenate([low * cosine - high * sine, high * cosine + low * sine], axis=-1)


def half_of(value, which, dim=0):
    size = value.shape[dim] // 2
    return lax.dynamic_slice_in_dim(value, which * size, size, dim)


def ordered(first, own, other, dim=0):
    return jnp.where(
        first, jnp.concatenate([own, other], dim), jnp.concatenate([other, own], dim)
    )


def dot(a, b):
    return jnp.dot(a, b, preferred_element_type=jnp.float32)


def local(tokens, norm_gain, query_weight, kv_weight, out_weight, lengths):
    core = lax.axis_index("core")
    chip = lax.axis_index(("zl", "x"))
    y = lax.axis_index("y")
    zh = lax.axis_index("zh")
    is_first = core == 0

    gain = lax.dynamic_slice_in_dim(norm_gain, (chip * 2 + core) * 512, 512, 0)
    wide = tokens.astype(jnp.float32)
    gained = (wide * gain[None, :]).astype(jnp.bfloat16)
    mine = send(half_of(gained, core), to_slice(0))
    theirs = send(half_of(gained, 1 - core), to_slice(1))
    block = ordered(is_first, mine, theirs, 1)
    gathered = lax.all_gather(block, ("zl", "x"), axis=0, tiled=False)
    gathered = gathered.reshape(4, 2, HALF, 1024)
    squares = lax.psum(jnp.sum(wide * wide, axis=-1), ("zl", "x", "core"))

    kv_own = lax.dynamic_slice_in_dim(kv_weight, chip * 256 + core * 128, 128, 1)
    near = jnp.concatenate([query_weight, kv_own], axis=1)
    far = zh_swap(near)
    near_other = core_swap(near)
    far_other = core_swap(far)

    def whole(own, other):
        kv = ordered(is_first, own[:, 512:], other[:, 512:], 1)
        return jnp.concatenate([own[:, :512], other[:, :512], kv], axis=1)

    near_whole = whole(near, near_other)
    far_whole = whole(far, far_other)

    out_far = zh_swap(out_weight)
    pair = ordered(zh == 0, out_weight[:, None], out_far[:, None], 1)
    up = y_shift(pair, 1)
    down = y_shift(pair, -1)
    across_a = y_shift(up[:256], 1)
    across_b = y_shift(down[256:], -1)
    across = jnp.concatenate([across_a, across_b], 0)
    own_rows = jnp.zeros((4, 512, 2, 1024), jnp.bfloat16)
    for k, part in ((0, pair), (3, up), (1, down), (2, across)):
        own_rows = lax.dynamic_update_slice(own_rows, part[None], ((y + k) % 4, 0, 0, 0))
    other_rows = core_swap(own_rows)

    rows_near = lax.dynamic_index_in_dim(gathered, zh, 1, keepdims=False).reshape(1024, 1024)
    rows_far = lax.dynamic_index_in_dim(gathered, 1 - zh, 1, keepdims=False).reshape(1024, 1024)
    projected = (dot(rows_near, near_whole) + dot(rows_far, far_whole)).astype(jnp.bfloat16)
    summed = lax.psum_scatter(
        projected.reshape(4, HALF, 1280), "y", scatter_dimension=0, tiled=False
    ).astype(jnp.float32)
    scale = half_of(lax.rsqrt(squares / 8192.0 + norm_eps), core)
    summed = summed * scale[:, None]

    own_slots = core * HALF + jnp.arange(HALF, dtype=jnp.int32)
    tables = rope_tables(own_slots)
    queries = apply_rope(summed[:, :1024].reshape(HALF, 8, HEAD_SIZE), tables).astype(jnp.bfloat16)
    key_own = apply_rope(summed[:, None, 1024:1152], tables)[:, 0].astype(jnp.bfloat16)
    kv_rows = jnp.concatenate([key_own, summed[:, 1152:].astype(jnp.bfloat16)], axis=1)
    kv_all = jnp.concatenate([kv_rows, core_swap(kv_rows)], axis=0)
    keys, values = kv_all[:, :HEAD_SIZE], kv_all[:, HEAD_SIZE:]
    slot_k = jnp.concatenate([own_slots, (1 - core) * HALF + jnp.arange(HALF, dtype=jnp.int32)])
    scores = jnp.einsum(
        "qhd,kd->hqk", queries, keys, preferred_element_type=jnp.float32
    ) / jnp.sqrt(jnp.float32(HEAD_SIZE))
    allowed = (slot_k[None, :] <= own_slots[:, None]) & (slot_k[None, :] < lengths[0])
    scores = jnp.where(allowed[None], scores, -jnp.inf)
    expd = jnp.exp(scores - jnp.max(scores, axis=-1, keepdims=True))
    probs = (expd / jnp.sum(expd, axis=-1, keepdims=True)).astype(jnp.bfloat16)
    attended = jnp.einsum("hqk,kd->qhd", probs, values, preferred_element_type=jnp.float32)
    attended = attended.astype(jnp.bfloat16).reshape(HALF, 1024)

    partial = jnp.einsum(
        "qr,yrzc->yzqc", attended[:, :512], own_rows, preferred_element_type=jnp.float32
    ) + jnp.einsum(
        "qr,yrzc->yzqc", attended[:, 512:], other_rows, preferred_element_type=jnp.float32
    )
    partial = partial.astype(jnp.bfloat16).reshape(8, HALF, 1024)
    mixed = lax.psum_scatter(partial, ("zl", "x"), scatter_dimension=0, tiled=False)
    keep = half_of(mixed, core, 1)
    got = core_swap(half_of(mixed, 1 - core, 1))
    return (wide + ordered(is_first, keep, got, 0).astype(jnp.float32)).astype(jnp.bfloat16)


def solution(mesh):
    split = Mesh(mesh.devices.reshape(SIZES), AXES)
    gx, gy = ("zl", "x", "core"), ("y", "zh")
    placed = (P(gy, gx), P(), P(gy, gx), P(gy, None), P(gx, gy), P(gy))
    return jax.shard_map(
        local, mesh=split, in_specs=placed, out_specs=P(gy, gx), check_vma=False
    )
```

```python
import jax
import jax.numpy as jnp
from jax import lax
from jax.sharding import Mesh, PartitionSpec as P

HEAD_SIZE = 128
SLOTS = 512
HALF = 256
AXES = ("zl", "x", "core", "y", "zh")
SIZES = (2, 4, 2, 4, 2)

rope_base = 500000.0
norm_eps = 1e-05


def coords(i):
    out = {}
    for name, size in zip(AXES[::-1], SIZES[::-1]):
        i, out[name] = divmod(i, size)
    return out


def index(c):
    i = 0
    for name, size in zip(AXES, SIZES):
        i = i * size + c[name] % size
    return i


def pairs(change):
    out = []
    for i in range(128):
        c = coords(i)
        out.append((i, index({**c, **change(c)})))
    return out


def send(value, change):
    return lax.ppermute(value, AXES, pairs(change))


def core_swap(value):
    return send(value, lambda c: dict(core=1 - c["core"]))


def zh_swap(value):
    return send(value, lambda c: dict(zh=1 - c["zh"]))


def zl_swap(value):
    return send(value, lambda c: dict(zl=1 - c["zl"]))


def x_shift(value, k):
    return send(value, lambda c: dict(x=c["x"] + k))


def after(value, other):
    return lax.optimization_barrier((value, other))[0]


def y_shift(value, k):
    return send(value, lambda c: dict(y=c["y"] + k))


def to_slice(flip):
    def change(c):
        return dict(
            y=2 * c["zl"] + c["x"] // 2,
            zl=c["y"] // 2,
            x=(c["y"] % 2) * 2 + c["x"] % 2,
            core=c["core"] ^ flip,
        )

    return change


def rope_tables(positions):
    half_dim = HEAD_SIZE // 2
    steps_up = jnp.arange(0, half_dim, dtype=jnp.float32) * (2.0 / HEAD_SIZE)
    inverse = jnp.power(jnp.float32(rope_base), -steps_up)
    angles = positions.astype(jnp.float32)[:, None] * inverse[None, :]
    return jnp.cos(angles)[:, None, :], jnp.sin(angles)[:, None, :]


def apply_rope(vectors, tables):
    cosine, sine = tables
    half_dim = HEAD_SIZE // 2
    low = vectors[..., :half_dim]
    high = vectors[..., half_dim:]
    return jnp.concatenate([low * cosine - high * sine, high * cosine + low * sine], axis=-1)


def half_of(value, which, dim=0):
    size = value.shape[dim] // 2
    return lax.dynamic_slice_in_dim(value, which * size, size, dim)


def ordered(first, own, other, dim=0):
    return jnp.where(
        first, jnp.concatenate([own, other], dim), jnp.concatenate([other, own], dim)
    )


def dot(a, b):
    return jnp.dot(a, b, preferred_element_type=jnp.float32)


def local(tokens, norm_gain, query_weight, kv_weight, out_weight, lengths):
    core = lax.axis_index("core")
    chip = lax.axis_index(("zl", "x"))
    zl = lax.axis_index("zl")
    x = lax.axis_index("x")
    y = lax.axis_index("y")
    zh = lax.axis_index("zh")
    is_first = core == 0

    kv_own = lax.dynamic_slice_in_dim(kv_weight, chip * 256 + core * 128, 128, 1)
    near = jnp.concatenate([query_weight, kv_own], axis=1)
    far = zh_swap(near)

    gain = lax.dynamic_slice_in_dim(norm_gain, (chip * 2 + core) * 512, 512, 0)
    wide = tokens.astype(jnp.float32)
    gained = (wide * gain[None, :]).astype(jnp.bfloat16)
    mine = send(half_of(gained, core), to_slice(0))
    theirs = send(half_of(gained, 1 - core), to_slice(1))
    block = ordered(is_first, mine, theirs, 1)

    beside = zl_swap(block)
    left = x_shift(block, 1)
    right = x_shift(block, -1)
    squares = lax.psum(after(jnp.sum(wide * wide, axis=-1), block), ("zl", "x", "core"))
    left, right, beside, squares = lax.optimization_barrier((left, right, beside, squares))
    beside_left = x_shift(beside, 1)
    beside_right = x_shift(beside, -1)
    opposite = jnp.concatenate([x_shift(left[:128], 1), x_shift(right[128:], -1)], 0)
    beside_opposite = jnp.concatenate(
        [x_shift(beside_left[:128], 1), x_shift(beside_right[128:], -1)], 0
    )
    gathered = jnp.zeros((2, 4, HALF, 1024), jnp.bfloat16)
    for dz, dx, part in (
        (0, 0, block),
        (0, 3, left),
        (0, 1, right),
        (1, 0, beside),
        (0, 2, opposite),
        (1, 3, beside_left),
        (1, 1, beside_right),
        (1, 2, beside_opposite),
    ):
        gathered = lax.dynamic_update_slice(
            gathered, part[None, None], (zl ^ dz, (x + dx) % 4, 0, 0)
        )
    gathered = gathered.reshape(4, 2, HALF, 1024)

    near_other = core_swap(near)
    far_other = core_swap(far)

    def whole(own, other):
        kv = ordered(is_first, own[:, 512:], other[:, 512:], 1)
        return jnp.concatenate([own[:, :512], other[:, :512], kv], axis=1)

    near_whole = whole(near, near_other)
    far_whole = whole(far, far_other)

    out_near = lax.all_gather(out_weight, "y", axis=0, tiled=False)
    far_own = zh_swap(after(out_weight, far))
    up = y_shift(far_own, 1)
    down = y_shift(far_own, -1)
    across = jnp.concatenate([y_shift(up[:256], 1), y_shift(down[256:], -1)], 0)
    out_far = jnp.zeros((4, 512, 1024), jnp.bfloat16)
    for k, part in ((0, far_own), (3, up), (1, down), (2, across)):
        out_far = lax.dynamic_update_slice(out_far, part[None], ((y + k) % 4, 0, 0))
    out_near_other = core_swap(out_near)
    out_far_other = core_swap(out_far)

    rows_near = lax.dynamic_index_in_dim(gathered, zh, 1, keepdims=False).reshape(1024, 1024)
    rows_far = lax.dynamic_index_in_dim(gathered, 1 - zh, 1, keepdims=False).reshape(1024, 1024)
    projected = (dot(rows_near, near_whole) + dot(rows_far, far_whole)).astype(jnp.bfloat16)
    summed = lax.psum_scatter(
        projected.reshape(4, HALF, 1280), "y", scatter_dimension=0, tiled=False
    ).astype(jnp.float32)
    scale = half_of(lax.rsqrt(squares / 8192.0 + norm_eps), core)
    summed = summed * scale[:, None]

    own_slots = core * HALF + jnp.arange(HALF, dtype=jnp.int32)
    tables = rope_tables(own_slots)
    queries = apply_rope(summed[:, :1024].reshape(HALF, 8, HEAD_SIZE), tables).astype(jnp.bfloat16)
    key_own = apply_rope(summed[:, None, 1024:1152], tables)[:, 0].astype(jnp.bfloat16)
    kv_rows = jnp.concatenate([key_own, summed[:, 1152:].astype(jnp.bfloat16)], axis=1)
    kv_all = jnp.concatenate([kv_rows, core_swap(kv_rows)], axis=0)
    keys, values = kv_all[:, :HEAD_SIZE], kv_all[:, HEAD_SIZE:]
    slot_k = jnp.concatenate([own_slots, (1 - core) * HALF + jnp.arange(HALF, dtype=jnp.int32)])
    scores = jnp.einsum(
        "qhd,kd->hqk", queries, keys, preferred_element_type=jnp.float32
    ) / jnp.sqrt(jnp.float32(HEAD_SIZE))
    allowed = (slot_k[None, :] <= own_slots[:, None]) & (slot_k[None, :] < lengths[0])
    scores = jnp.where(allowed[None], scores, -jnp.inf)
    expd = jnp.exp(scores - jnp.max(scores, axis=-1, keepdims=True))
    probs = (expd / jnp.sum(expd, axis=-1, keepdims=True)).astype(jnp.bfloat16)
    attended = jnp.einsum("hqk,kd->qhd", probs, values, preferred_element_type=jnp.float32)
    attended = attended.astype(jnp.bfloat16).reshape(HALF, 1024)

    def columns(own, other):
        return jnp.einsum(
            "qr,yrc->yqc", attended[:, :512], own, preferred_element_type=jnp.float32
        ) + jnp.einsum(
            "qr,yrc->yqc", attended[:, 512:], other, preferred_element_type=jnp.float32
        )

    near_part = columns(out_near, out_near_other).astype(jnp.bfloat16)[:, None]
    far_part = columns(out_far, out_far_other).astype(jnp.bfloat16)[:, None]
    partial = ordered(zh == 0, near_part, far_part, 1).reshape(8, HALF, 1024)
    mixed = lax.psum_scatter(partial, ("zl", "x"), scatter_dimension=0, tiled=False)
    keep = half_of(mixed, core, 1)
    got = core_swap(half_of(mixed, 1 - core, 1))
    return (wide + ordered(is_first, keep, got, 0).astype(jnp.float32)).astype(jnp.bfloat16)


def solution(mesh):
    split = Mesh(mesh.devices.reshape(SIZES), AXES)
    gx, gy = ("zl", "x", "core"), ("y", "zh")
    placed = (P(gy, gx), P(), P(gy, gx), P(gy, None), P(gx, gy), P(gy))
    return jax.shard_map(
        local, mesh=split, in_specs=placed, out_specs=P(gy, gx), check_vma=False
    )
```

```python
import jax
import jax.numpy as jnp
from jax import lax
from jax.experimental import pallas as pl
from jax.experimental.pallas import tpu as pltpu
from jax.sharding import Mesh, PartitionSpec as P

HEAD_SIZE = 128
SLOTS = 512
HALF = 256
AXES = ("zl", "x", "core", "y", "zh")
SIZES = (2, 4, 2, 4, 2)

rope_base = 500000.0
norm_eps = 1e-05


def coords(i):
    out = {}
    for name, size in zip(AXES[::-1], SIZES[::-1]):
        i, out[name] = divmod(i, size)
    return out


def index(c):
    i = 0
    for name, size in zip(AXES, SIZES):
        i = i * size + c[name] % size
    return i


def pairs(change):
    out = []
    for i in range(128):
        c = coords(i)
        out.append((i, index({**c, **change(c)})))
    return out


def send(value, change):
    return lax.ppermute(value, AXES, pairs(change))


def core_swap(value):
    return send(value, lambda c: dict(core=1 - c["core"]))


def zh_swap(value):
    return send(value, lambda c: dict(zh=1 - c["zh"]))


def zl_swap(value):
    return send(value, lambda c: dict(zl=1 - c["zl"]))


def x_shift(value, k):
    return send(value, lambda c: dict(x=c["x"] + k))


def after(value, other):
    return lax.optimization_barrier((value, other))[0]


def y_shift(value, k):
    return send(value, lambda c: dict(y=c["y"] + k))


def to_slice(flip):
    def change(c):
        return dict(
            y=2 * c["zl"] + c["x"] // 2,
            zl=c["y"] // 2,
            x=(c["y"] % 2) * 2 + c["x"] % 2,
            core=c["core"] ^ flip,
        )

    return change


def to_home(flip):
    def change(c):
        moves = c["x"] % 2 != c["zh"]
        return dict(x=c["x"] ^ moves, zh=c["zh"] ^ moves, core=c["core"] ^ flip)

    return change


def rope_tables(positions):
    half_dim = HEAD_SIZE // 2
    steps_up = jnp.arange(0, half_dim, dtype=jnp.float32) * (2.0 / HEAD_SIZE)
    inverse = jnp.power(jnp.float32(rope_base), -steps_up)
    angles = positions.astype(jnp.float32)[:, None] * inverse[None, :]
    cosine, sine = jnp.cos(angles), jnp.sin(angles)
    return jnp.concatenate([cosine, cosine], 1), jnp.concatenate([-sine, sine], 1)


def rotated(vectors, cosine, sine):
    return vectors * cosine + pltpu.roll(vectors, HEAD_SIZE // 2, 1) * sine


def key_value_kernel(sum_ref, scale_ref, cos_ref, sin_ref, out_ref):
    rows = sum_ref[...].astype(jnp.float32) * scale_ref[...]
    keys = rotated(rows[:, :HEAD_SIZE], cos_ref[...], sin_ref[...])
    out_ref[:, :HEAD_SIZE] = keys.astype(jnp.bfloat16)
    out_ref[:, HEAD_SIZE:] = rows[:, HEAD_SIZE:].astype(jnp.bfloat16)


def key_value_rows(summed, scale, cosine, sine):
    whole = pl.BlockSpec((HALF, HEAD_SIZE), lambda i: (0, 0))
    return pl.pallas_call(
        key_value_kernel,
        grid=(1,),
        in_specs=[
            pl.BlockSpec((HALF, 2 * HEAD_SIZE), lambda i: (0, 4)),
            pl.BlockSpec((HALF, 1), lambda i: (0, 0)),
            whole,
            whole,
        ],
        out_specs=pl.BlockSpec((HALF, 2 * HEAD_SIZE), lambda i: (0, 0)),
        out_shape=jax.ShapeDtypeStruct((HALF, 2 * HEAD_SIZE), jnp.bfloat16),
    )(summed, scale, cosine, sine)


def attention_kernel(sum_ref, scale_ref, cos_ref, sin_ref, bias_ref, own_ref, other_ref, out_ref):
    rows = sum_ref[...].astype(jnp.float32) * scale_ref[...]
    queries = rotated(rows, cos_ref[...], sin_ref[...]).astype(jnp.bfloat16)
    contract = (((1,), (1,)), ((), ()))

    def scores_of(ref, first):
        scores = lax.dot_general(
            queries, ref[:, :HEAD_SIZE], contract, preferred_element_type=jnp.float32
        )
        return scores * (HEAD_SIZE**-0.5) + bias_ref[:, first : first + HALF]

    own, other = scores_of(own_ref, 0), scores_of(other_ref, HALF)
    top = jnp.maximum(
        jnp.max(own, axis=-1, keepdims=True), jnp.max(other, axis=-1, keepdims=True)
    )
    own, other = jnp.exp(own - top), jnp.exp(other - top)
    total = jnp.sum(own, axis=-1, keepdims=True) + jnp.sum(other, axis=-1, keepdims=True)
    mixed = dot(own.astype(jnp.bfloat16), own_ref[:, HEAD_SIZE:]) + dot(
        other.astype(jnp.bfloat16), other_ref[:, HEAD_SIZE:]
    )
    out_ref[...] = (mixed / total).astype(jnp.bfloat16)


def attention(summed, scale, cosine, sine, bias, own, other):
    def fixed(shape):
        return pl.BlockSpec(shape, lambda h: (0, 0))

    return pl.pallas_call(
        attention_kernel,
        grid=(8,),
        in_specs=[
            pl.BlockSpec((HALF, HEAD_SIZE), lambda h: (0, h)),
            fixed((HALF, 1)),
            fixed((HALF, HEAD_SIZE)),
            fixed((HALF, HEAD_SIZE)),
            fixed((HALF, SLOTS)),
            fixed((HALF, 2 * HEAD_SIZE)),
            fixed((HALF, 2 * HEAD_SIZE)),
        ],
        out_specs=pl.BlockSpec((HALF, HEAD_SIZE), lambda h: (0, h)),
        out_shape=jax.ShapeDtypeStruct((HALF, 1024), jnp.bfloat16),
    )(summed, scale, cosine, sine, bias, own, other)


def half_of(value, which, dim=0):
    size = value.shape[dim] // 2
    return lax.dynamic_slice_in_dim(value, which * size, size, dim)


def ordered(first, own, other, dim=0):
    return jnp.where(
        first, jnp.concatenate([own, other], dim), jnp.concatenate([other, own], dim)
    )


def dot(a, b):
    return jnp.dot(a, b, preferred_element_type=jnp.float32)


def local(tokens, norm_gain, query_weight, kv_weight, out_weight, lengths):
    core = lax.axis_index("core")
    chip = lax.axis_index(("zl", "x"))
    zl = lax.axis_index("zl")
    x = lax.axis_index("x")
    y = lax.axis_index("y")
    zh = lax.axis_index("zh")
    is_first = core == 0

    kv_own = lax.dynamic_slice_in_dim(kv_weight, chip * 256 + core * 128, 128, 1)
    near = jnp.concatenate([query_weight, kv_own], axis=1)
    far = zh_swap(near)

    gain = lax.dynamic_slice_in_dim(norm_gain, (chip * 2 + core) * 512, 512, 0)
    wide = tokens.astype(jnp.float32)
    gained = (wide * gain[None, :]).astype(jnp.bfloat16)
    mine = send(half_of(gained, core), to_slice(0))
    theirs = send(half_of(gained, 1 - core), to_slice(1))
    block = ordered(is_first, mine, theirs, 1)

    beside = zl_swap(block)
    left = x_shift(block, 1)
    right = x_shift(block, -1)
    left, right, beside, far = lax.optimization_barrier((left, right, beside, far))
    beside_left = x_shift(beside, 1)
    beside_right = x_shift(beside, -1)
    opposite = jnp.concatenate([x_shift(left[:128], 1), x_shift(right[128:], -1)], 0)
    beside_opposite = jnp.concatenate(
        [x_shift(beside_left[:128], 1), x_shift(beside_right[128:], -1)], 0
    )
    gathered = jnp.zeros((4, HALF, 2048), jnp.bfloat16)
    for dz, dx, part in (
        (0, 0, block),
        (0, 3, left),
        (0, 1, right),
        (1, 0, beside),
        (0, 2, opposite),
        (1, 3, beside_left),
        (1, 1, beside_right),
        (1, 2, beside_opposite),
    ):
        zs, xs = zl ^ dz, (x + dx) % 4
        gathered = lax.dynamic_update_slice(
            gathered, part[None], (zs * 2 + xs // 2, 0, (xs % 2) * 1024)
        )

    near_other = core_swap(near)
    far_other = core_swap(far)

    def whole(own, other):
        kv = ordered(is_first, own[:, 512:], other[:, 512:], 1)
        return jnp.concatenate([own[:, :512], other[:, :512], kv], axis=1)

    weights = ordered(zh == 0, whole(near, near_other), whole(far, far_other), 0)

    out_near = lax.all_gather(out_weight, "y", axis=0, tiled=False)
    out_other = core_swap(out_near)

    projected = dot(gathered.reshape(1024, 2048), weights).astype(jnp.bfloat16)
    summed = lax.psum_scatter(
        projected.reshape(4, HALF, 1280), "y", scatter_dimension=0, tiled=True
    ).reshape(HALF, 1280)

    slice_gain = lax.dynamic_slice_in_dim(norm_gain, y * 2048, 2048, 0)
    plain = gathered.astype(jnp.float32) * (1.0 / slice_gain)
    squares = jnp.sum(plain * plain, axis=-1)
    total = lax.dynamic_index_in_dim(squares, y, 0, keepdims=False)
    for k in (1, 2, 3):
        total += y_shift(lax.dynamic_index_in_dim(squares, (y + k) % 4, 0, keepdims=False), k)
    scale = lax.rsqrt(total / 8192.0 + norm_eps)[:, None]

    own_slots = core * HALF + jnp.arange(HALF, dtype=jnp.int32)
    slot_k = jnp.concatenate([own_slots, (1 - core) * HALF + jnp.arange(HALF, dtype=jnp.int32)])
    allowed = (slot_k[None, :] <= own_slots[:, None]) & (slot_k[None, :] < lengths[0])
    bias = jnp.where(allowed, 0.0, -jnp.inf).astype(jnp.float32)
    cosine, sine = rope_tables(own_slots)

    kv_rows = key_value_rows(summed, scale, cosine, sine)
    attended = attention(summed, scale, cosine, sine, bias, kv_rows, core_swap(kv_rows))

    def columns(rows):
        return (
            jnp.einsum("qr,yrc->yqc", rows[:, :512], out_near, preferred_element_type=jnp.float32)
            + jnp.einsum("qr,yrc->yqc", rows[:, 512:], out_other, preferred_element_type=jnp.float32)
        ).astype(jnp.bfloat16)[:, None]

    partial = ordered(zh == 0, columns(attended), columns(zh_swap(attended)), 1)
    mixed = lax.psum_scatter(
        partial.reshape(8, HALF, 1024), ("zl", "x"), scatter_dimension=0, tiled=True
    ).reshape(HALF, 1024)
    keep = send(half_of(mixed, core, 1), to_home(0))
    got = send(half_of(mixed, 1 - core, 1), to_home(1))
    return (wide + ordered(is_first, keep, got, 0).astype(jnp.float32)).astype(jnp.bfloat16)


def solution(mesh):
    split = Mesh(mesh.devices.reshape(SIZES), AXES)
    gx, gy = ("zl", "x", "core"), ("y", "zh")
    placed = (P(gy, gx), P(), P(gy, gx), P(gy, None), P(gx, gy), P(gy))
    return jax.shard_map(
        local, mesh=split, in_specs=placed, out_specs=P(gy, gx), check_vma=False
    )
```

```python
import jax
import jax.numpy as jnp
from jax import lax
from jax.experimental import pallas as pl
from jax.experimental.pallas import tpu as pltpu
from jax.sharding import Mesh, PartitionSpec as P

HEAD_SIZE = 128
SLOTS = 512
HALF = 256
AXES = ("zl", "x", "core", "y", "zh")
SIZES = (2, 4, 2, 4, 2)

rope_base = 500000.0
norm_eps = 1e-05


def coords(i):
    out = {}
    for name, size in zip(AXES[::-1], SIZES[::-1]):
        i, out[name] = divmod(i, size)
    return out


def index(c):
    i = 0
    for name, size in zip(AXES, SIZES):
        i = i * size + c[name] % size
    return i


def pairs(change):
    out = []
    for i in range(128):
        c = coords(i)
        out.append((i, index({**c, **change(c)})))
    return out


def send(value, change):
    return lax.ppermute(value, AXES, pairs(change))


def core_swap(value):
    return send(value, lambda c: dict(core=1 - c["core"]))


def zh_swap(value):
    return send(value, lambda c: dict(zh=1 - c["zh"]))


def zl_swap(value):
    return send(value, lambda c: dict(zl=1 - c["zl"]))


def x_shift(value, k):
    return send(value, lambda c: dict(x=c["x"] + k))


def after(value, other):
    return lax.optimization_barrier((value, other))[0]


def y_shift(value, k):
    return send(value, lambda c: dict(y=c["y"] + k))


def to_slice(flip):
    def change(c):
        return dict(
            y=2 * c["zl"] + c["x"] // 2,
            zl=c["y"] // 2,
            x=(c["y"] % 2) * 2 + c["x"] % 2,
            core=c["core"] ^ flip,
        )

    return change


def to_home(flip):
    def change(c):
        moves = c["x"] % 2 != c["zh"]
        return dict(x=c["x"] ^ moves, zh=c["zh"] ^ moves, core=c["core"] ^ flip)

    return change


def rope_tables(positions):
    half_dim = HEAD_SIZE // 2
    steps_up = jnp.arange(0, half_dim, dtype=jnp.float32) * (2.0 / HEAD_SIZE)
    inverse = jnp.power(jnp.float32(rope_base), -steps_up)
    angles = positions.astype(jnp.float32)[:, None] * inverse[None, :]
    cosine, sine = jnp.cos(angles), jnp.sin(angles)
    return jnp.concatenate([cosine, cosine], 1), jnp.concatenate([-sine, sine], 1)


def rotated(vectors, cosine, sine):
    return vectors * cosine + pltpu.roll(vectors, HEAD_SIZE // 2, 1) * sine


def key_value_kernel(sum_ref, scale_ref, cos_ref, sin_ref, out_ref):
    rows = sum_ref[...].astype(jnp.float32) * scale_ref[...]
    keys = rotated(rows[:, :HEAD_SIZE], cos_ref[...], sin_ref[...])
    out_ref[:, :HEAD_SIZE] = keys.astype(jnp.bfloat16)
    out_ref[:, HEAD_SIZE:] = rows[:, HEAD_SIZE:].astype(jnp.bfloat16)


def key_value_rows(summed, scale, cosine, sine):
    whole = pl.BlockSpec((HALF, HEAD_SIZE), lambda i: (0, 0))
    return pl.pallas_call(
        key_value_kernel,
        grid=(1,),
        in_specs=[
            pl.BlockSpec((HALF, 2 * HEAD_SIZE), lambda i: (0, 4)),
            pl.BlockSpec((HALF, 1), lambda i: (0, 0)),
            whole,
            whole,
        ],
        out_specs=pl.BlockSpec((HALF, 2 * HEAD_SIZE), lambda i: (0, 0)),
        out_shape=jax.ShapeDtypeStruct((HALF, 2 * HEAD_SIZE), jnp.bfloat16),
    )(summed, scale, cosine, sine)


def attention_kernel(sum_ref, scale_ref, cos_ref, sin_ref, bias_ref, own_ref, other_ref, out_ref):
    rows = sum_ref[...].astype(jnp.float32) * scale_ref[...]
    queries = rotated(rows, cos_ref[...], sin_ref[...]).astype(jnp.bfloat16)
    contract = (((1,), (1,)), ((), ()))

    def scores_of(ref, first):
        scores = lax.dot_general(
            queries, ref[:, :HEAD_SIZE], contract, preferred_element_type=jnp.float32
        )
        return scores * (HEAD_SIZE**-0.5) + bias_ref[:, first : first + HALF]

    own, other = scores_of(own_ref, 0), scores_of(other_ref, HALF)
    top = jnp.maximum(
        jnp.max(own, axis=-1, keepdims=True), jnp.max(other, axis=-1, keepdims=True)
    )
    own, other = jnp.exp(own - top), jnp.exp(other - top)
    total = jnp.sum(own, axis=-1, keepdims=True) + jnp.sum(other, axis=-1, keepdims=True)
    mixed = dot(own.astype(jnp.bfloat16), own_ref[:, HEAD_SIZE:]) + dot(
        other.astype(jnp.bfloat16), other_ref[:, HEAD_SIZE:]
    )
    out_ref[...] = (mixed / total).astype(jnp.bfloat16)


def attention(first, summed, scale, cosine, sine, bias, own, other):
    def fixed(shape):
        return pl.BlockSpec(shape, lambda h: (0, 0))

    return pl.pallas_call(
        attention_kernel,
        grid=(4,),
        in_specs=[
            pl.BlockSpec((HALF, HEAD_SIZE), lambda h: (0, h + first)),
            fixed((HALF, 1)),
            fixed((HALF, HEAD_SIZE)),
            fixed((HALF, HEAD_SIZE)),
            fixed((HALF, SLOTS)),
            fixed((HALF, 2 * HEAD_SIZE)),
            fixed((HALF, 2 * HEAD_SIZE)),
        ],
        out_specs=pl.BlockSpec((HALF, HEAD_SIZE), lambda h: (0, h)),
        out_shape=jax.ShapeDtypeStruct((HALF, 512), jnp.bfloat16),
    )(summed, scale, cosine, sine, bias, own, other)


def columns_kernel(zh_ref, own_a, own_b, far_a, far_b, near_ref, other_ref, out_ref):
    def put(which, left, right):
        rows = dot(left[...], near_ref[0]) + dot(right[...], other_ref[0])
        start = pl.multiple_of(which * HALF, HALF)
        out_ref[0, pl.ds(start, HALF), :] = rows.astype(jnp.bfloat16)

    put(zh_ref[0], own_a, own_b)
    put(1 - zh_ref[0], far_a, far_b)


def columns(zh, own_a, own_b, far_a, far_b, near, other):
    rows = pl.BlockSpec((HALF, 512), lambda j, z: (0, 0))
    block = pl.BlockSpec((1, 512, 1024), lambda j, z: (j, 0, 0))
    return pl.pallas_call(
        columns_kernel,
        grid_spec=pltpu.PrefetchScalarGridSpec(
            num_scalar_prefetch=1,
            grid=(4,),
            in_specs=[rows, rows, rows, rows, block, block],
            out_specs=pl.BlockSpec((1, SLOTS, 1024), lambda j, z: (j, 0, 0)),
        ),
        out_shape=jax.ShapeDtypeStruct((4, SLOTS, 1024), jnp.bfloat16),
        compiler_params=pltpu.CompilerParams(vmem_limit_bytes=32 * 1024 * 1024),
    )(zh.reshape(1), own_a, own_b, far_a, far_b, near, other)


def half_of(value, which, dim=0):
    size = value.shape[dim] // 2
    return lax.dynamic_slice_in_dim(value, which * size, size, dim)


def ordered(first, own, other, dim=0):
    return jnp.where(
        first, jnp.concatenate([own, other], dim), jnp.concatenate([other, own], dim)
    )


def dot(a, b):
    return jnp.dot(a, b, preferred_element_type=jnp.float32)


def local(tokens, norm_gain, query_weight, kv_weight, out_weight, lengths):
    core = lax.axis_index("core")
    chip = lax.axis_index(("zl", "x"))
    zl = lax.axis_index("zl")
    x = lax.axis_index("x")
    y = lax.axis_index("y")
    zh = lax.axis_index("zh")
    is_first = core == 0

    gain = lax.dynamic_slice_in_dim(norm_gain, (chip * 2 + core) * 512, 512, 0)
    wide = tokens.astype(jnp.float32)
    gained = (wide * gain[None, :]).astype(jnp.bfloat16)
    mine_out, theirs_out = half_of(gained, core), half_of(gained, 1 - core)
    mine = send(mine_out, to_slice(0))
    theirs = send(theirs_out, to_slice(1))
    block = ordered(is_first, mine, theirs, 1)

    kv_own = lax.dynamic_slice_in_dim(kv_weight, chip * 256 + core * 128, 128, 1)
    near = after(jnp.concatenate([query_weight, kv_own], axis=1), (mine_out, theirs_out))
    far_top = zh_swap(near[:512])

    beside = zl_swap(block)
    left = x_shift(block, 1)
    right = x_shift(block, -1)
    left, right, beside, far_top = lax.optimization_barrier((left, right, beside, far_top))
    far_bottom = zh_swap(after(near[512:], beside))
    beside_left = x_shift(beside, 1)
    beside_right = x_shift(beside, -1)
    opposite = jnp.concatenate([x_shift(left[:128], 1), x_shift(right[128:], -1)], 0)
    beside_opposite = jnp.concatenate(
        [x_shift(beside_left[:128], 1), x_shift(beside_right[128:], -1)], 0
    )
    gathered = jnp.zeros((4, HALF, 2048), jnp.bfloat16)
    for dz, dx, part in (
        (0, 0, block),
        (0, 3, left),
        (0, 1, right),
        (1, 0, beside),
        (0, 2, opposite),
        (1, 3, beside_left),
        (1, 1, beside_right),
        (1, 2, beside_opposite),
    ):
        zs, xs = zl ^ dz, (x + dx) % 4
        gathered = lax.dynamic_update_slice(
            gathered, part[None], (zs * 2 + xs // 2, 0, (xs % 2) * 1024)
        )

    near_other = core_swap(near)
    far = jnp.concatenate([far_top, far_bottom], axis=0)
    far_other = core_swap(far)

    def whole(own, other):
        kv = ordered(is_first, own[:, 512:], other[:, 512:], 1)
        return jnp.concatenate([own[:, :512], other[:, :512], kv], axis=1)

    weights = lax.optimization_barrier(
        ordered(zh == 0, whole(near, near_other), whole(far, far_other), 0)
    )

    out_near = lax.all_gather(out_weight, "y", axis=0, tiled=False)
    out_other = core_swap(out_near)

    def term(k):
        rows = lax.dynamic_index_in_dim(gathered, (y + k) % 4, 0, keepdims=False)
        return dot(rows, weights)

    farthest = term(2).astype(jnp.bfloat16)
    from_below = y_shift(farthest[:128], 1)
    from_above = y_shift(farthest[128:], -1)
    upper, lower, kept = lax.optimization_barrier((term(1), term(3), term(0)))
    upper = jnp.concatenate([upper[:128] + from_below.astype(jnp.float32), upper[128:]], 0)
    lower = jnp.concatenate([lower[:128], lower[128:] + from_above.astype(jnp.float32)], 0)
    from_below = y_shift(upper.astype(jnp.bfloat16), 1)
    from_above = y_shift(lower.astype(jnp.bfloat16), -1)
    summed = kept + from_below.astype(jnp.float32) + from_above.astype(jnp.float32)
    summed = summed.astype(jnp.bfloat16)

    slice_gain = lax.dynamic_slice_in_dim(norm_gain, y * 2048, 2048, 0)
    plain = gathered.astype(jnp.float32) * (1.0 / slice_gain)
    squares = jnp.sum(plain * plain, axis=-1)
    total = lax.dynamic_index_in_dim(squares, y, 0, keepdims=False)
    for k in (1, 2, 3):
        total += y_shift(lax.dynamic_index_in_dim(squares, (y + k) % 4, 0, keepdims=False), k)
    scale = lax.rsqrt(total / 8192.0 + norm_eps)[:, None]

    own_slots = core * HALF + jnp.arange(HALF, dtype=jnp.int32)
    slot_k = jnp.concatenate([own_slots, (1 - core) * HALF + jnp.arange(HALF, dtype=jnp.int32)])
    allowed = (slot_k[None, :] <= own_slots[:, None]) & (slot_k[None, :] < lengths[0])
    bias = jnp.where(allowed, 0.0, -jnp.inf).astype(jnp.float32)
    cosine, sine = rope_tables(own_slots)

    kv_rows = key_value_rows(summed, scale, cosine, sine)
    kv_other = core_swap(kv_rows)
    own_a = attention(0, summed, scale, cosine, sine, bias, kv_rows, kv_other)
    far_a = zh_swap(own_a)
    own_b = attention(4, summed, scale, cosine, sine, bias, kv_rows, kv_other)
    far_b = zh_swap(own_b)

    partial = columns(zh, own_a, own_b, far_a, far_b, out_near, out_other)
    mixed = lax.psum_scatter(
        partial.reshape(8, HALF, 1024), ("zl", "x"), scatter_dimension=0, tiled=True
    ).reshape(HALF, 1024)
    keep = send(half_of(mixed, core, 1), to_home(0))
    got = send(half_of(mixed, 1 - core, 1), to_home(1))
    return (wide + ordered(is_first, keep, got, 0).astype(jnp.float32)).astype(jnp.bfloat16)


def solution(mesh):
    split = Mesh(mesh.devices.reshape(SIZES), AXES)
    gx, gy = ("zl", "x", "core"), ("y", "zh")
    placed = (P(gy, gx), P(), P(gy, gx), P(gy, None), P(gx, gy), P(gy))
    return jax.shard_map(
        local, mesh=split, in_specs=placed, out_specs=P(gy, gx), check_vma=False
    )
```

```python
import jax
import jax.numpy as jnp
from jax import lax
from jax.experimental import pallas as pl
from jax.experimental.pallas import tpu as pltpu
from jax.sharding import Mesh, PartitionSpec as P

HEAD_SIZE = 128
SLOTS = 512
HALF = 256
AXES = ("zl", "x", "core", "y", "zh")
SIZES = (2, 4, 2, 4, 2)

rope_base = 500000.0
norm_eps = 1e-05


def coords(i):
    out = {}
    for name, size in zip(AXES[::-1], SIZES[::-1]):
        i, out[name] = divmod(i, size)
    return out


def index(c):
    i = 0
    for name, size in zip(AXES, SIZES):
        i = i * size + c[name] % size
    return i


def pairs(change):
    out = []
    for i in range(128):
        c = coords(i)
        out.append((i, index({**c, **change(c)})))
    return out


def send(value, change):
    return lax.ppermute(value, AXES, pairs(change))


def core_swap(value):
    return send(value, lambda c: dict(core=1 - c["core"]))


def zh_swap(value):
    return send(value, lambda c: dict(zh=1 - c["zh"]))


def zl_swap(value):
    return send(value, lambda c: dict(zl=1 - c["zl"]))


def x_shift(value, k):
    return send(value, lambda c: dict(x=c["x"] + k))


def after(value, other):
    return lax.optimization_barrier((value, other))[0]


def y_shift(value, k):
    return send(value, lambda c: dict(y=c["y"] + k))


def to_slice(flip):
    def change(c):
        return dict(
            y=2 * c["zl"] + c["x"] // 2,
            zl=c["y"] // 2,
            x=(c["y"] % 2) * 2 + c["x"] % 2,
            core=c["core"] ^ flip,
        )

    return change


def to_home(flip):
    def change(c):
        moves = c["x"] % 2 != c["zh"]
        return dict(x=c["x"] ^ moves, zh=c["zh"] ^ moves, core=c["core"] ^ flip)

    return change


def rope_tables(positions):
    half_dim = HEAD_SIZE // 2
    steps_up = jnp.arange(0, half_dim, dtype=jnp.float32) * (2.0 / HEAD_SIZE)
    inverse = jnp.power(jnp.float32(rope_base), -steps_up)
    angles = positions.astype(jnp.float32)[:, None] * inverse[None, :]
    cosine, sine = jnp.cos(angles), jnp.sin(angles)
    return jnp.concatenate([cosine, cosine], 1), jnp.concatenate([-sine, sine], 1)


def rotated(vectors, cosine, sine):
    return vectors * cosine + pltpu.roll(vectors, HEAD_SIZE // 2, 1) * sine


WIDE = 640
GRANT = pltpu.CompilerParams(vmem_limit_bytes=40 * 1024 * 1024)


def total_of(refs, cols=slice(None)):
    total = refs[0][:, cols].astype(jnp.float32)
    for ref in refs[1:]:
        total += ref[:, cols].astype(jnp.float32)
    return total


def key_value_kernel(core_ref, k0, k1, k2, v0, v1, v2, scale_ref, cos_ref, sin_ref, out_ref):
    scale = scale_ref[...]
    keys = rotated(total_of((k0, k1, k2)) * scale, cos_ref[...], sin_ref[...])
    out_ref[:, :HEAD_SIZE] = keys.astype(jnp.bfloat16)
    out_ref[:, HEAD_SIZE:] = (total_of((v0, v1, v2)) * scale).astype(jnp.bfloat16)


def key_value_rows(core, sums, scale, cosine, sine):
    keys = pl.BlockSpec((HALF, HEAD_SIZE), lambda i, c: (0, 4 + 5 * c[0]))
    values = pl.BlockSpec((HALF, HEAD_SIZE), lambda i, c: (0, 9 - 5 * c[0]))
    table = pl.BlockSpec((HALF, HEAD_SIZE), lambda i, c: (0, 0))
    return pl.pallas_call(
        key_value_kernel,
        grid_spec=pltpu.PrefetchScalarGridSpec(
            num_scalar_prefetch=1,
            grid=(1,),
            in_specs=[keys] * 3
            + [values] * 3
            + [pl.BlockSpec((HALF, 1), lambda i, c: (0, 0)), table, table],
            out_specs=pl.BlockSpec((HALF, 2 * HEAD_SIZE), lambda i, c: (0, 0)),
        ),
        out_shape=jax.ShapeDtypeStruct((HALF, 2 * HEAD_SIZE), jnp.bfloat16),
    )(core.reshape(1), *sums, *sums, scale, cosine, sine)


def attention_kernel(
    s0, s1, s2, scale_ref, cos_ref, sin_ref, bias_ref, own_ref, other_ref, out_ref
):
    contract = (((1,), (1,)), ((), ()))
    for head in range(4):
        cols = slice(head * HEAD_SIZE, (head + 1) * HEAD_SIZE)
        rows = total_of((s0, s1, s2), cols) * scale_ref[...]
        queries = rotated(rows, cos_ref[...], sin_ref[...]).astype(jnp.bfloat16)

        def scores_of(ref, first):
            scores = lax.dot_general(
                queries, ref[:, :HEAD_SIZE], contract, preferred_element_type=jnp.float32
            )
            return scores * (HEAD_SIZE**-0.5) + bias_ref[:, first : first + HALF]

        own, other = scores_of(own_ref, 0), scores_of(other_ref, HALF)
        top = jnp.maximum(
            jnp.max(own, axis=-1, keepdims=True), jnp.max(other, axis=-1, keepdims=True)
        )
        own, other = jnp.exp(own - top), jnp.exp(other - top)
        total = jnp.sum(own, axis=-1, keepdims=True) + jnp.sum(other, axis=-1, keepdims=True)
        mixed = dot(own.astype(jnp.bfloat16), own_ref[:, HEAD_SIZE:]) + dot(
            other.astype(jnp.bfloat16), other_ref[:, HEAD_SIZE:]
        )
        out_ref[:, cols] = (mixed / total).astype(jnp.bfloat16)


def attention(part, sums, scale, cosine, sine, bias, own, other):
    def fixed(shape):
        return pl.BlockSpec(shape, lambda i: (0, 0))

    return pl.pallas_call(
        attention_kernel,
        grid=(1,),
        in_specs=[pl.BlockSpec((HALF, WIDE), lambda i: (0, part))] * 3
        + [
            fixed((HALF, 1)),
            fixed((HALF, HEAD_SIZE)),
            fixed((HALF, HEAD_SIZE)),
            fixed((HALF, SLOTS)),
            fixed((HALF, 2 * HEAD_SIZE)),
            fixed((HALF, 2 * HEAD_SIZE)),
        ],
        out_specs=fixed((HALF, 512)),
        out_shape=jax.ShapeDtypeStruct((HALF, 512), jnp.bfloat16),
        compiler_params=GRANT,
    )(*sums, scale, cosine, sine, bias, own, other)


def project_kernel(steps, at_ref, rows_ref, near, near_other, far, far_other, *outs):
    zh = at_ref[0]
    near_rows = rows_ref[0, :, pl.ds(pl.multiple_of(zh * 1024, 1024), 1024)]
    far_rows = rows_ref[0, :, pl.ds(pl.multiple_of((1 - zh) * 1024, 1024), 1024)]
    own = (dot(near_rows, near[...]) + dot(far_rows, far[...])).astype(jnp.bfloat16)
    other = (dot(near_rows, near_other[...]) + dot(far_rows, far_other[...])).astype(jnp.bfloat16)
    if steps == 1:
        for half, out in enumerate(outs):
            out[:, :WIDE] = own[half * 128 : half * 128 + 128]
            out[:, WIDE:] = other[half * 128 : half * 128 + 128]
        return
    for step, out in enumerate(outs):

        @pl.when(pl.program_id(0) == step)
        def _():
            out[:, :WIDE] = own
            out[:, WIDE:] = other


def project(which, zh, gathered, weights):
    steps = len(which)
    rows = 128 if steps == 1 else HALF
    outs = 2 if steps == 1 else steps
    whole = pl.BlockSpec((1024, WIDE), lambda i, at: (0, 0))
    return pl.pallas_call(
        lambda *refs: project_kernel(steps, *refs),
        grid_spec=pltpu.PrefetchScalarGridSpec(
            num_scalar_prefetch=1,
            grid=(steps,),
            in_specs=[pl.BlockSpec((1, HALF, 2048), lambda i, at: (at[1 + i], 0, 0))] + [whole] * 4,
            out_specs=[pl.BlockSpec((rows, 2 * WIDE), lambda i, at: (0, 0))] * outs,
        ),
        out_shape=[jax.ShapeDtypeStruct((rows, 2 * WIDE), jnp.bfloat16)] * outs,
        compiler_params=GRANT,
    )(jnp.stack([zh, *which]).astype(jnp.int32), gathered, *weights)


def chunk_kernel(starts, halves, at_ref, own_a, own_b, far_a, far_b, near, other, *refs):
    added, outs, rows = refs[: len(starts)], refs[len(starts) : -1], refs[-1]

    @pl.when(at_ref[1] == 1)
    def _():
        rows[:, :512] = own_a[...]
        rows[:, 512:] = own_b[...]

    @pl.when(at_ref[1] == 0)
    def _():
        rows[:, :512] = far_a[...]
        rows[:, 512:] = far_b[...]

    product = dot(rows[:, :512], near[0]) + dot(rows[:, 512:], other[0])
    parts = [product[:128], product[128:]]
    for start, ref in zip(starts, added):
        if start is None:
            parts[0] += ref[:128].astype(jnp.float32)
            parts[1] += ref[128:].astype(jnp.float32)
        else:
            parts[start] += ref[...].astype(jnp.float32)
    if halves:
        outs[0][...] = parts[0].astype(jnp.bfloat16)
        outs[1][...] = parts[1].astype(jnp.bfloat16)
    else:
        outs[0][:128] = parts[0].astype(jnp.bfloat16)
        outs[0][128:] = parts[1].astype(jnp.bfloat16)


def chunk(target, zh, attended, near, other, added=(), halves=False):
    zt, xt = target
    at = jnp.stack([zt * 2 + xt // 2, (xt % 2 == zh).astype(jnp.int32)]).astype(jnp.int32)
    rows = pl.BlockSpec((HALF, 512), lambda i, at: (0, 0))
    block = pl.BlockSpec((1, 512, 1024), lambda i, at: (at[0], 0, 0))
    size = 128 if halves else HALF
    starts = [start for _, start in added]
    out = pl.pallas_call(
        lambda *refs: chunk_kernel(starts, halves, *refs),
        grid_spec=pltpu.PrefetchScalarGridSpec(
            num_scalar_prefetch=1,
            grid=(1,),
            in_specs=[rows] * 4
            + [block] * 2
            + [pl.BlockSpec(value.shape, lambda i, at: (0, 0)) for value, _ in added],
            out_specs=[pl.BlockSpec((size, 1024), lambda i, at: (0, 0))] * (1 + halves),
            scratch_shapes=[pltpu.VMEM((HALF, 1024), jnp.bfloat16)],
        ),
        out_shape=[jax.ShapeDtypeStruct((size, 1024), jnp.bfloat16)] * (1 + halves),
        compiler_params=GRANT,
    )(at, *attended, near, other, *[value for value, _ in added])
    return out if halves else out[0]


def half_of(value, which, dim=0):
    size = value.shape[dim] // 2
    return lax.dynamic_slice_in_dim(value, which * size, size, dim)


def ordered(first, own, other, dim=0):
    return jnp.where(
        first, jnp.concatenate([own, other], dim), jnp.concatenate([other, own], dim)
    )


def dot(a, b):
    return jnp.dot(a, b, preferred_element_type=jnp.float32)


def local(tokens, norm_gain, query_weight, kv_weight, out_weight, lengths):
    core = lax.axis_index("core")
    chip = lax.axis_index(("zl", "x"))
    zl = lax.axis_index("zl")
    x = lax.axis_index("x")
    y = lax.axis_index("y")
    zh = lax.axis_index("zh")
    is_first = core == 0

    gain = lax.dynamic_slice_in_dim(norm_gain, (chip * 2 + core) * 512, 512, 0)
    wide = tokens.astype(jnp.float32)
    gained = (wide * gain[None, :]).astype(jnp.bfloat16)
    mine_out, theirs_out = half_of(gained, core), half_of(gained, 1 - core)
    mine = send(mine_out, to_slice(0))
    theirs = send(theirs_out, to_slice(1))
    block = ordered(is_first, mine, theirs, 1)

    kv_own = lax.dynamic_slice_in_dim(kv_weight, chip * 256 + core * 128, 128, 1)
    near = after(jnp.concatenate([query_weight, kv_own], axis=1), (mine_out, theirs_out))
    far_top = zh_swap(near[:512])

    beside = zl_swap(block)
    left = x_shift(block, 1)
    right = x_shift(block, -1)
    near_other = core_swap(near)
    left, right, beside, far_top, near_other = lax.optimization_barrier(
        (left, right, beside, far_top, near_other)
    )
    far_bottom = zh_swap(after(near[512:], beside))
    beside_left = x_shift(beside, 1)
    beside_right = x_shift(beside, -1)
    opposite = jnp.concatenate([x_shift(left[:128], 1), x_shift(right[128:], -1)], 0)
    beside_opposite = jnp.concatenate(
        [x_shift(beside_left[:128], 1), x_shift(beside_right[128:], -1)], 0
    )
    gathered = jnp.zeros((4, HALF, 2048), jnp.bfloat16)
    for dz, dx, part in (
        (0, 0, block),
        (0, 3, left),
        (0, 1, right),
        (1, 0, beside),
        (0, 2, opposite),
        (1, 3, beside_left),
        (1, 1, beside_right),
        (1, 2, beside_opposite),
    ):
        zs, xs = zl ^ dz, (x + dx) % 4
        gathered = lax.dynamic_update_slice(
            gathered, part[None], (zs * 2 + xs // 2, 0, (xs % 2) * 1024)
        )

    far = jnp.concatenate([far_top, far_bottom], axis=0)
    weights = (near, near_other, far, core_swap(far))

    out_near = lax.all_gather(out_weight, "y", axis=0, tiled=False)
    out_other = core_swap(out_near)

    low, high = project([(y + 2) % 4], zh, gathered, weights)
    from_below = y_shift(low, 1)
    from_above = y_shift(high, -1)
    from_below, from_above, out_other = lax.optimization_barrier(
        (from_below, from_above, out_other)
    )
    upper, lower, kept = project([(y + 1) % 4, (y + 3) % 4, y], zh, gathered, weights)
    upper = lax.dynamic_update_slice(upper, upper[:128] + from_below, (0, 0))
    lower = lax.dynamic_update_slice(lower, lower[128:] + from_above, (128, 0))
    sums = (kept, y_shift(upper, 1), y_shift(lower, -1))

    slice_gain = lax.dynamic_slice_in_dim(norm_gain, y * 2048, 2048, 0)
    plain = gathered.astype(jnp.float32) * (1.0 / slice_gain)
    squares = jnp.sum(plain * plain, axis=-1)
    total = lax.dynamic_index_in_dim(squares, y, 0, keepdims=False)
    for k in (1, 2, 3):
        total += y_shift(lax.dynamic_index_in_dim(squares, (y + k) % 4, 0, keepdims=False), k)
    scale = lax.rsqrt(total / 8192.0 + norm_eps)[:, None]

    own_slots = core * HALF + jnp.arange(HALF, dtype=jnp.int32)
    slot_k = jnp.concatenate([own_slots, (1 - core) * HALF + jnp.arange(HALF, dtype=jnp.int32)])
    allowed = (slot_k[None, :] <= own_slots[:, None]) & (slot_k[None, :] < lengths[0])
    bias = jnp.where(allowed, 0.0, -jnp.inf).astype(jnp.float32)
    cosine, sine = rope_tables(own_slots)

    kv_rows = key_value_rows(core, sums, scale, cosine, sine)
    kv_other = core_swap(kv_rows)
    own_a = attention(0, sums, scale, cosine, sine, bias, kv_rows, kv_other)
    far_a = zh_swap(own_a)
    own_b = attention(1, sums, scale, cosine, sine, bias, kv_rows, kv_other)
    far_b = zh_swap(own_b)
    attended = (own_a, own_b, far_a, far_b)

    def product(dz, dx, added=(), halves=False):
        return chunk((zl ^ dz, (x + dx) % 4), zh, attended, out_near, out_other, added, halves)

    low, high = product(1, 2, halves=True)
    beside_low, beside_high = x_shift(low, 1), x_shift(high, -1)
    low, high = product(0, 2, halves=True)
    beside_low, beside_high, low, high = lax.optimization_barrier(
        (beside_low, beside_high, low, high)
    )
    here_low, here_high = x_shift(low, 1), x_shift(high, -1)
    beside_a = x_shift(product(1, 1, [(beside_low, 0)]), 1)
    beside_b = x_shift(product(1, 3, [(beside_high, 1)]), -1)
    here_a = x_shift(product(0, 1, [(here_low, 0)]), 1)
    here_b = x_shift(product(0, 3, [(here_high, 1)]), -1)
    across = zl_swap(product(1, 0, [(beside_a, None), (beside_b, None)]))
    mixed = product(0, 0, [(here_a, None), (here_b, None), (across, None)])
    keep = send(half_of(mixed, core, 1), to_home(0))
    got = send(half_of(mixed, 1 - core, 1), to_home(1))
    return (wide + ordered(is_first, keep, got, 0).astype(jnp.float32)).astype(jnp.bfloat16)


def solution(mesh):
    split = Mesh(mesh.devices.reshape(SIZES), AXES)
    gx, gy = ("zl", "x", "core"), ("y", "zh")
    placed = (P(gy, gx), P(), P(gy, gx), P(gy, None), P(gx, gy), P(gy))
    return jax.shard_map(
        local, mesh=split, in_specs=placed, out_specs=P(gy, gx), check_vma=False
    )
```

```python
import jax
import jax.numpy as jnp
from jax import lax
from jax.experimental import pallas as pl
from jax.experimental.pallas import tpu as pltpu
from jax.sharding import Mesh, PartitionSpec as P

HEAD_SIZE = 128
SLOTS = 512
HALF = 256
AXES = ("zl", "x", "core", "y", "zh")
SIZES = (2, 4, 2, 4, 2)

rope_base = 500000.0
norm_eps = 1e-05


def coords(i):
    out = {}
    for name, size in zip(AXES[::-1], SIZES[::-1]):
        i, out[name] = divmod(i, size)
    return out


def index(c):
    i = 0
    for name, size in zip(AXES, SIZES):
        i = i * size + c[name] % size
    return i


def pairs(change):
    out = []
    for i in range(128):
        c = coords(i)
        out.append((i, index({**c, **change(c)})))
    return out


def send(value, change):
    return lax.ppermute(value, AXES, pairs(change))


def core_swap(value):
    return send(value, lambda c: dict(core=1 - c["core"]))


def zh_swap(value):
    return send(value, lambda c: dict(zh=1 - c["zh"]))


def zl_swap(value):
    return send(value, lambda c: dict(zl=1 - c["zl"]))


def x_shift(value, k):
    return send(value, lambda c: dict(x=c["x"] + k))


def after(value, other):
    return lax.optimization_barrier((value, other))[0]


def y_shift(value, k):
    return send(value, lambda c: dict(y=c["y"] + k))


def to_slice(flip):
    def change(c):
        return dict(
            y=2 * c["zl"] + c["x"] // 2,
            zl=c["y"] // 2,
            x=(c["y"] % 2) * 2 + c["x"] % 2,
            core=c["core"] ^ flip,
        )

    return change


def to_home(flip):
    def change(c):
        moves = c["x"] % 2 != c["zh"]
        return dict(x=c["x"] ^ moves, zh=c["zh"] ^ moves, core=c["core"] ^ flip)

    return change


def rope_tables(positions):
    half_dim = HEAD_SIZE // 2
    steps_up = jnp.arange(0, half_dim, dtype=jnp.float32) * (2.0 / HEAD_SIZE)
    inverse = jnp.power(jnp.float32(rope_base), -steps_up)
    angles = positions.astype(jnp.float32)[:, None] * inverse[None, :]
    cosine, sine = jnp.cos(angles), jnp.sin(angles)
    return jnp.concatenate([cosine, cosine], 1), jnp.concatenate([-sine, sine], 1)


def rotated(vectors, cosine, sine):
    return vectors * cosine + pltpu.roll(vectors, HEAD_SIZE // 2, 1) * sine


WIDE = 640
GRANT = pltpu.CompilerParams(vmem_limit_bytes=56 * 1024 * 1024)


def total_of(refs, cols=slice(None)):
    total = refs[0][:, cols].astype(jnp.float32)
    for ref in refs[1:]:
        total += ref[:, cols].astype(jnp.float32)
    return total


def key_value_kernel(core_ref, k0, k1, k2, v0, v1, v2, scale_ref, cos_ref, sin_ref, out_ref):
    scale = scale_ref[...]
    keys = rotated(total_of((k0, k1, k2)) * scale, cos_ref[...], sin_ref[...])
    out_ref[:, :HEAD_SIZE] = keys.astype(jnp.bfloat16)
    out_ref[:, HEAD_SIZE:] = (total_of((v0, v1, v2)) * scale).astype(jnp.bfloat16)


def key_value_rows(core, sums, scale, cosine, sine):
    keys = pl.BlockSpec((HALF, HEAD_SIZE), lambda i, c: (0, 4 + 5 * c[0]))
    values = pl.BlockSpec((HALF, HEAD_SIZE), lambda i, c: (0, 9 - 5 * c[0]))
    table = pl.BlockSpec((HALF, HEAD_SIZE), lambda i, c: (0, 0))
    return pl.pallas_call(
        key_value_kernel,
        grid_spec=pltpu.PrefetchScalarGridSpec(
            num_scalar_prefetch=1,
            grid=(1,),
            in_specs=[keys] * 3
            + [values] * 3
            + [pl.BlockSpec((HALF, 1), lambda i, c: (0, 0)), table, table],
            out_specs=pl.BlockSpec((HALF, 2 * HEAD_SIZE), lambda i, c: (0, 0)),
        ),
        out_shape=jax.ShapeDtypeStruct((HALF, 2 * HEAD_SIZE), jnp.bfloat16),
    )(core.reshape(1), *sums, *sums, scale, cosine, sine)


def attention_kernel(
    s0, s1, s2, scale_ref, cos_ref, sin_ref, bias_ref, own_ref, other_ref, out_ref
):
    contract = (((1,), (1,)), ((), ()))
    for head in range(4):
        cols = slice(head * HEAD_SIZE, (head + 1) * HEAD_SIZE)
        rows = total_of((s0, s1, s2), cols) * scale_ref[...]
        queries = rotated(rows, cos_ref[...], sin_ref[...]).astype(jnp.bfloat16)

        def scores_of(ref, first):
            scores = lax.dot_general(
                queries, ref[:, :HEAD_SIZE], contract, preferred_element_type=jnp.float32
            )
            return scores * (HEAD_SIZE**-0.5) + bias_ref[:, first : first + HALF]

        own, other = scores_of(own_ref, 0), scores_of(other_ref, HALF)
        top = jnp.maximum(
            jnp.max(own, axis=-1, keepdims=True), jnp.max(other, axis=-1, keepdims=True)
        )
        own, other = jnp.exp(own - top), jnp.exp(other - top)
        total = jnp.sum(own, axis=-1, keepdims=True) + jnp.sum(other, axis=-1, keepdims=True)
        mixed = dot(own.astype(jnp.bfloat16), own_ref[:, HEAD_SIZE:]) + dot(
            other.astype(jnp.bfloat16), other_ref[:, HEAD_SIZE:]
        )
        out_ref[:, cols] = (mixed / total).astype(jnp.bfloat16)


def attention(part, sums, scale, cosine, sine, bias, own, other):
    def fixed(shape):
        return pl.BlockSpec(shape, lambda i: (0, 0))

    return pl.pallas_call(
        attention_kernel,
        grid=(1,),
        in_specs=[pl.BlockSpec((HALF, WIDE), lambda i: (0, part))] * 3
        + [
            fixed((HALF, 1)),
            fixed((HALF, HEAD_SIZE)),
            fixed((HALF, HEAD_SIZE)),
            fixed((HALF, SLOTS)),
            fixed((HALF, 2 * HEAD_SIZE)),
            fixed((HALF, 2 * HEAD_SIZE)),
        ],
        out_specs=fixed((HALF, 512)),
        out_shape=jax.ShapeDtypeStruct((HALF, 512), jnp.bfloat16),
        compiler_params=GRANT,
    )(*sums, scale, cosine, sine, bias, own, other)


def project_kernel(steps, at_ref, rows_ref, near, near_other, far, far_other, *outs):
    zh = at_ref[0]
    near_rows = rows_ref[0, :, pl.ds(pl.multiple_of(zh * 1024, 1024), 1024)]
    far_rows = rows_ref[0, :, pl.ds(pl.multiple_of((1 - zh) * 1024, 1024), 1024)]
    own = (dot(near_rows, near[...]) + dot(far_rows, far[...])).astype(jnp.bfloat16)
    other = (dot(near_rows, near_other[...]) + dot(far_rows, far_other[...])).astype(jnp.bfloat16)
    if steps == 1:
        for half, out in enumerate(outs):
            out[:, :WIDE] = own[half * 128 : half * 128 + 128]
            out[:, WIDE:] = other[half * 128 : half * 128 + 128]
        return
    for step, out in enumerate(outs):

        @pl.when(pl.program_id(0) == step)
        def _():
            out[:, :WIDE] = own
            out[:, WIDE:] = other


def project(which, zh, gathered, weights):
    steps = len(which)
    rows = 128 if steps == 1 else HALF
    outs = 2 if steps == 1 else steps
    whole = pl.BlockSpec((1024, WIDE), lambda i, at: (0, 0))
    return pl.pallas_call(
        lambda *refs: project_kernel(steps, *refs),
        grid_spec=pltpu.PrefetchScalarGridSpec(
            num_scalar_prefetch=1,
            grid=(steps,),
            in_specs=[pl.BlockSpec((1, HALF, 2048), lambda i, at: (at[1 + i], 0, 0))] + [whole] * 4,
            out_specs=[pl.BlockSpec((rows, 2 * WIDE), lambda i, at: (0, 0))] * outs,
        ),
        out_shape=[jax.ShapeDtypeStruct((rows, 2 * WIDE), jnp.bfloat16)] * outs,
        compiler_params=GRANT,
    )(jnp.stack([zh, *which]).astype(jnp.int32), gathered, *weights)


def products_kernel(split, steps, at_ref, own_a, own_b, far_a, far_b, near, other, *refs):
    outs, rows = refs[:-1], refs[-1]
    step = pl.program_id(0)

    @pl.when(at_ref[steps + step] == 1)
    def _():
        rows[:, :512] = own_a[...]
        rows[:, 512:] = own_b[...]

    @pl.when(at_ref[steps + step] == 0)
    def _():
        rows[:, :512] = far_a[...]
        rows[:, 512:] = far_b[...]

    product = dot(rows[:, :512], near[0]) + dot(rows[:, 512:], other[0])
    product = product.astype(jnp.bfloat16)
    for i in range(steps):

        @pl.when(step == i)
        def _():
            if split:
                outs[0][i * 128 : i * 128 + 128] = product[:128]
                outs[1][i * 128 : i * 128 + 128] = product[128:]
            else:
                outs[i][...] = product


def products(targets, zh, attended, near, other, split=False):
    steps = len(targets)
    blocks = [zt * 2 + xt // 2 for zt, xt in targets]
    owns = [xt % 2 == zh for _, xt in targets]
    at = jnp.stack([v.astype(jnp.int32) for v in blocks + owns])
    rows = pl.BlockSpec((HALF, 512), lambda i, at: (0, 0))
    block = pl.BlockSpec((1, 512, 1024), lambda i, at: (at[i], 0, 0))
    count = 2 if split else steps
    return pl.pallas_call(
        lambda *refs: products_kernel(split, steps, *refs),
        grid_spec=pltpu.PrefetchScalarGridSpec(
            num_scalar_prefetch=1,
            grid=(steps,),
            in_specs=[rows] * 4 + [block] * 2,
            out_specs=[pl.BlockSpec((HALF, 1024), lambda i, at: (0, 0))] * count,
            scratch_shapes=[pltpu.VMEM((HALF, 1024), jnp.bfloat16)],
        ),
        out_shape=[jax.ShapeDtypeStruct((HALF, 1024), jnp.bfloat16)] * count,
        compiler_params=GRANT,
    )(at, *attended, near, other)


def add_rows(value, arrived, start):
    rows = arrived.shape[0]
    return lax.dynamic_update_slice(value, value[start : start + rows] + arrived, (start, 0))


def half_of(value, which, dim=0):
    size = value.shape[dim] // 2
    return lax.dynamic_slice_in_dim(value, which * size, size, dim)


def ordered(first, own, other, dim=0):
    return jnp.where(
        first, jnp.concatenate([own, other], dim), jnp.concatenate([other, own], dim)
    )


def dot(a, b):
    return jnp.dot(a, b, preferred_element_type=jnp.float32)


def local(tokens, norm_gain, query_weight, kv_weight, out_weight, lengths):
    core = lax.axis_index("core")
    chip = lax.axis_index(("zl", "x"))
    zl = lax.axis_index("zl")
    x = lax.axis_index("x")
    y = lax.axis_index("y")
    zh = lax.axis_index("zh")
    is_first = core == 0

    gain = lax.dynamic_slice_in_dim(norm_gain, (chip * 2 + core) * 512, 512, 0)
    wide = tokens.astype(jnp.float32)
    gained = (wide * gain[None, :]).astype(jnp.bfloat16)
    mine_out, theirs_out = half_of(gained, core), half_of(gained, 1 - core)
    mine = send(mine_out, to_slice(0))
    theirs = send(theirs_out, to_slice(1))
    block = ordered(is_first, mine, theirs, 1)

    kv_own = lax.dynamic_slice_in_dim(kv_weight, chip * 256 + core * 128, 128, 1)
    near = after(jnp.concatenate([query_weight, kv_own], axis=1), (mine_out, theirs_out))
    far_top = zh_swap(near[:512])
    near_other = core_swap(near)
    block, far_top, near_other = lax.optimization_barrier((block, far_top, near_other))

    beside = zl_swap(block)
    left = x_shift(block, 1)
    right = x_shift(block, -1)
    left, right, beside = lax.optimization_barrier((left, right, beside))
    far_bottom = zh_swap(after(near[512:], beside))
    beside_left = x_shift(beside, 1)
    beside_right = x_shift(beside, -1)
    opposite = jnp.concatenate([x_shift(left[:128], 1), x_shift(right[128:], -1)], 0)
    beside_opposite = jnp.concatenate(
        [x_shift(beside_left[:128], 1), x_shift(beside_right[128:], -1)], 0
    )
    gathered = jnp.zeros((4, HALF, 2048), jnp.bfloat16)
    for dz, dx, part in (
        (0, 0, block),
        (0, 3, left),
        (0, 1, right),
        (1, 0, beside),
        (0, 2, opposite),
        (1, 3, beside_left),
        (1, 1, beside_right),
        (1, 2, beside_opposite),
    ):
        zs, xs = zl ^ dz, (x + dx) % 4
        gathered = lax.dynamic_update_slice(
            gathered, part[None], (zs * 2 + xs // 2, 0, (xs % 2) * 1024)
        )

    far = jnp.concatenate([far_top, far_bottom], axis=0)
    weights = (near, near_other, far, core_swap(far))

    out_near = lax.all_gather(out_weight, "y", axis=0, tiled=False)

    low, high = project([(y + 2) % 4], zh, gathered, weights)
    from_below = y_shift(low, 1)
    from_above = y_shift(high, -1)
    upper, lower, kept = project([(y + 1) % 4, (y + 3) % 4, y], zh, gathered, weights)
    from_below, from_above, upper, lower, kept = lax.optimization_barrier(
        (from_below, from_above, upper, lower, kept)
    )
    out_other = core_swap(after(out_near, (from_below, from_above)))
    upper = add_rows(upper, from_below, 0)
    lower = add_rows(lower, from_above, 128)
    sums = (kept, y_shift(upper, 1), y_shift(lower, -1))

    slice_gain = lax.dynamic_slice_in_dim(norm_gain, y * 2048, 2048, 0)
    plain = gathered.astype(jnp.float32) * (1.0 / slice_gain)
    squares = jnp.sum(plain * plain, axis=-1)
    total = lax.dynamic_index_in_dim(squares, y, 0, keepdims=False)
    for k in (1, 2, 3):
        total += y_shift(lax.dynamic_index_in_dim(squares, (y + k) % 4, 0, keepdims=False), k)
    scale = lax.rsqrt(total / 8192.0 + norm_eps)[:, None]

    own_slots = core * HALF + jnp.arange(HALF, dtype=jnp.int32)
    slot_k = jnp.concatenate([own_slots, (1 - core) * HALF + jnp.arange(HALF, dtype=jnp.int32)])
    allowed = (slot_k[None, :] <= own_slots[:, None]) & (slot_k[None, :] < lengths[0])
    bias = jnp.where(allowed, 0.0, -jnp.inf).astype(jnp.float32)
    cosine, sine = rope_tables(own_slots)

    kv_rows = key_value_rows(core, sums, scale, cosine, sine)
    kv_other = core_swap(kv_rows)
    own_a = attention(0, sums, scale, cosine, sine, bias, kv_rows, kv_other)
    far_a = zh_swap(own_a)
    own_b = attention(1, sums, scale, cosine, sine, bias, kv_rows, kv_other)
    far_b = zh_swap(own_b)
    attended = (own_a, own_b, far_a, far_b)

    def made(moves, split=False):
        targets = [(zl ^ dz, (x + dx) % 4) for dz, dx in moves]
        return products(targets, zh, attended, out_near, out_other, split)

    low, high = made([(1, 2), (0, 2)], True)
    from_left, from_right = x_shift(low, 1), x_shift(high, -1)
    beside_a, beside_b, here_a, here_b, beside, mixed = made(
        [(1, 1), (1, 3), (0, 1), (0, 3), (1, 0), (0, 0)]
    )
    beside_a = x_shift(add_rows(beside_a, from_left[:128], 0), 1)
    beside_b = x_shift(add_rows(beside_b, from_right[:128], 128), -1)
    here_a = x_shift(add_rows(here_a, from_left[128:], 0), 1)
    here_b = x_shift(add_rows(here_b, from_right[128:], 128), -1)

    def sum_of(*values):
        return sum(v.astype(jnp.float32) for v in values).astype(jnp.bfloat16)

    across = zl_swap(sum_of(beside, beside_a, beside_b))
    mixed = sum_of(mixed, here_a, here_b, across)
    keep = send(half_of(mixed, core, 1), to_home(0))
    got = send(half_of(mixed, 1 - core, 1), to_home(1))
    return (wide + ordered(is_first, keep, got, 0).astype(jnp.float32)).astype(jnp.bfloat16)


def solution(mesh):
    split = Mesh(mesh.devices.reshape(SIZES), AXES)
    gx, gy = ("zl", "x", "core"), ("y", "zh")
    placed = (P(gy, gx), P(), P(gy, gx), P(gy, None), P(gx, gy), P(gy))
    return jax.shard_map(
        local, mesh=split, in_specs=placed, out_specs=P(gy, gx), check_vma=False
    )
```

```python
import jax
import jax.numpy as jnp
from jax import lax
from jax.experimental import pallas as pl
from jax.experimental.pallas import tpu as pltpu
from jax.sharding import Mesh, PartitionSpec as P

HEAD_SIZE = 128
SLOTS = 512
HALF = 256
AXES = ("zl", "x", "core", "y", "zh")
SIZES = (2, 4, 2, 4, 2)

rope_base = 500000.0
norm_eps = 1e-05


def coords(i):
    out = {}
    for name, size in zip(AXES[::-1], SIZES[::-1]):
        i, out[name] = divmod(i, size)
    return out


def index(c):
    i = 0
    for name, size in zip(AXES, SIZES):
        i = i * size + c[name] % size
    return i


def pairs(change):
    out = []
    for i in range(128):
        c = coords(i)
        out.append((i, index({**c, **change(c)})))
    return out


def send(value, change):
    return lax.ppermute(value, AXES, pairs(change))


def core_swap(value):
    return send(value, lambda c: dict(core=1 - c["core"]))


def zh_swap(value):
    return send(value, lambda c: dict(zh=1 - c["zh"]))


def zl_swap(value):
    return send(value, lambda c: dict(zl=1 - c["zl"]))


def x_shift(value, k):
    return send(value, lambda c: dict(x=c["x"] + k))


def after(value, other):
    return lax.optimization_barrier((value, other))[0]


def y_shift(value, k):
    return send(value, lambda c: dict(y=c["y"] + k))


def to_slice(flip):
    def change(c):
        return dict(
            y=2 * c["zl"] + c["x"] // 2,
            zl=c["y"] // 2,
            x=(c["y"] % 2) * 2 + c["x"] % 2,
            core=c["core"] ^ flip,
        )

    return change


def to_home(flip):
    def change(c):
        moves = c["x"] % 2 != c["zh"]
        return dict(x=c["x"] ^ moves, zh=c["zh"] ^ moves, core=c["core"] ^ flip)

    return change


def rope_tables(positions):
    half_dim = HEAD_SIZE // 2
    steps_up = jnp.arange(0, half_dim, dtype=jnp.float32) * (2.0 / HEAD_SIZE)
    inverse = jnp.power(jnp.float32(rope_base), -steps_up)
    angles = positions.astype(jnp.float32)[:, None] * inverse[None, :]
    cosine, sine = jnp.cos(angles), jnp.sin(angles)
    return jnp.concatenate([cosine, cosine], 1), jnp.concatenate([-sine, sine], 1)


def rotated(vectors, cosine, sine):
    return vectors * cosine + pltpu.roll(vectors, HEAD_SIZE // 2, 1) * sine


WIDE = 640
GRANT = pltpu.CompilerParams(vmem_limit_bytes=24 * 1024 * 1024)


def total_of(refs, cols=slice(None)):
    total = refs[0][:, cols].astype(jnp.float32)
    for ref in refs[1:]:
        total += ref[:, cols].astype(jnp.float32)
    return total


def key_value_kernel(core_ref, k0, k1, k2, v0, v1, v2, scale_ref, cos_ref, sin_ref, out_ref):
    scale = scale_ref[...]
    keys = rotated(total_of((k0, k1, k2)) * scale, cos_ref[...], sin_ref[...])
    out_ref[:, :HEAD_SIZE] = keys.astype(jnp.bfloat16)
    out_ref[:, HEAD_SIZE:] = (total_of((v0, v1, v2)) * scale).astype(jnp.bfloat16)


def key_value_rows(core, sums, scale, cosine, sine):
    keys = pl.BlockSpec((HALF, HEAD_SIZE), lambda i, c: (0, 4 + 5 * c[0]))
    values = pl.BlockSpec((HALF, HEAD_SIZE), lambda i, c: (0, 9 - 5 * c[0]))
    table = pl.BlockSpec((HALF, HEAD_SIZE), lambda i, c: (0, 0))
    return pl.pallas_call(
        key_value_kernel,
        grid_spec=pltpu.PrefetchScalarGridSpec(
            num_scalar_prefetch=1,
            grid=(1,),
            in_specs=[keys] * 3
            + [values] * 3
            + [pl.BlockSpec((HALF, 1), lambda i, c: (0, 0)), table, table],
            out_specs=pl.BlockSpec((HALF, 2 * HEAD_SIZE), lambda i, c: (0, 0)),
        ),
        out_shape=jax.ShapeDtypeStruct((HALF, 2 * HEAD_SIZE), jnp.bfloat16),
    )(core.reshape(1), *sums, *sums, scale, cosine, sine)


def attention_kernel(
    s0, s1, s2, scale_ref, cos_ref, sin_ref, bias_ref, own_ref, other_ref, out_ref
):
    contract = (((1,), (1,)), ((), ()))
    for head in range(4):
        cols = slice(head * HEAD_SIZE, (head + 1) * HEAD_SIZE)
        rows = total_of((s0, s1, s2), cols) * scale_ref[...]
        queries = rotated(rows, cos_ref[...], sin_ref[...]).astype(jnp.bfloat16)

        def scores_of(ref, first):
            scores = lax.dot_general(
                queries, ref[:, :HEAD_SIZE], contract, preferred_element_type=jnp.float32
            )
            return scores * (HEAD_SIZE**-0.5) + bias_ref[:, first : first + HALF]

        own, other = scores_of(own_ref, 0), scores_of(other_ref, HALF)
        top = jnp.maximum(
            jnp.max(own, axis=-1, keepdims=True), jnp.max(other, axis=-1, keepdims=True)
        )
        own, other = jnp.exp(own - top), jnp.exp(other - top)
        total = jnp.sum(own, axis=-1, keepdims=True) + jnp.sum(other, axis=-1, keepdims=True)
        mixed = dot(own.astype(jnp.bfloat16), own_ref[:, HEAD_SIZE:]) + dot(
            other.astype(jnp.bfloat16), other_ref[:, HEAD_SIZE:]
        )
        out_ref[:, cols] = (mixed / total).astype(jnp.bfloat16)


def attention(part, sums, scale, cosine, sine, bias, own, other):
    def fixed(shape):
        return pl.BlockSpec(shape, lambda i: (0, 0))

    return pl.pallas_call(
        attention_kernel,
        grid=(1,),
        in_specs=[pl.BlockSpec((HALF, WIDE), lambda i: (0, part))] * 3
        + [
            fixed((HALF, 1)),
            fixed((HALF, HEAD_SIZE)),
            fixed((HALF, HEAD_SIZE)),
            fixed((HALF, SLOTS)),
            fixed((HALF, 2 * HEAD_SIZE)),
            fixed((HALF, 2 * HEAD_SIZE)),
        ],
        out_specs=fixed((HALF, 512)),
        out_shape=jax.ShapeDtypeStruct((HALF, 512), jnp.bfloat16),
        compiler_params=GRANT,
    )(*sums, scale, cosine, sine, bias, own, other)


def project_kernel(steps, at_ref, rows_ref, near, near_other, far, far_other, *outs):
    zh = at_ref[0]
    near_rows = rows_ref[0, :, pl.ds(pl.multiple_of(zh * 1024, 1024), 1024)]
    far_rows = rows_ref[0, :, pl.ds(pl.multiple_of((1 - zh) * 1024, 1024), 1024)]
    own = (dot(near_rows, near[...]) + dot(far_rows, far[...])).astype(jnp.bfloat16)
    other = (dot(near_rows, near_other[...]) + dot(far_rows, far_other[...])).astype(jnp.bfloat16)
    if steps == 1:
        for half, out in enumerate(outs):
            out[:, :WIDE] = own[half * 128 : half * 128 + 128]
            out[:, WIDE:] = other[half * 128 : half * 128 + 128]
        return
    for step, out in enumerate(outs):

        @pl.when(pl.program_id(0) == step)
        def _():
            out[:, :WIDE] = own
            out[:, WIDE:] = other


def project(which, zh, gathered, weights):
    steps = len(which)
    rows = 128 if steps == 1 else HALF
    outs = 2 if steps == 1 else steps
    whole = pl.BlockSpec((1024, WIDE), lambda i, at: (0, 0))
    return pl.pallas_call(
        lambda *refs: project_kernel(steps, *refs),
        grid_spec=pltpu.PrefetchScalarGridSpec(
            num_scalar_prefetch=1,
            grid=(steps,),
            in_specs=[pl.BlockSpec((1, HALF, 2048), lambda i, at: (at[1 + i], 0, 0))] + [whole] * 4,
            out_specs=[pl.BlockSpec((rows, 2 * WIDE), lambda i, at: (0, 0))] * outs,
        ),
        out_shape=[jax.ShapeDtypeStruct((rows, 2 * WIDE), jnp.bfloat16)] * outs,
        compiler_params=GRANT,
    )(jnp.stack([zh, *which]).astype(jnp.int32), gathered, *weights)


def products_kernel(split, steps, at_ref, own_a, own_b, far_a, far_b, near, other, *outs):
    step = pl.program_id(0)

    def put(left, right):
        product = dot(left[...], near[0]) + dot(right[...], other[0])
        product = product.astype(jnp.bfloat16)
        for i in range(steps):

            @pl.when(step == i)
            def _():
                if split:
                    outs[0][i * 128 : i * 128 + 128] = product[:128]
                    outs[1][i * 128 : i * 128 + 128] = product[128:]
                else:
                    outs[i][...] = product

    @pl.when(at_ref[steps + step] == 1)
    def _():
        put(own_a, own_b)

    @pl.when(at_ref[steps + step] == 0)
    def _():
        put(far_a, far_b)


def products(targets, zh, attended, near, other, split=False):
    steps = len(targets)
    blocks = [zt * 2 + xt // 2 for zt, xt in targets]
    owns = [xt % 2 == zh for _, xt in targets]
    at = jnp.stack([v.astype(jnp.int32) for v in blocks + owns])
    rows = pl.BlockSpec((HALF, 512), lambda i, at: (0, 0))
    block = pl.BlockSpec((1, 512, 1024), lambda i, at: (at[i], 0, 0))
    count = 2 if split else steps
    return pl.pallas_call(
        lambda *refs: products_kernel(split, steps, *refs),
        grid_spec=pltpu.PrefetchScalarGridSpec(
            num_scalar_prefetch=1,
            grid=(steps,),
            in_specs=[rows] * 4 + [block] * 2,
            out_specs=[pl.BlockSpec((HALF, 1024), lambda i, at: (0, 0))] * count,
        ),
        out_shape=[jax.ShapeDtypeStruct((HALF, 1024), jnp.bfloat16)] * count,
        compiler_params=GRANT,
    )(at, *attended, near, other)


def add_rows(value, arrived, start):
    rows = arrived.shape[0]
    return lax.dynamic_update_slice(value, value[start : start + rows] + arrived, (start, 0))


def half_of(value, which, dim=0):
    size = value.shape[dim] // 2
    return lax.dynamic_slice_in_dim(value, which * size, size, dim)


def ordered(first, own, other, dim=0):
    return jnp.where(
        first, jnp.concatenate([own, other], dim), jnp.concatenate([other, own], dim)
    )


def dot(a, b):
    return jnp.dot(a, b, preferred_element_type=jnp.float32)


def local(tokens, norm_gain, query_weight, kv_weight, out_weight, lengths):
    core = lax.axis_index("core")
    chip = lax.axis_index(("zl", "x"))
    zl = lax.axis_index("zl")
    x = lax.axis_index("x")
    y = lax.axis_index("y")
    zh = lax.axis_index("zh")
    is_first = core == 0

    gain = lax.dynamic_slice_in_dim(norm_gain, (chip * 2 + core) * 512, 512, 0)
    wide = tokens.astype(jnp.float32)
    gained = (wide * gain[None, :]).astype(jnp.bfloat16)
    mine_out, theirs_out = half_of(gained, core), half_of(gained, 1 - core)
    mine = send(mine_out, to_slice(0))
    theirs = send(theirs_out, to_slice(1))
    block = ordered(is_first, mine, theirs, 1)

    kv_own = lax.dynamic_slice_in_dim(kv_weight, chip * 256 + core * 128, 128, 1)
    near = jnp.concatenate([query_weight, kv_own], axis=1)
    block, near = lax.optimization_barrier((block, near))
    near_other = core_swap(near)

    beside = zl_swap(block)
    left = x_shift(block, 1)
    right = x_shift(block, -1)
    left, right, near_other = lax.optimization_barrier((left, right, near_other))
    far = zh_swap(near)
    beside_left = x_shift(beside, 1)
    beside_right = x_shift(beside, -1)
    opposite = jnp.concatenate([x_shift(left[:128], 1), x_shift(right[128:], -1)], 0)
    beside_opposite = jnp.concatenate(
        [x_shift(beside_left[:128], 1), x_shift(beside_right[128:], -1)], 0
    )
    gathered = jnp.zeros((4, HALF, 2048), jnp.bfloat16)
    for dz, dx, part in (
        (0, 0, block),
        (0, 3, left),
        (0, 1, right),
        (1, 0, beside),
        (0, 2, opposite),
        (1, 3, beside_left),
        (1, 1, beside_right),
        (1, 2, beside_opposite),
    ):
        zs, xs = zl ^ dz, (x + dx) % 4
        gathered = lax.dynamic_update_slice(
            gathered, part[None], (zs * 2 + xs // 2, 0, (xs % 2) * 1024)
        )

    far = after(far, (opposite, beside_left, beside_right))
    weights = (near, near_other, far, core_swap(far))

    out_near = lax.all_gather(after(out_weight, block), "y", axis=0, tiled=False)

    low, high = project([(y + 2) % 4], zh, gathered, weights)
    from_below = y_shift(low, 1)
    from_above = y_shift(high, -1)
    upper, lower, kept = project([(y + 1) % 4, (y + 3) % 4, y], zh, gathered, weights)
    from_below, from_above, upper, lower, kept = lax.optimization_barrier(
        (from_below, from_above, upper, lower, kept)
    )
    out_other = core_swap(after(out_near, (from_below, from_above)))
    upper = add_rows(upper, from_below, 0)
    lower = add_rows(lower, from_above, 128)
    sums = (kept, y_shift(upper, 1), y_shift(lower, -1))

    slice_gain = lax.dynamic_slice_in_dim(norm_gain, y * 2048, 2048, 0)
    plain = gathered.astype(jnp.float32) * (1.0 / slice_gain)
    squares = jnp.sum(plain * plain, axis=-1)
    total = lax.dynamic_index_in_dim(squares, y, 0, keepdims=False)
    for k in (1, 2, 3):
        total += y_shift(lax.dynamic_index_in_dim(squares, (y + k) % 4, 0, keepdims=False), k)
    scale = lax.rsqrt(total / 8192.0 + norm_eps)[:, None]

    own_slots = core * HALF + jnp.arange(HALF, dtype=jnp.int32)
    slot_k = jnp.concatenate([own_slots, (1 - core) * HALF + jnp.arange(HALF, dtype=jnp.int32)])
    allowed = (slot_k[None, :] <= own_slots[:, None]) & (slot_k[None, :] < lengths[0])
    bias = jnp.where(allowed, 0.0, -jnp.inf).astype(jnp.float32)
    cosine, sine = rope_tables(own_slots)

    kv_rows = key_value_rows(core, sums, scale, cosine, sine)
    kv_other = core_swap(kv_rows)
    own_a = attention(0, sums, scale, cosine, sine, bias, kv_rows, kv_other)
    far_a = zh_swap(own_a)
    own_b = attention(1, sums, scale, cosine, sine, bias, kv_rows, kv_other)
    far_b = zh_swap(own_b)
    attended = (own_a, own_b, far_a, far_b)

    def made(moves, split=False):
        targets = [(zl ^ dz, (x + dx) % 4) for dz, dx in moves]
        return products(targets, zh, attended, out_near, out_other, split)

    low, high = made([(1, 2), (0, 2)], True)
    from_left, from_right = x_shift(low, 1), x_shift(high, -1)
    beside_a, beside_b, here_a, here_b, beside, mixed = made(
        [(1, 1), (1, 3), (0, 1), (0, 3), (1, 0), (0, 0)]
    )
    beside_a = x_shift(add_rows(beside_a, from_left[:128], 0), 1)
    beside_b = x_shift(add_rows(beside_b, from_right[:128], 128), -1)
    here_a = x_shift(add_rows(here_a, from_left[128:], 0), 1)
    here_b = x_shift(add_rows(here_b, from_right[128:], 128), -1)

    def sum_of(*values):
        return sum(v.astype(jnp.float32) for v in values).astype(jnp.bfloat16)

    across = zl_swap(sum_of(beside, beside_a, beside_b))
    mixed = sum_of(mixed, here_a, here_b, across)
    keep = send(half_of(mixed, core, 1), to_home(0))
    got = send(half_of(mixed, 1 - core, 1), to_home(1))
    return (wide + ordered(is_first, keep, got, 0).astype(jnp.float32)).astype(jnp.bfloat16)


def solution(mesh):
    split = Mesh(mesh.devices.reshape(SIZES), AXES)
    gx, gy = ("zl", "x", "core"), ("y", "zh")
    placed = (P(gy, gx), P(), P(gy, gx), P(gy, None), P(gx, gy), P(gy))
    return jax.shard_map(
        local, mesh=split, in_specs=placed, out_specs=P(gy, gx), check_vma=False
    )
```

```python
import jax
import jax.numpy as jnp
from jax import lax
from jax.experimental import pallas as pl
from jax.experimental.pallas import tpu as pltpu
from jax.sharding import Mesh, PartitionSpec as P

HEAD_SIZE = 128
SLOTS = 512
HALF = 256
AXES = ("zl", "x", "core", "y", "zh")
SIZES = (2, 4, 2, 4, 2)

rope_base = 500000.0
norm_eps = 1e-05


def coords(i):
    out = {}
    for name, size in zip(AXES[::-1], SIZES[::-1]):
        i, out[name] = divmod(i, size)
    return out


def index(c):
    i = 0
    for name, size in zip(AXES, SIZES):
        i = i * size + c[name] % size
    return i


def pairs(change):
    out = []
    for i in range(128):
        c = coords(i)
        out.append((i, index({**c, **change(c)})))
    return out


def send(value, change):
    return lax.ppermute(value, AXES, pairs(change))


def core_swap(value):
    return send(value, lambda c: dict(core=1 - c["core"]))


def zh_swap(value):
    return send(value, lambda c: dict(zh=1 - c["zh"]))


def zl_swap(value):
    return send(value, lambda c: dict(zl=1 - c["zl"]))


def x_shift(value, k):
    return send(value, lambda c: dict(x=c["x"] + k))


def after(value, other):
    return lax.optimization_barrier((value, other))[0]


def y_shift(value, k):
    return send(value, lambda c: dict(y=c["y"] + k))


def to_slice(flip):
    def change(c):
        return dict(
            y=2 * c["zl"] + c["x"] // 2,
            zl=c["y"] // 2,
            x=(c["y"] % 2) * 2 + c["x"] % 2,
            core=c["core"] ^ flip,
        )

    return change


def to_home(flip):
    def change(c):
        moves = c["x"] % 2 != c["zh"]
        return dict(x=c["x"] ^ moves, zh=c["zh"] ^ moves, core=c["core"] ^ flip)

    return change


def rope_tables(positions):
    half_dim = HEAD_SIZE // 2
    steps_up = jnp.arange(0, half_dim, dtype=jnp.float32) * (2.0 / HEAD_SIZE)
    inverse = jnp.power(jnp.float32(rope_base), -steps_up)
    angles = positions.astype(jnp.float32)[:, None] * inverse[None, :]
    cosine, sine = jnp.cos(angles), jnp.sin(angles)
    return jnp.concatenate([cosine, cosine], 1), jnp.concatenate([-sine, sine], 1)


def rotated(vectors, cosine, sine):
    return vectors * cosine + pltpu.roll(vectors, HEAD_SIZE // 2, 1) * sine


WIDE = 640
GRANT = pltpu.CompilerParams(vmem_limit_bytes=24 * 1024 * 1024)


def total_of(refs, cols=slice(None)):
    total = refs[0][:, cols].astype(jnp.float32)
    for ref in refs[1:]:
        total += ref[:, cols].astype(jnp.float32)
    return total


def key_value_kernel(core_ref, k0, k1, k2, v0, v1, v2, scale_ref, cos_ref, sin_ref, out_ref):
    scale = scale_ref[...]
    keys = rotated(total_of((k0, k1, k2)) * scale, cos_ref[...], sin_ref[...])
    out_ref[:, :HEAD_SIZE] = keys.astype(jnp.bfloat16)
    out_ref[:, HEAD_SIZE:] = (total_of((v0, v1, v2)) * scale).astype(jnp.bfloat16)


def key_value_rows(core, sums, scale, cosine, sine):
    keys = pl.BlockSpec((HALF, HEAD_SIZE), lambda i, c: (0, 4 + 5 * c[0]))
    values = pl.BlockSpec((HALF, HEAD_SIZE), lambda i, c: (0, 9 - 5 * c[0]))
    table = pl.BlockSpec((HALF, HEAD_SIZE), lambda i, c: (0, 0))
    return pl.pallas_call(
        key_value_kernel,
        grid_spec=pltpu.PrefetchScalarGridSpec(
            num_scalar_prefetch=1,
            grid=(1,),
            in_specs=[keys] * 3
            + [values] * 3
            + [pl.BlockSpec((HALF, 1), lambda i, c: (0, 0)), table, table],
            out_specs=pl.BlockSpec((HALF, 2 * HEAD_SIZE), lambda i, c: (0, 0)),
        ),
        out_shape=jax.ShapeDtypeStruct((HALF, 2 * HEAD_SIZE), jnp.bfloat16),
    )(core.reshape(1), *sums, *sums, scale, cosine, sine)


def attention_kernel(
    s0, s1, s2, scale_ref, cos_ref, sin_ref, bias_ref, own_ref, other_ref, out_ref
):
    contract = (((1,), (1,)), ((), ()))
    for head in range(4):
        cols = slice(head * HEAD_SIZE, (head + 1) * HEAD_SIZE)
        rows = total_of((s0, s1, s2), cols) * scale_ref[...]
        queries = rotated(rows, cos_ref[...], sin_ref[...]).astype(jnp.bfloat16)

        def scores_of(ref, first):
            scores = lax.dot_general(
                queries, ref[:, :HEAD_SIZE], contract, preferred_element_type=jnp.float32
            )
            return scores * (HEAD_SIZE**-0.5) + bias_ref[:, first : first + HALF]

        own, other = scores_of(own_ref, 0), scores_of(other_ref, HALF)
        top = jnp.maximum(
            jnp.max(own, axis=-1, keepdims=True), jnp.max(other, axis=-1, keepdims=True)
        )
        own, other = jnp.exp(own - top), jnp.exp(other - top)
        total = jnp.sum(own, axis=-1, keepdims=True) + jnp.sum(other, axis=-1, keepdims=True)
        mixed = dot(own.astype(jnp.bfloat16), own_ref[:, HEAD_SIZE:]) + dot(
            other.astype(jnp.bfloat16), other_ref[:, HEAD_SIZE:]
        )
        out_ref[:, cols] = (mixed / total).astype(jnp.bfloat16)


def attention(part, sums, scale, cosine, sine, bias, own, other):
    def fixed(shape):
        return pl.BlockSpec(shape, lambda i: (0, 0))

    return pl.pallas_call(
        attention_kernel,
        grid=(1,),
        in_specs=[pl.BlockSpec((HALF, WIDE), lambda i: (0, part))] * 3
        + [
            fixed((HALF, 1)),
            fixed((HALF, HEAD_SIZE)),
            fixed((HALF, HEAD_SIZE)),
            fixed((HALF, SLOTS)),
            fixed((HALF, 2 * HEAD_SIZE)),
            fixed((HALF, 2 * HEAD_SIZE)),
        ],
        out_specs=fixed((HALF, 512)),
        out_shape=jax.ShapeDtypeStruct((HALF, 512), jnp.bfloat16),
        compiler_params=GRANT,
    )(*sums, scale, cosine, sine, bias, own, other)


def project_kernel(at_ref, rows_ref, near, near_other, near_kv, far, far_other, *outs):
    zh, core = at_ref[0], at_ref[1]
    step = pl.program_id(0)
    near_rows = rows_ref[0, :, pl.ds(pl.multiple_of(zh * 1024, 1024), 1024)]
    far_rows = rows_ref[0, :, pl.ds(pl.multiple_of((1 - zh) * 1024, 1024), 1024)]

    def put(start, near_part, far_part):
        cols = slice(start, start + near_part.shape[1])
        value = (dot(near_rows, near_part) + dot(far_rows, far_part)).astype(jnp.bfloat16)
        if outs[0].shape[0] == 128:
            outs[0][:, cols] = value[:128]
            outs[1][:, cols] = value[128:]
        elif len(outs) == 1:
            outs[0][:, cols] = value
        else:
            for i, out in enumerate(outs):

                @pl.when(step == i)
                def _():
                    out[:, cols] = value

    def kv_cols(which):
        return near_kv[:, pl.ds(pl.multiple_of(which * HEAD_SIZE, HEAD_SIZE), HEAD_SIZE)]

    put(0, near[...], far[:, :512])
    put(512, kv_cols(core), far[:, 512:])
    put(WIDE, near_other[...], far_other[:, :512])
    put(WIDE + 512, kv_cols(1 - core), far_other[:, 512:])


def project(which, zh, core, gathered, weights, halves=False):
    steps = len(which)
    rows, outs = (128, 2) if halves else (HALF, steps)
    return pl.pallas_call(
        project_kernel,
        grid_spec=pltpu.PrefetchScalarGridSpec(
            num_scalar_prefetch=1,
            grid=(steps,),
            in_specs=[pl.BlockSpec((1, HALF, 2048), lambda i, at: (at[2 + i], 0, 0))]
            + [pl.BlockSpec(w.shape, lambda i, at: (0, 0)) for w in weights],
            out_specs=[pl.BlockSpec((rows, 2 * WIDE), lambda i, at: (0, 0))] * outs,
        ),
        out_shape=[jax.ShapeDtypeStruct((rows, 2 * WIDE), jnp.bfloat16)] * outs,
        compiler_params=GRANT,
    )(jnp.stack([zh, core, *which]).astype(jnp.int32), gathered, *weights)


def products_kernel(split, steps, at_ref, own_a, own_b, far_a, far_b, near, other, *outs):
    step = pl.program_id(0)

    def put(left, right):
        product = dot(left[...], near[0]) + dot(right[...], other[0])
        product = product.astype(jnp.bfloat16)
        for i in range(steps):

            @pl.when(step == i)
            def _():
                if split:
                    outs[0][i * 128 : i * 128 + 128] = product[:128]
                    outs[1][i * 128 : i * 128 + 128] = product[128:]
                else:
                    outs[i][...] = product

    @pl.when(at_ref[steps + step] == 1)
    def _():
        put(own_a, own_b)

    @pl.when(at_ref[steps + step] == 0)
    def _():
        put(far_a, far_b)


def products(targets, zh, attended, near, other, split=False):
    steps = len(targets)
    blocks = [zt * 2 + xt // 2 for zt, xt in targets]
    owns = [xt % 2 == zh for _, xt in targets]
    at = jnp.stack([v.astype(jnp.int32) for v in blocks + owns])
    rows = pl.BlockSpec((HALF, 512), lambda i, at: (0, 0))
    block = pl.BlockSpec((1, 512, 1024), lambda i, at: (at[i], 0, 0))
    count = 2 if split else steps
    return pl.pallas_call(
        lambda *refs: products_kernel(split, steps, *refs),
        grid_spec=pltpu.PrefetchScalarGridSpec(
            num_scalar_prefetch=1,
            grid=(steps,),
            in_specs=[rows] * 4 + [block] * 2,
            out_specs=[pl.BlockSpec((HALF, 1024), lambda i, at: (0, 0))] * count,
        ),
        out_shape=[jax.ShapeDtypeStruct((HALF, 1024), jnp.bfloat16)] * count,
        compiler_params=GRANT,
    )(at, *attended, near, other)


def add_rows(value, arrived, start):
    rows = arrived.shape[0]
    return lax.dynamic_update_slice(value, value[start : start + rows] + arrived, (start, 0))


def half_of(value, which, dim=0):
    size = value.shape[dim] // 2
    return lax.dynamic_slice_in_dim(value, which * size, size, dim)


def ordered(first, own, other, dim=0):
    return jnp.where(
        first, jnp.concatenate([own, other], dim), jnp.concatenate([other, own], dim)
    )


def dot(a, b):
    return jnp.dot(a, b, preferred_element_type=jnp.float32)


def local(tokens, norm_gain, query_weight, kv_weight, out_weight, lengths):
    core = lax.axis_index("core")
    chip = lax.axis_index(("zl", "x"))
    zl = lax.axis_index("zl")
    x = lax.axis_index("x")
    y = lax.axis_index("y")
    zh = lax.axis_index("zh")
    is_first = core == 0

    near_other = core_swap(query_weight)

    gain = lax.dynamic_slice_in_dim(norm_gain, (chip * 2 + core) * 512, 512, 0)
    wide = tokens.astype(jnp.float32)
    gained = (wide * gain[None, :]).astype(jnp.bfloat16)
    mine = send(half_of(gained, core), to_slice(0))
    theirs = send(half_of(gained, 1 - core), to_slice(1))
    block = ordered(is_first, mine, theirs, 1)

    kv_near = lax.dynamic_slice_in_dim(kv_weight, chip * 256, 256, 1)
    kv_own = lax.dynamic_slice_in_dim(kv_weight, chip * 256 + core * 128, 128, 1)
    near = jnp.concatenate([query_weight, kv_own], axis=1)
    slice_gain = 1.0 / lax.dynamic_slice_in_dim(norm_gain, y * 2048, 2048, 0)
    own_slots = core * HALF + jnp.arange(HALF, dtype=jnp.int32)
    slot_k = jnp.concatenate([own_slots, (1 - core) * HALF + jnp.arange(HALF, dtype=jnp.int32)])
    allowed = (slot_k[None, :] <= own_slots[:, None]) & (slot_k[None, :] < lengths[0])
    bias = jnp.where(allowed, 0.0, -jnp.inf).astype(jnp.float32)
    cosine, sine = rope_tables(own_slots)
    block, near_other, kv_near, near = lax.optimization_barrier((block, near_other, kv_near, near))
    block, slice_gain, bias, cosine, sine = lax.optimization_barrier(
        (block, slice_gain, bias, cosine, sine)
    )

    beside = zl_swap(block)
    left = x_shift(block, 1)
    right = x_shift(block, -1)
    far = zh_swap(near)
    left, right = lax.optimization_barrier((left, right))
    beside_left = x_shift(beside, 1)
    beside_right = x_shift(beside, -1)
    opposite = jnp.concatenate([x_shift(left[:128], 1), x_shift(right[128:], -1)], 0)
    beside_opposite = jnp.concatenate(
        [x_shift(beside_left[:128], 1), x_shift(beside_right[128:], -1)], 0
    )
    far = after(far, (opposite, beside_left, beside_right))
    weights = (query_weight, near_other, kv_near, far, core_swap(far))
    gathered = jnp.zeros((4, HALF, 2048), jnp.bfloat16)
    for dz, dx, part in (
        (0, 0, block),
        (0, 3, left),
        (0, 1, right),
        (1, 0, beside),
        (0, 2, opposite),
        (1, 3, beside_left),
        (1, 1, beside_right),
        (1, 2, beside_opposite),
    ):
        zs, xs = zl ^ dz, (x + dx) % 4
        gathered = lax.dynamic_update_slice(
            gathered, part[None], (zs * 2 + xs // 2, 0, (xs % 2) * 1024)
        )

    out_near = lax.all_gather(after(out_weight, block), "y", axis=0, tiled=False)

    low, high = project([(y + 2) % 4], zh, core, gathered, weights, True)
    from_below = y_shift(low, 1)
    from_above = y_shift(high, -1)
    upper, lower = project([(y + 1) % 4, (y + 3) % 4], zh, core, gathered, weights)
    from_below, from_above, upper, lower = lax.optimization_barrier(
        (from_below, from_above, upper, lower)
    )
    upper = add_rows(upper, from_below, 0)
    lower = add_rows(lower, from_above, 128)
    gathered, upper, lower = lax.optimization_barrier((gathered, upper, lower))
    (kept,) = project([y], zh, core, gathered, weights)
    sums = (kept, y_shift(upper, 1), y_shift(lower, -1))

    plain = gathered.astype(jnp.float32) * slice_gain
    squares = jnp.sum(plain * plain, axis=-1)
    total = lax.dynamic_index_in_dim(squares, y, 0, keepdims=False)
    for k in (1, 2, 3):
        total += y_shift(lax.dynamic_index_in_dim(squares, (y + k) % 4, 0, keepdims=False), k)
    scale = lax.rsqrt(total / 8192.0 + norm_eps)[:, None]

    kv_rows = key_value_rows(core, sums, scale, cosine, sine)
    kv_other = core_swap(kv_rows)
    out_other = core_swap(after(out_near, kv_other))
    own_a = attention(0, sums, scale, cosine, sine, bias, kv_rows, kv_other)
    far_a = zh_swap(own_a)
    own_b = attention(1, sums, scale, cosine, sine, bias, kv_rows, kv_other)
    far_b = zh_swap(own_b)
    attended = (own_a, own_b, far_a, far_b)

    def made(moves, split=False):
        targets = [(zl ^ dz, (x + dx) % 4) for dz, dx in moves]
        return products(targets, zh, attended, out_near, out_other, split)

    low, high = made([(1, 2), (0, 2)], True)
    from_left, from_right = x_shift(low, 1), x_shift(high, -1)
    beside_a, beside_b, here_a, here_b, beside, mixed = made(
        [(1, 1), (1, 3), (0, 1), (0, 3), (1, 0), (0, 0)]
    )
    beside_a = x_shift(add_rows(beside_a, from_left[:128], 0), 1)
    beside_b = x_shift(add_rows(beside_b, from_right[:128], 128), -1)
    here_a = x_shift(add_rows(here_a, from_left[128:], 0), 1)
    here_b = x_shift(add_rows(here_b, from_right[128:], 128), -1)

    def sum_of(*values):
        return sum(v.astype(jnp.float32) for v in values).astype(jnp.bfloat16)

    across = zl_swap(sum_of(beside, beside_a, beside_b))
    mixed = sum_of(mixed, here_a, here_b, across)
    keep = send(half_of(mixed, core, 1), to_home(0))
    got = send(half_of(mixed, 1 - core, 1), to_home(1))
    return (wide + ordered(is_first, keep, got, 0).astype(jnp.float32)).astype(jnp.bfloat16)


def solution(mesh):
    split = Mesh(mesh.devices.reshape(SIZES), AXES)
    gx, gy = ("zl", "x", "core"), ("y", "zh")
    placed = (P(gy, gx), P(), P(gy, gx), P(gy, None), P(gx, gy), P(gy))
    return jax.shard_map(
        local, mesh=split, in_specs=placed, out_specs=P(gy, gx), check_vma=False
    )
```

```python
import jax
import jax.numpy as jnp
from jax import lax
from jax.experimental import pallas as pl
from jax.experimental.pallas import tpu as pltpu
from jax.sharding import Mesh, PartitionSpec as P

HEAD_SIZE = 128
SLOTS = 512
HALF = 256
AXES = ("zl", "x", "core", "y", "zh")
SIZES = (2, 4, 2, 4, 2)

rope_base = 500000.0
norm_eps = 1e-05


def coords(i):
    out = {}
    for name, size in zip(AXES[::-1], SIZES[::-1]):
        i, out[name] = divmod(i, size)
    return out


def index(c):
    i = 0
    for name, size in zip(AXES, SIZES):
        i = i * size + c[name] % size
    return i


def pairs(change):
    out = []
    for i in range(128):
        c = coords(i)
        out.append((i, index({**c, **change(c)})))
    return out


def send(value, change):
    return lax.ppermute(value, AXES, pairs(change))


def core_swap(value):
    return send(value, lambda c: dict(core=1 - c["core"]))


def zh_swap(value):
    return send(value, lambda c: dict(zh=1 - c["zh"]))


def zl_swap(value):
    return send(value, lambda c: dict(zl=1 - c["zl"]))


def x_shift(value, k):
    return send(value, lambda c: dict(x=c["x"] + k))


def after(value, other):
    return lax.optimization_barrier((value, other))[0]


def y_shift(value, k):
    return send(value, lambda c: dict(y=c["y"] + k))


def to_slice(flip):
    def change(c):
        return dict(
            y=2 * c["zl"] + c["x"] // 2,
            zl=c["y"] // 2,
            x=(c["y"] % 2) * 2 + c["x"] % 2,
            core=c["core"] ^ flip,
        )

    return change


def to_home(flip):
    def change(c):
        moves = c["x"] % 2 != c["zh"]
        return dict(x=c["x"] ^ moves, zh=c["zh"] ^ moves, core=c["core"] ^ flip)

    return change


def rope_tables(positions):
    half_dim = HEAD_SIZE // 2
    steps_up = jnp.arange(0, half_dim, dtype=jnp.float32) * (2.0 / HEAD_SIZE)
    inverse = jnp.power(jnp.float32(rope_base), -steps_up)
    angles = positions.astype(jnp.float32)[:, None] * inverse[None, :]
    cosine, sine = jnp.cos(angles), jnp.sin(angles)
    return jnp.concatenate([cosine, cosine], 1), jnp.concatenate([-sine, sine], 1)


def rotated(vectors, cosine, sine):
    return vectors * cosine + pltpu.roll(vectors, HEAD_SIZE // 2, 1) * sine


WIDE = 640
GRANT = pltpu.CompilerParams(vmem_limit_bytes=24 * 1024 * 1024)


def total_of(refs, cols=slice(None)):
    total = refs[0][:, cols].astype(jnp.float32)
    for ref in refs[1:]:
        total += ref[:, cols].astype(jnp.float32)
    return total


def key_value_kernel(core_ref, k0, k1, k2, v0, v1, v2, scale_ref, cos_ref, sin_ref, out_ref):
    scale = scale_ref[...]
    keys = rotated(total_of((k0, k1, k2)) * scale, cos_ref[...], sin_ref[...])
    out_ref[:, :HEAD_SIZE] = keys.astype(jnp.bfloat16)
    out_ref[:, HEAD_SIZE:] = (total_of((v0, v1, v2)) * scale).astype(jnp.bfloat16)


def key_value_rows(core, sums, scale, cosine, sine):
    keys = pl.BlockSpec((HALF, HEAD_SIZE), lambda i, c: (0, 4 + 5 * c[0]))
    values = pl.BlockSpec((HALF, HEAD_SIZE), lambda i, c: (0, 9 - 5 * c[0]))
    table = pl.BlockSpec((HALF, HEAD_SIZE), lambda i, c: (0, 0))
    return pl.pallas_call(
        key_value_kernel,
        grid_spec=pltpu.PrefetchScalarGridSpec(
            num_scalar_prefetch=1,
            grid=(1,),
            in_specs=[keys] * 3
            + [values] * 3
            + [pl.BlockSpec((HALF, 1), lambda i, c: (0, 0)), table, table],
            out_specs=pl.BlockSpec((HALF, 2 * HEAD_SIZE), lambda i, c: (0, 0)),
        ),
        out_shape=jax.ShapeDtypeStruct((HALF, 2 * HEAD_SIZE), jnp.bfloat16),
    )(core.reshape(1), *sums, *sums, scale, cosine, sine)


def attention_kernel(
    s0, s1, s2, scale_ref, cos_ref, sin_ref, bias_ref, own_ref, other_ref, out_ref
):
    contract = (((1,), (1,)), ((), ()))
    for head in range(4):
        cols = slice(head * HEAD_SIZE, (head + 1) * HEAD_SIZE)
        rows = total_of((s0, s1, s2), cols) * scale_ref[...]
        queries = rotated(rows, cos_ref[...], sin_ref[...]).astype(jnp.bfloat16)

        def scores_of(ref, first):
            scores = lax.dot_general(
                queries, ref[:, :HEAD_SIZE], contract, preferred_element_type=jnp.float32
            )
            return scores * (HEAD_SIZE**-0.5) + bias_ref[:, first : first + HALF]

        own, other = scores_of(own_ref, 0), scores_of(other_ref, HALF)
        top = jnp.maximum(
            jnp.max(own, axis=-1, keepdims=True), jnp.max(other, axis=-1, keepdims=True)
        )
        own, other = jnp.exp(own - top), jnp.exp(other - top)
        total = jnp.sum(own, axis=-1, keepdims=True) + jnp.sum(other, axis=-1, keepdims=True)
        mixed = dot(own.astype(jnp.bfloat16), own_ref[:, HEAD_SIZE:]) + dot(
            other.astype(jnp.bfloat16), other_ref[:, HEAD_SIZE:]
        )
        out_ref[:, cols] = (mixed / total).astype(jnp.bfloat16)


def attention(part, sums, scale, cosine, sine, bias, own, other):
    def fixed(shape):
        return pl.BlockSpec(shape, lambda i: (0, 0))

    return pl.pallas_call(
        attention_kernel,
        grid=(1,),
        in_specs=[pl.BlockSpec((HALF, WIDE), lambda i: (0, part))] * 3
        + [
            fixed((HALF, 1)),
            fixed((HALF, HEAD_SIZE)),
            fixed((HALF, HEAD_SIZE)),
            fixed((HALF, SLOTS)),
            fixed((HALF, 2 * HEAD_SIZE)),
            fixed((HALF, 2 * HEAD_SIZE)),
        ],
        out_specs=fixed((HALF, 512)),
        out_shape=jax.ShapeDtypeStruct((HALF, 512), jnp.bfloat16),
        compiler_params=GRANT,
    )(*sums, scale, cosine, sine, bias, own, other)


def project_kernel(at_ref, rows_ref, near, near_other, near_kv, far, far_other, *outs):
    zh, core = at_ref[0], at_ref[1]
    step = pl.program_id(0)
    near_rows = rows_ref[0, :, pl.ds(pl.multiple_of(zh * 1024, 1024), 1024)]
    far_rows = rows_ref[0, :, pl.ds(pl.multiple_of((1 - zh) * 1024, 1024), 1024)]

    def put(start, near_part, far_part):
        cols = slice(start, start + near_part.shape[1])
        value = (dot(near_rows, near_part) + dot(far_rows, far_part)).astype(jnp.bfloat16)
        if outs[0].shape[0] == 128:
            outs[0][:, cols] = value[:128]
            outs[1][:, cols] = value[128:]
        elif len(outs) == 1:
            outs[0][:, cols] = value
        else:
            for i, out in enumerate(outs):

                @pl.when(step == i)
                def _():
                    out[:, cols] = value

    def kv_cols(which):
        return near_kv[:, pl.ds(pl.multiple_of(which * HEAD_SIZE, HEAD_SIZE), HEAD_SIZE)]

    put(0, near[...], far[:, :512])
    put(512, kv_cols(core), far[:, 512:])
    put(WIDE, near_other[...], far_other[:, :512])
    put(WIDE + 512, kv_cols(1 - core), far_other[:, 512:])


def project(which, zh, core, gathered, weights, halves=False):
    steps = len(which)
    rows, outs = (128, 2) if halves else (HALF, steps)
    return pl.pallas_call(
        project_kernel,
        grid_spec=pltpu.PrefetchScalarGridSpec(
            num_scalar_prefetch=1,
            grid=(steps,),
            in_specs=[pl.BlockSpec((1, HALF, 2048), lambda i, at: (at[2 + i], 0, 0))]
            + [pl.BlockSpec(w.shape, lambda i, at: (0, 0)) for w in weights],
            out_specs=[pl.BlockSpec((rows, 2 * WIDE), lambda i, at: (0, 0))] * outs,
        ),
        out_shape=[jax.ShapeDtypeStruct((rows, 2 * WIDE), jnp.bfloat16)] * outs,
        compiler_params=GRANT,
    )(jnp.stack([zh, core, *which]).astype(jnp.int32), gathered, *weights)


def halves_kernel(at_ref, own_a, own_b, far_a, far_b, near, other, low, high, held, sems):
    copies = []
    for i in range(2):
        for j, source in enumerate((near, other)):
            copy = pltpu.make_async_copy(source.at[at_ref[i]], held.at[i, j], sems.at[i, j])
            copy.start()
            copies.append(copy)

    def put(i, left, right):
        product = dot(left[...], held[i, 0]) + dot(right[...], held[i, 1])
        product = product.astype(jnp.bfloat16)
        low[i * 128 : i * 128 + 128] = product[:128]
        high[i * 128 : i * 128 + 128] = product[128:]

    for i in range(2):
        copies[2 * i].wait()
        copies[2 * i + 1].wait()

        @pl.when(at_ref[2 + i] == 1)
        def _():
            put(i, own_a, own_b)

        @pl.when(at_ref[2 + i] == 0)
        def _():
            put(i, far_a, far_b)


def products_kernel(steps, at_ref, own_a, own_b, far_a, far_b, near, other, *outs):
    step = pl.program_id(0)

    def put(left, right):
        product = dot(left[...], near[0]) + dot(right[...], other[0])
        product = product.astype(jnp.bfloat16)
        for i in range(steps):

            @pl.when(step == i)
            def _():
                outs[i][...] = product

    @pl.when(at_ref[steps + step] == 1)
    def _():
        put(own_a, own_b)

    @pl.when(at_ref[steps + step] == 0)
    def _():
        put(far_a, far_b)


def products(targets, zh, attended, near, other, split=False):
    steps = len(targets)
    blocks = [zt * 2 + xt // 2 for zt, xt in targets]
    owns = [xt % 2 == zh for _, xt in targets]
    at = jnp.stack([v.astype(jnp.int32) for v in blocks + owns])
    rows = pl.BlockSpec((HALF, 512), lambda i, at: (0, 0))
    block = pl.BlockSpec((1, 512, 1024), lambda i, at: (at[i], 0, 0))
    scratch = []
    if split:
        block = pl.BlockSpec(memory_space=pltpu.HBM)
        scratch = [
            pltpu.VMEM((2, 2, 512, 1024), jnp.bfloat16),
            pltpu.SemaphoreType.DMA((2, 2)),
        ]
    count = 2 if split else steps
    return pl.pallas_call(
        halves_kernel if split else lambda *refs: products_kernel(steps, *refs),
        grid_spec=pltpu.PrefetchScalarGridSpec(
            num_scalar_prefetch=1,
            grid=(1 if split else steps,),
            in_specs=[rows] * 4 + [block] * 2,
            out_specs=[pl.BlockSpec((HALF, 1024), lambda i, at: (0, 0))] * count,
            scratch_shapes=scratch,
        ),
        out_shape=[jax.ShapeDtypeStruct((HALF, 1024), jnp.bfloat16)] * count,
        compiler_params=GRANT,
    )(at, *attended, near, other)


def add_rows(value, arrived, start):
    rows = arrived.shape[0]
    return lax.dynamic_update_slice(value, value[start : start + rows] + arrived, (start, 0))


def half_of(value, which, dim=0):
    size = value.shape[dim] // 2
    return lax.dynamic_slice_in_dim(value, which * size, size, dim)


def ordered(first, own, other, dim=0):
    return jnp.where(
        first, jnp.concatenate([own, other], dim), jnp.concatenate([other, own], dim)
    )


def dot(a, b):
    return jnp.dot(a, b, preferred_element_type=jnp.float32)


def local(tokens, norm_gain, query_weight, kv_weight, out_weight, lengths):
    core = lax.axis_index("core")
    chip = lax.axis_index(("zl", "x"))
    zl = lax.axis_index("zl")
    x = lax.axis_index("x")
    y = lax.axis_index("y")
    zh = lax.axis_index("zh")
    is_first = core == 0

    near_other = core_swap(query_weight)

    gain = lax.dynamic_slice_in_dim(norm_gain, (chip * 2 + core) * 512, 512, 0)
    wide = tokens.astype(jnp.float32)
    gained = (wide * gain[None, :]).astype(jnp.bfloat16)
    mine = send(half_of(gained, core), to_slice(0))
    theirs = send(half_of(gained, 1 - core), to_slice(1))
    block = ordered(is_first, mine, theirs, 1)

    kv_near = lax.dynamic_slice_in_dim(kv_weight, chip * 256, 256, 1)
    kv_own = lax.dynamic_slice_in_dim(kv_weight, chip * 256 + core * 128, 128, 1)
    near = jnp.concatenate([query_weight, kv_own], axis=1)
    slice_gain = 1.0 / lax.dynamic_slice_in_dim(norm_gain, y * 2048, 2048, 0)
    own_slots = core * HALF + jnp.arange(HALF, dtype=jnp.int32)
    slot_k = jnp.concatenate([own_slots, (1 - core) * HALF + jnp.arange(HALF, dtype=jnp.int32)])
    allowed = (slot_k[None, :] <= own_slots[:, None]) & (slot_k[None, :] < lengths[0])
    bias = jnp.where(allowed, 0.0, -jnp.inf).astype(jnp.float32)
    cosine, sine = rope_tables(own_slots)
    block, near_other, kv_near, near = lax.optimization_barrier((block, near_other, kv_near, near))
    block, slice_gain, bias, cosine, sine = lax.optimization_barrier(
        (block, slice_gain, bias, cosine, sine)
    )

    beside = zl_swap(block)
    left = x_shift(block, 1)
    right = x_shift(block, -1)
    left, right, beside = lax.optimization_barrier((left, right, beside))
    far = zh_swap(after(near, beside))
    beside_left = x_shift(beside, 1)
    beside_right = x_shift(beside, -1)
    opposite = jnp.concatenate([x_shift(left[:128], 1), x_shift(right[128:], -1)], 0)
    beside_opposite = jnp.concatenate(
        [x_shift(beside_left[:128], 1), x_shift(beside_right[128:], -1)], 0
    )
    weights = (query_weight, near_other, kv_near, far, core_swap(after(far, beside_opposite)))
    gathered = jnp.zeros((4, HALF, 2048), jnp.bfloat16)
    for dz, dx, part in (
        (0, 0, block),
        (0, 3, left),
        (0, 1, right),
        (1, 0, beside),
        (0, 2, opposite),
        (1, 3, beside_left),
        (1, 1, beside_right),
        (1, 2, beside_opposite),
    ):
        zs, xs = zl ^ dz, (x + dx) % 4
        gathered = lax.dynamic_update_slice(
            gathered, part[None], (zs * 2 + xs // 2, 0, (xs % 2) * 1024)
        )

    out_near = lax.all_gather(after(out_weight, block), "y", axis=0, tiled=False)

    low, high = project([(y + 2) % 4], zh, core, gathered, weights, True)
    from_below = y_shift(low, 1)
    from_above = y_shift(high, -1)
    upper, lower = project([(y + 1) % 4, (y + 3) % 4], zh, core, gathered, weights)
    from_below, from_above, upper, lower = lax.optimization_barrier(
        (from_below, from_above, upper, lower)
    )
    upper = add_rows(upper, from_below, 0)
    lower = add_rows(lower, from_above, 128)
    gathered, upper, lower = lax.optimization_barrier((gathered, upper, lower))
    (kept,) = project([y], zh, core, gathered, weights)
    sums = (kept, y_shift(upper, 1), y_shift(lower, -1))

    plain = gathered.astype(jnp.float32) * slice_gain
    squares = jnp.sum(plain * plain, axis=-1)
    total = lax.dynamic_index_in_dim(squares, y, 0, keepdims=False)
    for k in (1, 2, 3):
        total += y_shift(lax.dynamic_index_in_dim(squares, (y + k) % 4, 0, keepdims=False), k)
    scale = lax.rsqrt(total / 8192.0 + norm_eps)[:, None]

    kv_rows = key_value_rows(core, sums, scale, cosine, sine)
    kv_other = core_swap(kv_rows)
    out_other = core_swap(after(out_near, kv_other))
    own_a = attention(0, sums, scale, cosine, sine, bias, kv_rows, kv_other)
    far_a = zh_swap(own_a)
    own_b = attention(1, sums, scale, cosine, sine, bias, kv_rows, kv_other)
    far_b = zh_swap(own_b)
    attended = (own_a, own_b, far_a, far_b)

    def made(moves, split=False):
        targets = [(zl ^ dz, (x + dx) % 4) for dz, dx in moves]
        return products(targets, zh, attended, out_near, out_other, split)

    low, high = made([(1, 2), (0, 2)], True)
    from_left, from_right = x_shift(low, 1), x_shift(high, -1)
    beside_a, beside_b, here_a, here_b, beside, mixed = made(
        [(1, 1), (1, 3), (0, 1), (0, 3), (1, 0), (0, 0)]
    )
    beside_a = x_shift(add_rows(beside_a, from_left[:128], 0), 1)
    beside_b = x_shift(add_rows(beside_b, from_right[:128], 128), -1)
    here_a = x_shift(add_rows(here_a, from_left[128:], 0), 1)
    here_b = x_shift(add_rows(here_b, from_right[128:], 128), -1)

    def sum_of(*values):
        return sum(v.astype(jnp.float32) for v in values).astype(jnp.bfloat16)

    across = zl_swap(sum_of(beside, beside_a, beside_b))
    mixed = sum_of(mixed, here_a, here_b, across)
    keep = send(half_of(mixed, core, 1), to_home(0))
    got = send(half_of(mixed, 1 - core, 1), to_home(1))
    return (wide + ordered(is_first, keep, got, 0).astype(jnp.float32)).astype(jnp.bfloat16)


def solution(mesh):
    split = Mesh(mesh.devices.reshape(SIZES), AXES)
    gx, gy = ("zl", "x", "core"), ("y", "zh")
    placed = (P(gy, gx), P(), P(gy, gx), P(gy, None), P(gx, gy), P(gy))
    return jax.shard_map(
        local, mesh=split, in_specs=placed, out_specs=P(gy, gx), check_vma=False
    )
```

```python
import jax
import jax.numpy as jnp
from jax import lax
from jax.experimental import pallas as pl
from jax.experimental.pallas import tpu as pltpu
from jax.sharding import Mesh, PartitionSpec as P

HEAD_SIZE = 128
SLOTS = 512
HALF = 256
AXES = ("zl", "x", "core", "y", "zh")
SIZES = (2, 4, 2, 4, 2)

rope_base = 500000.0
norm_eps = 1e-05


def coords(i):
    out = {}
    for name, size in zip(AXES[::-1], SIZES[::-1]):
        i, out[name] = divmod(i, size)
    return out


def index(c):
    i = 0
    for name, size in zip(AXES, SIZES):
        i = i * size + c[name] % size
    return i


def pairs(change):
    out = []
    for i in range(128):
        c = coords(i)
        out.append((i, index({**c, **change(c)})))
    return out


def send(value, change):
    return lax.ppermute(value, AXES, pairs(change))


def core_swap(value):
    return send(value, lambda c: dict(core=1 - c["core"]))


def zh_swap(value):
    return send(value, lambda c: dict(zh=1 - c["zh"]))


def zl_swap(value):
    return send(value, lambda c: dict(zl=1 - c["zl"]))


def x_shift(value, k):
    return send(value, lambda c: dict(x=c["x"] + k))


def after(value, other):
    return lax.optimization_barrier((value, other))[0]


def y_shift(value, k):
    return send(value, lambda c: dict(y=c["y"] + k))


def to_slice(flip):
    def change(c):
        return dict(
            y=2 * c["zl"] + c["x"] // 2,
            zl=c["y"] // 2,
            x=(c["y"] % 2) * 2 + c["x"] % 2,
            core=c["core"] ^ flip,
        )

    return change


def to_home(flip):
    def change(c):
        moves = c["x"] % 2 != c["zh"]
        return dict(x=c["x"] ^ moves, zh=c["zh"] ^ moves, core=c["core"] ^ flip)

    return change


def rope_tables(positions):
    half_dim = HEAD_SIZE // 2
    steps_up = jnp.arange(0, half_dim, dtype=jnp.float32) * (2.0 / HEAD_SIZE)
    inverse = jnp.power(jnp.float32(rope_base), -steps_up)
    angles = positions.astype(jnp.float32)[:, None] * inverse[None, :]
    cosine, sine = jnp.cos(angles), jnp.sin(angles)
    return jnp.concatenate([cosine, cosine], 1), jnp.concatenate([-sine, sine], 1)


def rotated(vectors, cosine, sine):
    return vectors * cosine + pltpu.roll(vectors, HEAD_SIZE // 2, 1) * sine


WIDE = 640
GRANT = pltpu.CompilerParams(vmem_limit_bytes=24 * 1024 * 1024)


def total_of(refs, cols=slice(None)):
    whole, *halves = (ref[:, cols].astype(jnp.float32) for ref in refs)
    a_top, a_bottom, b_top, b_bottom = halves
    return whole + jnp.concatenate([a_top + b_top, a_bottom + b_bottom], axis=0)


def total_kernel(*refs):
    refs[-1][...] = total_of(refs[:-1]).astype(jnp.bfloat16)


def summed_up(*values):
    return pl.pallas_call(
        total_kernel, out_shape=jax.ShapeDtypeStruct(values[0].shape, jnp.bfloat16)
    )(*values)


def key_value_kernel(core_ref, *refs):
    scale_ref, cos_ref, sin_ref, out_ref = refs[10:]
    scale = scale_ref[...]
    keys = rotated(total_of(refs[:5]) * scale, cos_ref[...], sin_ref[...])
    out_ref[:, :HEAD_SIZE] = keys.astype(jnp.bfloat16)
    out_ref[:, HEAD_SIZE:] = (total_of(refs[5:10]) * scale).astype(jnp.bfloat16)


def key_value_rows(core, sums, scale, cosine, sine):
    keys = [
        pl.BlockSpec((v.shape[0], HEAD_SIZE), lambda i, c: (0, 4 + 5 * c[0])) for v in sums
    ]
    values = [
        pl.BlockSpec((v.shape[0], HEAD_SIZE), lambda i, c: (0, 9 - 5 * c[0])) for v in sums
    ]
    table = pl.BlockSpec((HALF, HEAD_SIZE), lambda i, c: (0, 0))
    return pl.pallas_call(
        key_value_kernel,
        grid_spec=pltpu.PrefetchScalarGridSpec(
            num_scalar_prefetch=1,
            grid=(1,),
            in_specs=keys
            + values
            + [pl.BlockSpec((HALF, 1), lambda i, c: (0, 0)), table, table],
            out_specs=pl.BlockSpec((HALF, 2 * HEAD_SIZE), lambda i, c: (0, 0)),
        ),
        out_shape=jax.ShapeDtypeStruct((HALF, 2 * HEAD_SIZE), jnp.bfloat16),
    )(core.reshape(1), *sums, *sums, scale, cosine, sine)


def attention_kernel(*refs):
    scale_ref, cos_ref, sin_ref, bias_ref, own_ref, other_ref, out_ref = refs[5:]
    contract = (((1,), (1,)), ((), ()))
    for head in range(4):
        cols = slice(head * HEAD_SIZE, (head + 1) * HEAD_SIZE)
        rows = total_of(refs[:5], cols) * scale_ref[...]
        queries = rotated(rows, cos_ref[...], sin_ref[...]).astype(jnp.bfloat16)

        def scores_of(ref, first):
            scores = lax.dot_general(
                queries, ref[:, :HEAD_SIZE], contract, preferred_element_type=jnp.float32
            )
            return scores * (HEAD_SIZE**-0.5) + bias_ref[:, first : first + HALF]

        own, other = scores_of(own_ref, 0), scores_of(other_ref, HALF)
        top = jnp.maximum(
            jnp.max(own, axis=-1, keepdims=True), jnp.max(other, axis=-1, keepdims=True)
        )
        own, other = jnp.exp(own - top), jnp.exp(other - top)
        total = jnp.sum(own, axis=-1, keepdims=True) + jnp.sum(other, axis=-1, keepdims=True)
        mixed = dot(own.astype(jnp.bfloat16), own_ref[:, HEAD_SIZE:]) + dot(
            other.astype(jnp.bfloat16), other_ref[:, HEAD_SIZE:]
        )
        out_ref[:, cols] = (mixed / total).astype(jnp.bfloat16)


def attention(part, sums, scale, cosine, sine, bias, own, other):
    def fixed(shape):
        return pl.BlockSpec(shape, lambda i: (0, 0))

    return pl.pallas_call(
        attention_kernel,
        grid=(1,),
        in_specs=[pl.BlockSpec((v.shape[0], WIDE), lambda i: (0, part)) for v in sums]
        + [
            fixed((HALF, 1)),
            fixed((HALF, HEAD_SIZE)),
            fixed((HALF, HEAD_SIZE)),
            fixed((HALF, SLOTS)),
            fixed((HALF, 2 * HEAD_SIZE)),
            fixed((HALF, 2 * HEAD_SIZE)),
        ],
        out_specs=fixed((HALF, 512)),
        out_shape=jax.ShapeDtypeStruct((HALF, 512), jnp.bfloat16),
        compiler_params=GRANT,
    )(*sums, scale, cosine, sine, bias, own, other)


def project_kernel(at_ref, rows_ref, near, near_other, near_kv, far, far_other, *outs):
    zh, core = at_ref[0], at_ref[1]
    step = pl.program_id(0)
    near_rows = rows_ref[0, :, pl.ds(pl.multiple_of(zh * 1024, 1024), 1024)]
    far_rows = rows_ref[0, :, pl.ds(pl.multiple_of((1 - zh) * 1024, 1024), 1024)]

    def put(start, near_part, far_part):
        cols = slice(start, start + near_part.shape[1])
        value = (dot(near_rows, near_part) + dot(far_rows, far_part)).astype(jnp.bfloat16)
        if len(outs) == 1:
            outs[0][:, cols] = value
            return
        for i in range(len(outs) // 2):

            @pl.when(step == i)
            def _():
                outs[2 * i][:, cols] = value[:128]
                outs[2 * i + 1][:, cols] = value[128:]

    def kv_cols(which):
        return near_kv[:, pl.ds(pl.multiple_of(which * HEAD_SIZE, HEAD_SIZE), HEAD_SIZE)]

    put(0, near[...], far[:, :512])
    put(512, kv_cols(core), far[:, 512:])
    put(WIDE, near_other[...], far_other[:, :512])
    put(WIDE + 512, kv_cols(1 - core), far_other[:, 512:])


def project(which, zh, core, gathered, weights, halves=False):
    steps = len(which)
    rows, outs = (128, 2 * steps) if halves else (HALF, 1)
    return pl.pallas_call(
        project_kernel,
        grid_spec=pltpu.PrefetchScalarGridSpec(
            num_scalar_prefetch=1,
            grid=(steps,),
            in_specs=[pl.BlockSpec((1, HALF, 2048), lambda i, at: (at[2 + i], 0, 0))]
            + [pl.BlockSpec(w.shape, lambda i, at: (0, 0)) for w in weights],
            out_specs=[pl.BlockSpec((rows, 2 * WIDE), lambda i, at: (0, 0))] * outs,
        ),
        out_shape=[jax.ShapeDtypeStruct((rows, 2 * WIDE), jnp.bfloat16)] * outs,
        compiler_params=GRANT,
    )(jnp.stack([zh, core, *which]).astype(jnp.int32), gathered, *weights)


def products_kernel(form, steps, at_ref, own_a, own_b, far_a, far_b, near, other, *outs):
    step = pl.program_id(0)

    def put(left, right):
        product = dot(left[...], near[0]) + dot(right[...], other[0])
        product = product.astype(jnp.bfloat16)
        for i in range(steps):

            @pl.when(step == i)
            def _():
                if form == "joined":
                    outs[0][i * 128 : i * 128 + 128] = product[:128]
                    outs[1][i * 128 : i * 128 + 128] = product[128:]
                elif form == "halves":
                    outs[2 * i][...] = product[:128]
                    outs[2 * i + 1][...] = product[128:]
                else:
                    outs[i][...] = product

    @pl.when(at_ref[steps + step] == 1)
    def _():
        put(own_a, own_b)

    @pl.when(at_ref[steps + step] == 0)
    def _():
        put(far_a, far_b)


def products(targets, zh, attended, near, other, form="whole"):
    steps = len(targets)
    blocks = [zt * 2 + xt // 2 for zt, xt in targets]
    owns = [xt % 2 == zh for _, xt in targets]
    at = jnp.stack([v.astype(jnp.int32) for v in blocks + owns])
    rows = pl.BlockSpec((HALF, 512), lambda i, at: (0, 0))
    block = pl.BlockSpec((1, 512, 1024), lambda i, at: (at[i], 0, 0))
    count = {"joined": 2, "halves": 2 * steps, "whole": steps}[form]
    size = 128 if form == "halves" else HALF
    return pl.pallas_call(
        lambda *refs: products_kernel(form, steps, *refs),
        grid_spec=pltpu.PrefetchScalarGridSpec(
            num_scalar_prefetch=1,
            grid=(steps,),
            in_specs=[rows] * 4 + [block] * 2,
            out_specs=[pl.BlockSpec((size, 1024), lambda i, at: (0, 0))] * count,
        ),
        out_shape=[jax.ShapeDtypeStruct((size, 1024), jnp.bfloat16)] * count,
        compiler_params=GRANT,
    )(at, *attended, near, other)


def add_rows(value, arrived, start):
    rows = arrived.shape[0]
    return lax.dynamic_update_slice(value, value[start : start + rows] + arrived, (start, 0))


def half_of(value, which, dim=0):
    size = value.shape[dim] // 2
    return lax.dynamic_slice_in_dim(value, which * size, size, dim)


def ordered(first, own, other, dim=0):
    return jnp.where(
        first, jnp.concatenate([own, other], dim), jnp.concatenate([other, own], dim)
    )


def dot(a, b):
    return jnp.dot(a, b, preferred_element_type=jnp.float32)


def local(tokens, norm_gain, query_weight, kv_weight, out_weight, lengths):
    core = lax.axis_index("core")
    chip = lax.axis_index(("zl", "x"))
    zl = lax.axis_index("zl")
    x = lax.axis_index("x")
    y = lax.axis_index("y")
    zh = lax.axis_index("zh")
    is_first = core == 0

    near_other = core_swap(query_weight)

    gain = lax.dynamic_slice_in_dim(norm_gain, (chip * 2 + core) * 512, 512, 0)
    wide = tokens.astype(jnp.float32)
    gained = (wide * gain[None, :]).astype(jnp.bfloat16)
    mine = send(half_of(gained, core), to_slice(0))
    theirs = send(half_of(gained, 1 - core), to_slice(1))
    block = ordered(is_first, mine, theirs, 1)

    kv_near = lax.dynamic_slice_in_dim(kv_weight, chip * 256, 256, 1)
    kv_own = lax.dynamic_slice_in_dim(kv_weight, chip * 256 + core * 128, 128, 1)
    near = jnp.concatenate([query_weight, kv_own], axis=1)
    slice_gain = 1.0 / lax.dynamic_slice_in_dim(norm_gain, y * 2048, 2048, 0)
    own_slots = core * HALF + jnp.arange(HALF, dtype=jnp.int32)
    slot_k = jnp.concatenate([own_slots, (1 - core) * HALF + jnp.arange(HALF, dtype=jnp.int32)])
    allowed = (slot_k[None, :] <= own_slots[:, None]) & (slot_k[None, :] < lengths[0])
    bias = jnp.where(allowed, 0.0, -jnp.inf).astype(jnp.float32)
    cosine, sine = rope_tables(own_slots)
    block, near_other, kv_near, near = lax.optimization_barrier((block, near_other, kv_near, near))
    block, slice_gain, bias, cosine, sine = lax.optimization_barrier(
        (block, slice_gain, bias, cosine, sine)
    )

    beside = zl_swap(block)
    left = x_shift(block, 1)
    right = x_shift(block, -1)
    left, right, beside = lax.optimization_barrier((left, right, beside))
    far = zh_swap(after(near, beside))
    beside_left = x_shift(beside, 1)
    beside_right = x_shift(beside, -1)
    opposite = jnp.concatenate([x_shift(left[:128], 1), x_shift(right[128:], -1)], 0)
    beside_opposite = jnp.concatenate(
        [x_shift(beside_left[:128], 1), x_shift(beside_right[128:], -1)], 0
    )
    weights = (query_weight, near_other, kv_near, far, core_swap(after(far, beside_opposite)))
    gathered = jnp.zeros((4, HALF, 2048), jnp.bfloat16)
    for dz, dx, part in (
        (0, 0, block),
        (0, 3, left),
        (0, 1, right),
        (1, 0, beside),
        (0, 2, opposite),
        (1, 3, beside_left),
        (1, 1, beside_right),
        (1, 2, beside_opposite),
    ):
        zs, xs = zl ^ dz, (x + dx) % 4
        gathered = lax.dynamic_update_slice(
            gathered, part[None], (zs * 2 + xs // 2, 0, (xs % 2) * 1024)
        )

    out_near = lax.all_gather(after(out_weight, block), "y", axis=0, tiled=False)

    squares = jnp.sum(jnp.square(gathered.astype(jnp.float32) * slice_gain), axis=-1)
    gathered, squares = lax.optimization_barrier((gathered, squares))
    low, high = project([(y + 2) % 4], zh, core, gathered, weights, True)
    from_below = y_shift(low, 1)
    from_above = y_shift(high, -1)
    a_top, a_bottom, b_top, b_bottom = project(
        [(y + 1) % 4, (y + 3) % 4], zh, core, gathered, weights, True
    )
    from_below, from_above, a_top, b_bottom = lax.optimization_barrier(
        (from_below, from_above, a_top, b_bottom)
    )
    a_bottom, b_top = y_shift(a_bottom, 1), y_shift(b_top, -1)
    a_top, b_bottom = a_top + from_below, b_bottom + from_above
    gathered = after(gathered, (a_top, b_bottom, a_bottom, b_top))
    (kept,) = project([y], zh, core, gathered, weights)
    sums = (kept, y_shift(a_top, 1), a_bottom, b_top, y_shift(b_bottom, -1))

    squares, a_top, b_bottom = lax.optimization_barrier((squares, a_top, b_bottom))
    total = lax.dynamic_index_in_dim(squares, y, 0, keepdims=False)
    for k in (1, 2, 3):
        total += y_shift(lax.dynamic_index_in_dim(squares, (y + k) % 4, 0, keepdims=False), k)
    scale = lax.rsqrt(total / 8192.0 + norm_eps)[:, None]

    kv_rows = key_value_rows(core, sums, scale, cosine, sine)
    kv_other = core_swap(kv_rows)
    out_other = core_swap(after(out_near, kv_other))
    own_a = attention(0, sums, scale, cosine, sine, bias, kv_rows, kv_other)
    far_a = zh_swap(own_a)
    own_b = attention(1, sums, scale, cosine, sine, bias, kv_rows, kv_other)
    far_b = zh_swap(own_b)
    attended = (own_a, own_b, far_a, far_b)

    def made(moves, form="whole"):
        targets = [(zl ^ dz, (x + dx) % 4) for dz, dx in moves]
        return products(targets, zh, attended, out_near, out_other, form)

    low, high = made([(1, 2), (0, 2)], "joined")
    from_left, from_right = x_shift(low, 1), x_shift(high, -1)
    a_top, a_bottom, b_top, b_bottom = made([(1, 1), (1, 3)], "halves")
    here_a, here_b, beside, mixed = made([(0, 1), (0, 3), (1, 0), (0, 0)])
    from_left, from_right, here_a, here_b = lax.optimization_barrier(
        (from_left, from_right, here_a, here_b)
    )
    a_bottom, b_top = x_shift(a_bottom, 1), x_shift(b_top, -1)
    a_top = x_shift(a_top + from_left[:128], 1)
    b_bottom = x_shift(b_bottom + from_right[:128], -1)
    here_a = x_shift(add_rows(here_a, from_left[128:], 0), 1)
    here_b = x_shift(add_rows(here_b, from_right[128:], 128), -1)

    def sum_of(*values):
        return sum(v.astype(jnp.float32) for v in values).astype(jnp.bfloat16)

    across = zl_swap(summed_up(beside, a_top, a_bottom, b_top, b_bottom))
    mixed = sum_of(mixed, here_a, here_b, across)
    keep = send(half_of(mixed, core, 1), to_home(0))
    got = send(half_of(mixed, 1 - core, 1), to_home(1))
    return (wide + ordered(is_first, keep, got, 0).astype(jnp.float32)).astype(jnp.bfloat16)


def solution(mesh):
    split = Mesh(mesh.devices.reshape(SIZES), AXES)
    gx, gy = ("zl", "x", "core"), ("y", "zh")
    placed = (P(gy, gx), P(), P(gy, gx), P(gy, None), P(gx, gy), P(gy))
    return jax.shard_map(
        local, mesh=split, in_specs=placed, out_specs=P(gy, gx), check_vma=False
    )
```

```python
import jax
import jax.numpy as jnp
from jax import lax
from jax.experimental import pallas as pl
from jax.experimental.pallas import tpu as pltpu
from jax.sharding import Mesh, PartitionSpec as P

HEAD_SIZE = 128
SLOTS = 512
HALF = 256
AXES = ("zl", "x", "core", "y", "zh")
SIZES = (2, 4, 2, 4, 2)

rope_base = 500000.0
norm_eps = 1e-05


def coords(i):
    out = {}
    for name, size in zip(AXES[::-1], SIZES[::-1]):
        i, out[name] = divmod(i, size)
    return out


def index(c):
    i = 0
    for name, size in zip(AXES, SIZES):
        i = i * size + c[name] % size
    return i


def pairs(change):
    out = []
    for i in range(128):
        c = coords(i)
        out.append((i, index({**c, **change(c)})))
    return out


def send(value, change):
    return lax.ppermute(value, AXES, pairs(change))


def core_swap(value):
    return send(value, lambda c: dict(core=1 - c["core"]))


def zh_swap(value):
    return send(value, lambda c: dict(zh=1 - c["zh"]))


def zl_swap(value):
    return send(value, lambda c: dict(zl=1 - c["zl"]))


def x_shift(value, k):
    return send(value, lambda c: dict(x=c["x"] + k))


def after(value, other):
    return lax.optimization_barrier((value, other))[0]


def y_shift(value, k):
    return send(value, lambda c: dict(y=c["y"] + k))


def to_slice(flip):
    def change(c):
        return dict(
            y=2 * c["zl"] + c["x"] // 2,
            zl=c["y"] // 2,
            x=(c["y"] % 2) * 2 + c["x"] % 2,
            core=c["core"] ^ flip,
        )

    return change


def to_home(flip):
    def change(c):
        moves = c["x"] % 2 != c["zh"]
        return dict(x=c["x"] ^ moves, zh=c["zh"] ^ moves, core=c["core"] ^ flip)

    return change


def rope_tables(positions):
    half_dim = HEAD_SIZE // 2
    steps_up = jnp.arange(0, half_dim, dtype=jnp.float32) * (2.0 / HEAD_SIZE)
    inverse = jnp.power(jnp.float32(rope_base), -steps_up)
    angles = positions.astype(jnp.float32)[:, None] * inverse[None, :]
    cosine, sine = jnp.cos(angles), jnp.sin(angles)
    return jnp.concatenate([cosine, cosine], 1), jnp.concatenate([-sine, sine], 1)


def rotated(vectors, cosine, sine):
    return vectors * cosine + pltpu.roll(vectors, HEAD_SIZE // 2, 1) * sine


WIDE = 640
GRANT = pltpu.CompilerParams(vmem_limit_bytes=24 * 1024 * 1024)


def total_of(refs, cols=slice(None)):
    whole, *halves = (ref[:, cols].astype(jnp.float32) for ref in refs)
    a_top, a_bottom, b_top, b_bottom = halves
    return whole + jnp.concatenate([a_top + b_top, a_bottom + b_bottom], axis=0)


def total_kernel(*refs):
    refs[-1][...] = total_of(refs[:-1]).astype(jnp.bfloat16)


def summed_up(*values):
    return pl.pallas_call(
        total_kernel, out_shape=jax.ShapeDtypeStruct(values[0].shape, jnp.bfloat16)
    )(*values)


def key_value_kernel(core_ref, *refs):
    scale_ref, cos_ref, sin_ref, out_ref = refs[10:]
    scale = scale_ref[...]
    keys = rotated(total_of(refs[:5]) * scale, cos_ref[...], sin_ref[...])
    out_ref[:, :HEAD_SIZE] = keys.astype(jnp.bfloat16)
    out_ref[:, HEAD_SIZE:] = (total_of(refs[5:10]) * scale).astype(jnp.bfloat16)


def key_value_rows(core, sums, scale, cosine, sine):
    keys = [
        pl.BlockSpec((v.shape[0], HEAD_SIZE), lambda i, c: (0, 4 + 5 * c[0])) for v in sums
    ]
    values = [
        pl.BlockSpec((v.shape[0], HEAD_SIZE), lambda i, c: (0, 9 - 5 * c[0])) for v in sums
    ]
    table = pl.BlockSpec((HALF, HEAD_SIZE), lambda i, c: (0, 0))
    return pl.pallas_call(
        key_value_kernel,
        grid_spec=pltpu.PrefetchScalarGridSpec(
            num_scalar_prefetch=1,
            grid=(1,),
            in_specs=keys
            + values
            + [pl.BlockSpec((HALF, 1), lambda i, c: (0, 0)), table, table],
            out_specs=pl.BlockSpec((HALF, 2 * HEAD_SIZE), lambda i, c: (0, 0)),
        ),
        out_shape=jax.ShapeDtypeStruct((HALF, 2 * HEAD_SIZE), jnp.bfloat16),
    )(core.reshape(1), *sums, *sums, scale, cosine, sine)


def attention_kernel(*refs):
    scale_ref, cos_ref, sin_ref, bias_ref, own_ref, other_ref, out_ref = refs[5:]
    contract = (((1,), (1,)), ((), ()))
    for head in range(4):
        cols = slice(head * HEAD_SIZE, (head + 1) * HEAD_SIZE)
        rows = total_of(refs[:5], cols) * scale_ref[...]
        queries = rotated(rows, cos_ref[...], sin_ref[...]).astype(jnp.bfloat16)

        def scores_of(ref, first):
            scores = lax.dot_general(
                queries, ref[:, :HEAD_SIZE], contract, preferred_element_type=jnp.float32
            )
            return scores * (HEAD_SIZE**-0.5) + bias_ref[:, first : first + HALF]

        own, other = scores_of(own_ref, 0), scores_of(other_ref, HALF)
        top = jnp.maximum(
            jnp.max(own, axis=-1, keepdims=True), jnp.max(other, axis=-1, keepdims=True)
        )
        own, other = jnp.exp(own - top), jnp.exp(other - top)
        total = jnp.sum(own, axis=-1, keepdims=True) + jnp.sum(other, axis=-1, keepdims=True)
        mixed = dot(own.astype(jnp.bfloat16), own_ref[:, HEAD_SIZE:]) + dot(
            other.astype(jnp.bfloat16), other_ref[:, HEAD_SIZE:]
        )
        out_ref[:, cols] = (mixed / total).astype(jnp.bfloat16)


def attention(part, sums, scale, cosine, sine, bias, own, other):
    def fixed(shape):
        return pl.BlockSpec(shape, lambda i: (0, 0))

    return pl.pallas_call(
        attention_kernel,
        grid=(1,),
        in_specs=[pl.BlockSpec((v.shape[0], WIDE), lambda i: (0, part)) for v in sums]
        + [
            fixed((HALF, 1)),
            fixed((HALF, HEAD_SIZE)),
            fixed((HALF, HEAD_SIZE)),
            fixed((HALF, SLOTS)),
            fixed((HALF, 2 * HEAD_SIZE)),
            fixed((HALF, 2 * HEAD_SIZE)),
        ],
        out_specs=fixed((HALF, 512)),
        out_shape=jax.ShapeDtypeStruct((HALF, 512), jnp.bfloat16),
        compiler_params=GRANT,
    )(*sums, scale, cosine, sine, bias, own, other)


def project_kernel(at_ref, rows_ref, near, near_other, near_kv, far, far_other, *outs):
    zh, core = at_ref[0], at_ref[1]
    step = pl.program_id(0)
    near_rows = rows_ref[0, :, pl.ds(pl.multiple_of(zh * 1024, 1024), 1024)]
    far_rows = rows_ref[0, :, pl.ds(pl.multiple_of((1 - zh) * 1024, 1024), 1024)]

    def put(start, near_part, far_part):
        cols = slice(start, start + near_part.shape[1])
        value = (dot(near_rows, near_part) + dot(far_rows, far_part)).astype(jnp.bfloat16)
        for i in range(3):

            @pl.when(step == i)
            def _():
                outs[2 * i][:, cols] = value[:128]
                outs[2 * i + 1][:, cols] = value[128:]

        @pl.when(step == 3)
        def _():
            outs[6][:, cols] = value

    def kv_cols(which):
        return near_kv[:, pl.ds(pl.multiple_of(which * HEAD_SIZE, HEAD_SIZE), HEAD_SIZE)]

    put(0, near[...], far[:, :512])
    put(512, kv_cols(core), far[:, 512:])
    put(WIDE, near_other[...], far_other[:, :512])
    put(WIDE + 512, kv_cols(1 - core), far_other[:, 512:])


def project(which, zh, core, gathered, weights):
    rows = [128] * 6 + [HALF]
    return pl.pallas_call(
        project_kernel,
        grid_spec=pltpu.PrefetchScalarGridSpec(
            num_scalar_prefetch=1,
            grid=(4,),
            in_specs=[pl.BlockSpec((1, HALF, 2048), lambda i, at: (at[2 + i], 0, 0))]
            + [pl.BlockSpec(w.shape, lambda i, at: (0, 0)) for w in weights],
            out_specs=[pl.BlockSpec((r, 2 * WIDE), lambda i, at: (0, 0)) for r in rows],
        ),
        out_shape=[jax.ShapeDtypeStruct((r, 2 * WIDE), jnp.bfloat16) for r in rows],
        compiler_params=GRANT,
    )(jnp.stack([zh, core, *which]).astype(jnp.int32), gathered, *weights)


def two_sums_kernel(a, b, c, d, first, second):
    for left, right, out in ((a, b, first), (c, d, second)):
        out[...] = (left[...].astype(jnp.float32) + right[...].astype(jnp.float32)).astype(
            jnp.bfloat16
        )


def two_sums(a, b, c, d):
    shape = jax.ShapeDtypeStruct(a.shape, jnp.bfloat16)
    return pl.pallas_call(two_sums_kernel, out_shape=[shape, shape])(a, b, c, d)


def products_kernel(form, steps, at_ref, own_a, own_b, far_a, far_b, near, other, *outs):
    step = pl.program_id(0)

    def put(left, right):
        product = dot(left[...], near[0]) + dot(right[...], other[0])
        product = product.astype(jnp.bfloat16)
        for i in range(steps):

            @pl.when(step == i)
            def _():
                if form == "joined":
                    outs[0][i * 128 : i * 128 + 128] = product[:128]
                    outs[1][i * 128 : i * 128 + 128] = product[128:]
                elif form == "halves":
                    outs[2 * i][...] = product[:128]
                    outs[2 * i + 1][...] = product[128:]
                else:
                    outs[i][...] = product

    @pl.when(at_ref[steps + step] == 1)
    def _():
        put(own_a, own_b)

    @pl.when(at_ref[steps + step] == 0)
    def _():
        put(far_a, far_b)


def products(targets, zh, attended, near, other, form="whole"):
    steps = len(targets)
    blocks = [zt * 2 + xt // 2 for zt, xt in targets]
    owns = [xt % 2 == zh for _, xt in targets]
    at = jnp.stack([v.astype(jnp.int32) for v in blocks + owns])
    rows = pl.BlockSpec((HALF, 512), lambda i, at: (0, 0))
    block = pl.BlockSpec((1, 512, 1024), lambda i, at: (at[i], 0, 0))
    count = {"joined": 2, "halves": 2 * steps, "whole": steps}[form]
    size = 128 if form == "halves" else HALF
    return pl.pallas_call(
        lambda *refs: products_kernel(form, steps, *refs),
        grid_spec=pltpu.PrefetchScalarGridSpec(
            num_scalar_prefetch=1,
            grid=(steps,),
            in_specs=[rows] * 4 + [block] * 2,
            out_specs=[pl.BlockSpec((size, 1024), lambda i, at: (0, 0))] * count,
        ),
        out_shape=[jax.ShapeDtypeStruct((size, 1024), jnp.bfloat16)] * count,
        compiler_params=GRANT,
    )(at, *attended, near, other)


def add_rows(value, arrived, start):
    rows = arrived.shape[0]
    return lax.dynamic_update_slice(value, value[start : start + rows] + arrived, (start, 0))


def half_of(value, which, dim=0):
    size = value.shape[dim] // 2
    return lax.dynamic_slice_in_dim(value, which * size, size, dim)


def ordered(first, own, other, dim=0):
    return jnp.where(
        first, jnp.concatenate([own, other], dim), jnp.concatenate([other, own], dim)
    )


def dot(a, b):
    return jnp.dot(a, b, preferred_element_type=jnp.float32)


def local(tokens, norm_gain, query_weight, kv_weight, out_weight, lengths):
    core = lax.axis_index("core")
    chip = lax.axis_index(("zl", "x"))
    zl = lax.axis_index("zl")
    x = lax.axis_index("x")
    y = lax.axis_index("y")
    zh = lax.axis_index("zh")
    is_first = core == 0

    near_other = core_swap(query_weight)

    gain = lax.dynamic_slice_in_dim(norm_gain, (chip * 2 + core) * 512, 512, 0)
    wide = tokens.astype(jnp.float32)
    gained = (wide * gain[None, :]).astype(jnp.bfloat16)
    mine = send(half_of(gained, core), to_slice(0))
    theirs = send(half_of(gained, 1 - core), to_slice(1))
    block = ordered(is_first, mine, theirs, 1)

    kv_near = lax.dynamic_slice_in_dim(kv_weight, chip * 256, 256, 1)
    kv_own = lax.dynamic_slice_in_dim(kv_weight, chip * 256 + core * 128, 128, 1)
    near = jnp.concatenate([query_weight, kv_own], axis=1)
    slice_gain = 1.0 / lax.dynamic_slice_in_dim(norm_gain, y * 2048, 2048, 0)
    own_slots = core * HALF + jnp.arange(HALF, dtype=jnp.int32)
    slot_k = jnp.concatenate([own_slots, (1 - core) * HALF + jnp.arange(HALF, dtype=jnp.int32)])
    allowed = (slot_k[None, :] <= own_slots[:, None]) & (slot_k[None, :] < lengths[0])
    bias = jnp.where(allowed, 0.0, -jnp.inf).astype(jnp.float32)
    cosine, sine = rope_tables(own_slots)
    block, near_other, kv_near, near = lax.optimization_barrier((block, near_other, kv_near, near))
    block, slice_gain, bias, cosine, sine = lax.optimization_barrier(
        (block, slice_gain, bias, cosine, sine)
    )

    beside = zl_swap(block)
    left = x_shift(block, 1)
    right = x_shift(block, -1)
    left, right, beside = lax.optimization_barrier((left, right, beside))
    far = zh_swap(after(near, beside))
    beside_left = x_shift(beside, 1)
    beside_right = x_shift(beside, -1)
    opposite = jnp.concatenate([x_shift(left[:128], 1), x_shift(right[128:], -1)], 0)

    def placed(whole, *parts):
        for dz, dx, part in parts:
            zs, xs = zl ^ dz, (x + dx) % 4
            whole = lax.dynamic_update_slice(
                whole, part[None], (zs * 2 + xs // 2, 0, (xs % 2) * 1024)
            )
        return whole

    gathered = placed(
        jnp.zeros((4, HALF, 2048), jnp.bfloat16),
        (0, 0, block),
        (0, 3, left),
        (0, 1, right),
        (1, 0, beside),
    )
    gathered, beside_left, beside_right = lax.optimization_barrier(
        (gathered, beside_left, beside_right)
    )
    beside_opposite = (x_shift(beside_left[:128], 1), x_shift(beside_right[128:], -1))
    gathered = placed(
        gathered, (0, 2, opposite), (1, 3, beside_left), (1, 1, beside_right)
    )
    gathered = placed(gathered, (1, 2, jnp.concatenate(beside_opposite, 0)))
    far_other = core_swap(after(far, beside_opposite))
    weights = (query_weight, near_other, kv_near, far, far_other)

    out_near = lax.all_gather(after(out_weight, block), "y", axis=0, tiled=False)

    squares = jnp.sum(jnp.square(gathered.astype(jnp.float32) * slice_gain), axis=-1)
    square_total = lax.dynamic_index_in_dim(squares, y, 0, keepdims=False)
    arrived = [
        y_shift(lax.dynamic_index_in_dim(squares, (y + k) % 4, 0, keepdims=False), k)
        for k in (1, 2, 3)
    ]
    gathered, arrived = lax.optimization_barrier((gathered, arrived))
    low, high, a_top, a_bottom, b_top, b_bottom, kept = project(
        [(y + 2) % 4, (y + 1) % 4, (y + 3) % 4, y], zh, core, gathered, weights
    )
    from_below = y_shift(low, 1)
    from_above = y_shift(high, -1)
    a_bottom, b_top = y_shift(a_bottom, 1), y_shift(b_top, -1)
    a_top, b_bottom = two_sums(a_top, from_below, b_bottom, from_above)
    sums = (kept, y_shift(a_top, 1), a_bottom, b_top, y_shift(b_bottom, -1))

    square_total += arrived[0] + arrived[1] + arrived[2]
    scale = lax.rsqrt(square_total / 8192.0 + norm_eps)[:, None]
    kv_rows = key_value_rows(core, sums, scale, cosine, sine)
    kv_other = core_swap(kv_rows)
    out_other = core_swap(after(out_near, kv_other))
    own_a = attention(0, sums, scale, cosine, sine, bias, kv_rows, kv_other)
    far_a = zh_swap(own_a)
    own_b = attention(1, sums, scale, cosine, sine, bias, kv_rows, kv_other)
    far_b = zh_swap(own_b)
    attended = (own_a, own_b, far_a, far_b)

    def made(moves, form="whole"):
        targets = [(zl ^ dz, (x + dx) % 4) for dz, dx in moves]
        return products(targets, zh, attended, out_near, out_other, form)

    low, high = made([(1, 2), (0, 2)], "joined")
    from_left, from_right = x_shift(low, 1), x_shift(high, -1)
    a_top, a_bottom, b_top, b_bottom = made([(1, 1), (1, 3)], "halves")
    here_a, here_b, beside, mixed = made([(0, 1), (0, 3), (1, 0), (0, 0)])
    from_left, from_right, here_a, here_b = lax.optimization_barrier(
        (from_left, from_right, here_a, here_b)
    )
    a_bottom, b_top = x_shift(a_bottom, 1), x_shift(b_top, -1)
    a_top = x_shift(a_top + from_left[:128], 1)
    b_bottom = x_shift(b_bottom + from_right[:128], -1)
    here_a = x_shift(add_rows(here_a, from_left[128:], 0), 1)
    here_b = x_shift(add_rows(here_b, from_right[128:], 128), -1)

    def sum_of(*values):
        return sum(v.astype(jnp.float32) for v in values).astype(jnp.bfloat16)

    across = zl_swap(summed_up(beside, a_top, a_bottom, b_top, b_bottom))
    mixed = sum_of(mixed, here_a, here_b, across)
    keep = send(half_of(mixed, core, 1), to_home(0))
    got = send(half_of(mixed, 1 - core, 1), to_home(1))
    return (wide + ordered(is_first, keep, got, 0).astype(jnp.float32)).astype(jnp.bfloat16)


def solution(mesh):
    split = Mesh(mesh.devices.reshape(SIZES), AXES)
    gx, gy = ("zl", "x", "core"), ("y", "zh")
    placed = (P(gy, gx), P(), P(gy, gx), P(gy, None), P(gx, gy), P(gy))
    return jax.shard_map(
        local, mesh=split, in_specs=placed, out_specs=P(gy, gx), check_vma=False
    )
```

```python
import jax
import jax.numpy as jnp
from jax import lax
from jax.experimental import pallas as pl
from jax.experimental.pallas import tpu as pltpu
from jax.sharding import Mesh, PartitionSpec as P

HEAD_SIZE = 128
SLOTS = 512
HALF = 256
AXES = ("zl", "x", "core", "y", "zh")
SIZES = (2, 4, 2, 4, 2)

rope_base = 500000.0
norm_eps = 1e-05


def coords(i):
    out = {}
    for name, size in zip(AXES[::-1], SIZES[::-1]):
        i, out[name] = divmod(i, size)
    return out


def index(c):
    i = 0
    for name, size in zip(AXES, SIZES):
        i = i * size + c[name] % size
    return i


def pairs(change):
    out = []
    for i in range(128):
        c = coords(i)
        out.append((i, index({**c, **change(c)})))
    return out


def send(value, change):
    return lax.ppermute(value, AXES, pairs(change))


def core_swap(value):
    return send(value, lambda c: dict(core=1 - c["core"]))


def zh_swap(value):
    return send(value, lambda c: dict(zh=1 - c["zh"]))


def zl_swap(value):
    return send(value, lambda c: dict(zl=1 - c["zl"]))


def x_shift(value, k):
    return send(value, lambda c: dict(x=c["x"] + k))


def after(value, other):
    return lax.optimization_barrier((value, other))[0]


def y_shift(value, k):
    return send(value, lambda c: dict(y=c["y"] + k))


def to_slice(flip):
    def change(c):
        return dict(
            y=2 * c["zl"] + c["x"] // 2,
            zl=c["y"] // 2,
            x=(c["y"] % 2) * 2 + c["x"] % 2,
            core=c["core"] ^ flip,
        )

    return change


def to_home(flip):
    def change(c):
        moves = c["x"] % 2 != c["zh"]
        return dict(x=c["x"] ^ moves, zh=c["zh"] ^ moves, core=c["core"] ^ flip)

    return change


def rope_tables(positions):
    half_dim = HEAD_SIZE // 2
    steps_up = jnp.arange(0, half_dim, dtype=jnp.float32) * (2.0 / HEAD_SIZE)
    inverse = jnp.power(jnp.float32(rope_base), -steps_up)
    angles = positions.astype(jnp.float32)[:, None] * inverse[None, :]
    cosine, sine = jnp.cos(angles), jnp.sin(angles)
    return jnp.concatenate([cosine, cosine], 1), jnp.concatenate([-sine, sine], 1)


def rotated(vectors, cosine, sine):
    return vectors * cosine + pltpu.roll(vectors, HEAD_SIZE // 2, 1) * sine


WIDE = 640
GRANT = pltpu.CompilerParams(vmem_limit_bytes=24 * 1024 * 1024)


def total_of(refs, cols=slice(None)):
    whole, *halves = (ref[:, cols].astype(jnp.float32) for ref in refs)
    a_top, a_bottom, b_top, b_bottom = halves
    return whole + jnp.concatenate([a_top + b_top, a_bottom + b_bottom], axis=0)


def total_kernel(*refs):
    refs[-1][...] = total_of(refs[:-1]).astype(jnp.bfloat16)


def summed_up(*values):
    return pl.pallas_call(
        total_kernel, out_shape=jax.ShapeDtypeStruct(values[0].shape, jnp.bfloat16)
    )(*values)


def key_value_kernel(core_ref, *refs):
    scale_ref, cos_ref, sin_ref, out_ref = refs[10:]
    scale = scale_ref[...]
    keys = rotated(total_of(refs[:5]) * scale, cos_ref[...], sin_ref[...])
    out_ref[:, :HEAD_SIZE] = keys.astype(jnp.bfloat16)
    out_ref[:, HEAD_SIZE:] = (total_of(refs[5:10]) * scale).astype(jnp.bfloat16)


def key_value_rows(core, sums, scale, cosine, sine):
    keys = [
        pl.BlockSpec((v.shape[0], HEAD_SIZE), lambda i, c: (0, 4 + 5 * c[0])) for v in sums
    ]
    values = [
        pl.BlockSpec((v.shape[0], HEAD_SIZE), lambda i, c: (0, 9 - 5 * c[0])) for v in sums
    ]
    table = pl.BlockSpec((HALF, HEAD_SIZE), lambda i, c: (0, 0))
    return pl.pallas_call(
        key_value_kernel,
        grid_spec=pltpu.PrefetchScalarGridSpec(
            num_scalar_prefetch=1,
            grid=(1,),
            in_specs=keys
            + values
            + [pl.BlockSpec((HALF, 1), lambda i, c: (0, 0)), table, table],
            out_specs=pl.BlockSpec((HALF, 2 * HEAD_SIZE), lambda i, c: (0, 0)),
        ),
        out_shape=jax.ShapeDtypeStruct((HALF, 2 * HEAD_SIZE), jnp.bfloat16),
    )(core.reshape(1), *sums, *sums, scale, cosine, sine)


def attention_kernel(*refs):
    scale_ref, cos_ref, sin_ref, bias_ref, own_ref, other_ref, out_ref = refs[5:]
    contract = (((1,), (1,)), ((), ()))
    for head in range(4):
        cols = slice(head * HEAD_SIZE, (head + 1) * HEAD_SIZE)
        rows = total_of(refs[:5], cols) * scale_ref[...]
        queries = rotated(rows, cos_ref[...], sin_ref[...]).astype(jnp.bfloat16)

        def scores_of(ref, first):
            scores = lax.dot_general(
                queries, ref[:, :HEAD_SIZE], contract, preferred_element_type=jnp.float32
            )
            return scores * (HEAD_SIZE**-0.5) + bias_ref[:, first : first + HALF]

        own, other = scores_of(own_ref, 0), scores_of(other_ref, HALF)
        top = jnp.maximum(
            jnp.max(own, axis=-1, keepdims=True), jnp.max(other, axis=-1, keepdims=True)
        )
        own, other = jnp.exp(own - top), jnp.exp(other - top)
        total = jnp.sum(own, axis=-1, keepdims=True) + jnp.sum(other, axis=-1, keepdims=True)
        mixed = dot(own.astype(jnp.bfloat16), own_ref[:, HEAD_SIZE:]) + dot(
            other.astype(jnp.bfloat16), other_ref[:, HEAD_SIZE:]
        )
        out_ref[:, cols] = (mixed / total).astype(jnp.bfloat16)


def attention(part, sums, scale, cosine, sine, bias, own, other):
    def fixed(shape):
        return pl.BlockSpec(shape, lambda i: (0, 0))

    return pl.pallas_call(
        attention_kernel,
        grid=(1,),
        in_specs=[pl.BlockSpec((v.shape[0], WIDE), lambda i: (0, part)) for v in sums]
        + [
            fixed((HALF, 1)),
            fixed((HALF, HEAD_SIZE)),
            fixed((HALF, HEAD_SIZE)),
            fixed((HALF, SLOTS)),
            fixed((HALF, 2 * HEAD_SIZE)),
            fixed((HALF, 2 * HEAD_SIZE)),
        ],
        out_specs=fixed((HALF, 512)),
        out_shape=jax.ShapeDtypeStruct((HALF, 512), jnp.bfloat16),
        compiler_params=GRANT,
    )(*sums, scale, cosine, sine, bias, own, other)


def project_kernel(at_ref, rows_ref, near, near_other, near_kv, far, far_other, *outs):
    zh, core = at_ref[0], at_ref[1]
    step = pl.program_id(0)
    near_rows = rows_ref[0, :, pl.ds(pl.multiple_of(zh * 1024, 1024), 1024)]
    far_rows = rows_ref[0, :, pl.ds(pl.multiple_of((1 - zh) * 1024, 1024), 1024)]

    def put(start, near_part, far_part):
        cols = slice(start, start + near_part.shape[1])
        value = (dot(near_rows, near_part) + dot(far_rows, far_part)).astype(jnp.bfloat16)
        for i in range(len(outs) // 2):

            @pl.when(step == i)
            def _():
                outs[2 * i][:, cols] = value[:128]
                outs[2 * i + 1][:, cols] = value[128:]

        if len(outs) % 2:

            @pl.when(step == len(outs) // 2)
            def _():
                outs[-1][:, cols] = value

    def kv_cols(which):
        return near_kv[:, pl.ds(pl.multiple_of(which * HEAD_SIZE, HEAD_SIZE), HEAD_SIZE)]

    put(0, near[...], far[:, :512])
    put(512, kv_cols(core), far[:, 512:])
    put(WIDE, near_other[...], far_other[:, :512])
    put(WIDE + 512, kv_cols(1 - core), far_other[:, 512:])


def project(which, zh, core, gathered, weights, whole_last=False):
    steps = len(which)
    rows = [128] * 2 * steps if not whole_last else [128] * 2 * (steps - 1) + [HALF]
    return pl.pallas_call(
        project_kernel,
        grid_spec=pltpu.PrefetchScalarGridSpec(
            num_scalar_prefetch=1,
            grid=(steps,),
            in_specs=[pl.BlockSpec((1, HALF, 2048), lambda i, at: (at[2 + i], 0, 0))]
            + [pl.BlockSpec(w.shape, lambda i, at: (0, 0)) for w in weights],
            out_specs=[pl.BlockSpec((r, 2 * WIDE), lambda i, at: (0, 0)) for r in rows],
        ),
        out_shape=[jax.ShapeDtypeStruct((r, 2 * WIDE), jnp.bfloat16) for r in rows],
        compiler_params=GRANT,
    )(jnp.stack([zh, core, *which]).astype(jnp.int32), gathered, *weights)


def two_sums_kernel(a, b, c, d, first, second):
    for left, right, out in ((a, b, first), (c, d, second)):
        out[...] = (left[...].astype(jnp.float32) + right[...].astype(jnp.float32)).astype(
            jnp.bfloat16
        )


def two_sums(a, b, c, d):
    shape = jax.ShapeDtypeStruct(a.shape, jnp.bfloat16)
    return pl.pallas_call(two_sums_kernel, out_shape=[shape, shape])(a, b, c, d)


def products_kernel(form, steps, at_ref, own_a, own_b, far_a, far_b, near, other, *outs):
    step = pl.program_id(0)

    def put(left, right):
        product = dot(left[...], near[0]) + dot(right[...], other[0])
        product = product.astype(jnp.bfloat16)
        for i in range(steps):

            @pl.when(step == i)
            def _():
                if form == "joined":
                    outs[0][i * 128 : i * 128 + 128] = product[:128]
                    outs[1][i * 128 : i * 128 + 128] = product[128:]
                elif form == "halves":
                    outs[2 * i][...] = product[:128]
                    outs[2 * i + 1][...] = product[128:]
                else:
                    outs[i][...] = product

    @pl.when(at_ref[steps + step] == 1)
    def _():
        put(own_a, own_b)

    @pl.when(at_ref[steps + step] == 0)
    def _():
        put(far_a, far_b)


def products(targets, zh, attended, near, other, form="whole"):
    steps = len(targets)
    blocks = [zt * 2 + xt // 2 for zt, xt in targets]
    owns = [xt % 2 == zh for _, xt in targets]
    at = jnp.stack([v.astype(jnp.int32) for v in blocks + owns])
    rows = pl.BlockSpec((HALF, 512), lambda i, at: (0, 0))
    block = pl.BlockSpec((1, 512, 1024), lambda i, at: (at[i], 0, 0))
    count = {"joined": 2, "halves": 2 * steps, "whole": steps}[form]
    size = 128 if form == "halves" else HALF
    return pl.pallas_call(
        lambda *refs: products_kernel(form, steps, *refs),
        grid_spec=pltpu.PrefetchScalarGridSpec(
            num_scalar_prefetch=1,
            grid=(steps,),
            in_specs=[rows] * 4 + [block] * 2,
            out_specs=[pl.BlockSpec((size, 1024), lambda i, at: (0, 0))] * count,
        ),
        out_shape=[jax.ShapeDtypeStruct((size, 1024), jnp.bfloat16)] * count,
        compiler_params=GRANT,
    )(at, *attended, near, other)


def add_rows(value, arrived, start):
    rows = arrived.shape[0]
    return lax.dynamic_update_slice(value, value[start : start + rows] + arrived, (start, 0))


def half_of(value, which, dim=0):
    size = value.shape[dim] // 2
    return lax.dynamic_slice_in_dim(value, which * size, size, dim)


def ordered(first, own, other, dim=0):
    return jnp.where(
        first, jnp.concatenate([own, other], dim), jnp.concatenate([other, own], dim)
    )


def dot(a, b):
    return jnp.dot(a, b, preferred_element_type=jnp.float32)


def local(tokens, norm_gain, query_weight, kv_weight, out_weight, lengths):
    core = lax.axis_index("core")
    chip = lax.axis_index(("zl", "x"))
    zl = lax.axis_index("zl")
    x = lax.axis_index("x")
    y = lax.axis_index("y")
    zh = lax.axis_index("zh")
    is_first = core == 0

    near_other = core_swap(query_weight)

    gain = lax.dynamic_slice_in_dim(norm_gain, (chip * 2 + core) * 512, 512, 0)
    wide = tokens.astype(jnp.float32)
    gained = (wide * gain[None, :]).astype(jnp.bfloat16)
    mine = send(half_of(gained, core), to_slice(0))
    theirs = send(half_of(gained, 1 - core), to_slice(1))
    block = ordered(is_first, mine, theirs, 1)

    kv_near = lax.dynamic_slice_in_dim(kv_weight, chip * 256, 256, 1)
    kv_own = lax.dynamic_slice_in_dim(kv_weight, chip * 256 + core * 128, 128, 1)
    near = jnp.concatenate([query_weight, kv_own], axis=1)
    slice_gain = 1.0 / lax.dynamic_slice_in_dim(norm_gain, y * 2048, 2048, 0)
    own_slots = core * HALF + jnp.arange(HALF, dtype=jnp.int32)
    slot_k = jnp.concatenate([own_slots, (1 - core) * HALF + jnp.arange(HALF, dtype=jnp.int32)])
    allowed = (slot_k[None, :] <= own_slots[:, None]) & (slot_k[None, :] < lengths[0])
    bias = jnp.where(allowed, 0.0, -jnp.inf).astype(jnp.float32)
    cosine, sine = rope_tables(own_slots)
    block, near_other, kv_near, near = lax.optimization_barrier((block, near_other, kv_near, near))
    block, slice_gain, bias, cosine, sine = lax.optimization_barrier(
        (block, slice_gain, bias, cosine, sine)
    )

    beside = zl_swap(block)
    left = x_shift(block, 1)
    right = x_shift(block, -1)
    left, right, beside = lax.optimization_barrier((left, right, beside))
    far = zh_swap(after(near, beside))
    beside_left = x_shift(beside, 1)
    beside_right = x_shift(beside, -1)
    opposite = jnp.concatenate([x_shift(left[:128], 1), x_shift(right[128:], -1)], 0)
    beside_opposite = jnp.concatenate(
        [x_shift(beside_left[:128], 1), x_shift(beside_right[128:], -1)], 0
    )
    weights = (query_weight, near_other, kv_near, far, core_swap(after(far, beside_opposite)))
    gathered = jnp.zeros((4, HALF, 2048), jnp.bfloat16)
    for dz, dx, part in (
        (0, 0, block),
        (0, 3, left),
        (0, 1, right),
        (1, 0, beside),
        (0, 2, opposite),
        (1, 3, beside_left),
        (1, 1, beside_right),
        (1, 2, beside_opposite),
    ):
        zs, xs = zl ^ dz, (x + dx) % 4
        gathered = lax.dynamic_update_slice(
            gathered, part[None], (zs * 2 + xs // 2, 0, (xs % 2) * 1024)
        )

    out_near = lax.all_gather(after(out_weight, block), "y", axis=0, tiled=False)

    squares = jnp.sum(jnp.square(gathered.astype(jnp.float32) * slice_gain), axis=-1)
    gathered, squares = lax.optimization_barrier((gathered, squares))
    low, high = project([(y + 2) % 4], zh, core, gathered, weights)
    from_below = y_shift(low, 1)
    from_above = y_shift(high, -1)
    a_top, a_bottom, b_top, b_bottom, kept = project(
        [(y + 1) % 4, (y + 3) % 4, y], zh, core, gathered, weights, True
    )
    from_below, from_above, a_top, b_bottom = lax.optimization_barrier(
        (from_below, from_above, a_top, b_bottom)
    )
    a_bottom, b_top = y_shift(a_bottom, 1), y_shift(b_top, -1)
    a_top, b_bottom = two_sums(a_top, from_below, b_bottom, from_above)
    squares, a_bottom, b_top = lax.optimization_barrier((squares, a_bottom, b_top))
    sums = (kept, y_shift(a_top, 1), a_bottom, b_top, y_shift(b_bottom, -1))

    squares, a_top, b_bottom = lax.optimization_barrier((squares, a_top, b_bottom))
    total = lax.dynamic_index_in_dim(squares, y, 0, keepdims=False)
    for k in (1, 2, 3):
        total += y_shift(lax.dynamic_index_in_dim(squares, (y + k) % 4, 0, keepdims=False), k)
    scale = lax.rsqrt(total / 8192.0 + norm_eps)[:, None]

    kv_rows = key_value_rows(core, sums, scale, cosine, sine)
    kv_other = core_swap(kv_rows)
    out_other = core_swap(after(out_near, kv_other))
    own_a = attention(0, sums, scale, cosine, sine, bias, kv_rows, kv_other)
    far_a = zh_swap(own_a)
    own_b = attention(1, sums, scale, cosine, sine, bias, kv_rows, kv_other)
    far_b = zh_swap(own_b)
    attended = (own_a, own_b, far_a, far_b)

    def made(moves, form="whole"):
        targets = [(zl ^ dz, (x + dx) % 4) for dz, dx in moves]
        return products(targets, zh, attended, out_near, out_other, form)

    low, high = made([(1, 2), (0, 2)], "joined")
    from_left, from_right = x_shift(low, 1), x_shift(high, -1)
    a_top, a_bottom, b_top, b_bottom = made([(1, 1), (1, 3)], "halves")
    here_a, here_b, beside, mixed = made([(0, 1), (0, 3), (1, 0), (0, 0)])
    from_left, from_right, here_a, here_b = lax.optimization_barrier(
        (from_left, from_right, here_a, here_b)
    )
    a_bottom, b_top = x_shift(a_bottom, 1), x_shift(b_top, -1)
    a_top = x_shift(a_top + from_left[:128], 1)
    b_bottom = x_shift(b_bottom + from_right[:128], -1)
    here_a = x_shift(add_rows(here_a, from_left[128:], 0), 1)
    here_b = x_shift(add_rows(here_b, from_right[128:], 128), -1)

    def sum_of(*values):
        return sum(v.astype(jnp.float32) for v in values).astype(jnp.bfloat16)

    across = zl_swap(summed_up(beside, a_top, a_bottom, b_top, b_bottom))
    mixed = sum_of(mixed, here_a, here_b, across)
    keep = send(half_of(mixed, core, 1), to_home(0))
    got = send(half_of(mixed, 1 - core, 1), to_home(1))
    return (wide + ordered(is_first, keep, got, 0).astype(jnp.float32)).astype(jnp.bfloat16)


def solution(mesh):
    split = Mesh(mesh.devices.reshape(SIZES), AXES)
    gx, gy = ("zl", "x", "core"), ("y", "zh")
    placed = (P(gy, gx), P(), P(gy, gx), P(gy, None), P(gx, gy), P(gy))
    return jax.shard_map(
        local, mesh=split, in_specs=placed, out_specs=P(gy, gx), check_vma=False
    )
```

```python
import jax
import jax.numpy as jnp
from jax import lax
from jax.experimental import pallas as pl
from jax.experimental.pallas import tpu as pltpu
from jax.sharding import Mesh, PartitionSpec as P

HEAD_SIZE = 128
SLOTS = 512
HALF = 256
AXES = ("zl", "x", "core", "y", "zh")
SIZES = (2, 4, 2, 4, 2)

rope_base = 500000.0
norm_eps = 1e-05


def coords(i):
    out = {}
    for name, size in zip(AXES[::-1], SIZES[::-1]):
        i, out[name] = divmod(i, size)
    return out


def index(c):
    i = 0
    for name, size in zip(AXES, SIZES):
        i = i * size + c[name] % size
    return i


def pairs(change):
    out = []
    for i in range(128):
        c = coords(i)
        out.append((i, index({**c, **change(c)})))
    return out


def send(value, change):
    return lax.ppermute(value, AXES, pairs(change))


def core_swap(value):
    return send(value, lambda c: dict(core=1 - c["core"]))


def zh_swap(value):
    return send(value, lambda c: dict(zh=1 - c["zh"]))


def zl_swap(value):
    return send(value, lambda c: dict(zl=1 - c["zl"]))


def x_shift(value, k):
    return send(value, lambda c: dict(x=c["x"] + k))


def after(value, other):
    return lax.optimization_barrier((value, other))[0]


def y_shift(value, k):
    return send(value, lambda c: dict(y=c["y"] + k))


def to_slice(flip):
    def change(c):
        return dict(
            y=2 * c["zl"] + c["x"] // 2,
            zl=c["y"] // 2,
            x=(c["y"] % 2) * 2 + c["x"] % 2,
            core=c["core"] ^ flip,
        )

    return change


def to_home(flip):
    def change(c):
        moves = c["x"] % 2 != c["zh"]
        return dict(x=c["x"] ^ moves, zh=c["zh"] ^ moves, core=c["core"] ^ flip)

    return change


def rope_tables(positions):
    half_dim = HEAD_SIZE // 2
    steps_up = jnp.arange(0, half_dim, dtype=jnp.float32) * (2.0 / HEAD_SIZE)
    inverse = jnp.power(jnp.float32(rope_base), -steps_up)
    angles = positions.astype(jnp.float32)[:, None] * inverse[None, :]
    cosine, sine = jnp.cos(angles), jnp.sin(angles)
    return jnp.concatenate([cosine, cosine], 1), jnp.concatenate([-sine, sine], 1)


def rotated(vectors, cosine, sine):
    return vectors * cosine + pltpu.roll(vectors, HEAD_SIZE // 2, 1) * sine


WIDE = 640
GRANT = pltpu.CompilerParams(vmem_limit_bytes=24 * 1024 * 1024)


def total_of(refs, cols=slice(None)):
    whole, *halves = (ref[:, cols].astype(jnp.float32) for ref in refs)
    a_top, a_bottom, b_top, b_bottom = halves
    return whole + jnp.concatenate([a_top + b_top, a_bottom + b_bottom], axis=0)


def total_kernel(*refs):
    refs[-1][...] = total_of(refs[:-1]).astype(jnp.bfloat16)


def summed_up(*values):
    return pl.pallas_call(
        total_kernel, out_shape=jax.ShapeDtypeStruct(values[0].shape, jnp.bfloat16)
    )(*values)


def key_value_kernel(core_ref, *refs):
    scale_ref, cos_ref, sin_ref, out_ref = refs[10:]
    scale = scale_ref[...]
    keys = rotated(total_of(refs[:5]) * scale, cos_ref[...], sin_ref[...])
    out_ref[:, :HEAD_SIZE] = keys.astype(jnp.bfloat16)
    out_ref[:, HEAD_SIZE:] = (total_of(refs[5:10]) * scale).astype(jnp.bfloat16)


def key_value_rows(core, sums, scale, cosine, sine):
    keys = [
        pl.BlockSpec((v.shape[0], HEAD_SIZE), lambda i, c: (0, 4 + 5 * c[0])) for v in sums
    ]
    values = [
        pl.BlockSpec((v.shape[0], HEAD_SIZE), lambda i, c: (0, 9 - 5 * c[0])) for v in sums
    ]
    table = pl.BlockSpec((HALF, HEAD_SIZE), lambda i, c: (0, 0))
    return pl.pallas_call(
        key_value_kernel,
        grid_spec=pltpu.PrefetchScalarGridSpec(
            num_scalar_prefetch=1,
            grid=(1,),
            in_specs=keys
            + values
            + [pl.BlockSpec((HALF, 1), lambda i, c: (0, 0)), table, table],
            out_specs=pl.BlockSpec((HALF, 2 * HEAD_SIZE), lambda i, c: (0, 0)),
        ),
        out_shape=jax.ShapeDtypeStruct((HALF, 2 * HEAD_SIZE), jnp.bfloat16),
    )(core.reshape(1), *sums, *sums, scale, cosine, sine)


def attention_kernel(*refs):
    scale_ref, cos_ref, sin_ref, bias_ref, own_ref, other_ref, out_ref = refs[5:]
    contract = (((1,), (1,)), ((), ()))
    for head in range(4):
        cols = slice(head * HEAD_SIZE, (head + 1) * HEAD_SIZE)
        rows = total_of(refs[:5], cols) * scale_ref[...]
        queries = rotated(rows, cos_ref[...], sin_ref[...]).astype(jnp.bfloat16)

        def scores_of(ref, first):
            scores = lax.dot_general(
                queries, ref[:, :HEAD_SIZE], contract, preferred_element_type=jnp.float32
            )
            return scores * (HEAD_SIZE**-0.5) + bias_ref[:, first : first + HALF]

        own, other = scores_of(own_ref, 0), scores_of(other_ref, HALF)
        top = jnp.maximum(
            jnp.max(own, axis=-1, keepdims=True), jnp.max(other, axis=-1, keepdims=True)
        )
        own, other = jnp.exp(own - top), jnp.exp(other - top)
        total = jnp.sum(own, axis=-1, keepdims=True) + jnp.sum(other, axis=-1, keepdims=True)
        mixed = dot(own.astype(jnp.bfloat16), own_ref[:, HEAD_SIZE:]) + dot(
            other.astype(jnp.bfloat16), other_ref[:, HEAD_SIZE:]
        )
        out_ref[:, cols] = (mixed / total).astype(jnp.bfloat16)


def attention(part, sums, scale, cosine, sine, bias, own, other):
    def fixed(shape):
        return pl.BlockSpec(shape, lambda i: (0, 0))

    return pl.pallas_call(
        attention_kernel,
        grid=(1,),
        in_specs=[pl.BlockSpec((v.shape[0], WIDE), lambda i: (0, part)) for v in sums]
        + [
            fixed((HALF, 1)),
            fixed((HALF, HEAD_SIZE)),
            fixed((HALF, HEAD_SIZE)),
            fixed((HALF, SLOTS)),
            fixed((HALF, 2 * HEAD_SIZE)),
            fixed((HALF, 2 * HEAD_SIZE)),
        ],
        out_specs=fixed((HALF, 512)),
        out_shape=jax.ShapeDtypeStruct((HALF, 512), jnp.bfloat16),
        compiler_params=GRANT,
    )(*sums, scale, cosine, sine, bias, own, other)


def project_kernel(at_ref, rows_ref, near, near_other, near_kv, far, far_other, *outs):
    zh, core = at_ref[0], at_ref[1]
    step = pl.program_id(0)
    near_rows = rows_ref[0, :, pl.ds(pl.multiple_of(zh * 1024, 1024), 1024)]
    far_rows = rows_ref[0, :, pl.ds(pl.multiple_of((1 - zh) * 1024, 1024), 1024)]

    def put(start, near_part, far_part):
        cols = slice(start, start + near_part.shape[1])
        value = (dot(near_rows, near_part) + dot(far_rows, far_part)).astype(jnp.bfloat16)
        if len(outs) == 1:
            outs[0][:, cols] = value
            return
        for i in range(len(outs) // 2):

            @pl.when(step == i)
            def _():
                outs[2 * i][:, cols] = value[:128]
                outs[2 * i + 1][:, cols] = value[128:]

    def kv_cols(which):
        return near_kv[:, pl.ds(pl.multiple_of(which * HEAD_SIZE, HEAD_SIZE), HEAD_SIZE)]

    put(0, near[...], far[:, :512])
    put(512, kv_cols(core), far[:, 512:])
    put(WIDE, near_other[...], far_other[:, :512])
    put(WIDE + 512, kv_cols(1 - core), far_other[:, 512:])


def project(which, zh, core, gathered, weights, halves=False):
    steps = len(which)
    rows, outs = (128, 2 * steps) if halves else (HALF, 1)
    return pl.pallas_call(
        project_kernel,
        grid_spec=pltpu.PrefetchScalarGridSpec(
            num_scalar_prefetch=1,
            grid=(steps,),
            in_specs=[pl.BlockSpec((1, HALF, 2048), lambda i, at: (at[2 + i], 0, 0))]
            + [pl.BlockSpec(w.shape, lambda i, at: (0, 0)) for w in weights],
            out_specs=[pl.BlockSpec((rows, 2 * WIDE), lambda i, at: (0, 0))] * outs,
        ),
        out_shape=[jax.ShapeDtypeStruct((rows, 2 * WIDE), jnp.bfloat16)] * outs,
        compiler_params=GRANT,
    )(jnp.stack([zh, core, *which]).astype(jnp.int32), gathered, *weights)


def products_kernel(form, steps, at_ref, own_a, own_b, far_a, far_b, near, other, *outs):
    step = pl.program_id(0)

    def put(left, right):
        product = dot(left[...], near[0]) + dot(right[...], other[0])
        product = product.astype(jnp.bfloat16)
        for i in range(steps):

            @pl.when(step == i)
            def _():
                if form == "joined":
                    outs[0][i * 128 : i * 128 + 128] = product[:128]
                    outs[1][i * 128 : i * 128 + 128] = product[128:]
                elif form == "halves":
                    outs[2 * i][...] = product[:128]
                    outs[2 * i + 1][...] = product[128:]
                else:
                    outs[i][...] = product

    @pl.when(at_ref[steps + step] == 1)
    def _():
        put(own_a, own_b)

    @pl.when(at_ref[steps + step] == 0)
    def _():
        put(far_a, far_b)


def products(targets, zh, attended, near, other, form="whole"):
    steps = len(targets)
    blocks = [zt * 2 + xt // 2 for zt, xt in targets]
    owns = [xt % 2 == zh for _, xt in targets]
    at = jnp.stack([v.astype(jnp.int32) for v in blocks + owns])
    rows = pl.BlockSpec((HALF, 512), lambda i, at: (0, 0))
    block = pl.BlockSpec((1, 512, 1024), lambda i, at: (at[i], 0, 0))
    count = {"joined": 2, "halves": 2 * steps, "whole": steps}[form]
    size = 128 if form == "halves" else HALF
    return pl.pallas_call(
        lambda *refs: products_kernel(form, steps, *refs),
        grid_spec=pltpu.PrefetchScalarGridSpec(
            num_scalar_prefetch=1,
            grid=(steps,),
            in_specs=[rows] * 4 + [block] * 2,
            out_specs=[pl.BlockSpec((size, 1024), lambda i, at: (0, 0))] * count,
        ),
        out_shape=[jax.ShapeDtypeStruct((size, 1024), jnp.bfloat16)] * count,
        compiler_params=GRANT,
    )(at, *attended, near, other)


def two_sums_kernel(a, b, c, d, first, second):
    for left, right, out in ((a, b, first), (c, d, second)):
        out[...] = (left[...].astype(jnp.float32) + right[...].astype(jnp.float32)).astype(
            jnp.bfloat16
        )


def two_sums(a, b, c, d):
    shape = jax.ShapeDtypeStruct(a.shape, jnp.bfloat16)
    return pl.pallas_call(two_sums_kernel, out_shape=[shape, shape])(a, b, c, d)


def final_kernel(core_ref, a, b, c, d, keep, give):
    core = core_ref[0]
    for which, out in ((core, keep), (1 - core, give)):
        cols = pl.ds(pl.multiple_of(which * 512, 512), 512)
        value = a[:, cols].astype(jnp.float32) + b[:, cols].astype(jnp.float32)
        value += c[:, cols].astype(jnp.float32) + d[:, cols].astype(jnp.float32)
        out[...] = value.astype(jnp.bfloat16)


def final_sums(core, *values):
    whole = pl.BlockSpec((HALF, 1024), lambda i, c: (0, 0))
    half = pl.BlockSpec((HALF, 512), lambda i, c: (0, 0))
    shape = jax.ShapeDtypeStruct((HALF, 512), jnp.bfloat16)
    return pl.pallas_call(
        final_kernel,
        grid_spec=pltpu.PrefetchScalarGridSpec(
            num_scalar_prefetch=1, grid=(1,), in_specs=[whole] * 4, out_specs=[half, half]
        ),
        out_shape=[shape, shape],
    )(core.reshape(1), *values)


def add_rows(value, arrived, start):
    rows = arrived.shape[0]
    return lax.dynamic_update_slice(value, value[start : start + rows] + arrived, (start, 0))


def half_of(value, which, dim=0):
    size = value.shape[dim] // 2
    return lax.dynamic_slice_in_dim(value, which * size, size, dim)


def ordered(first, own, other, dim=0):
    return jnp.where(
        first, jnp.concatenate([own, other], dim), jnp.concatenate([other, own], dim)
    )


def dot(a, b):
    return jnp.dot(a, b, preferred_element_type=jnp.float32)


def local(tokens, norm_gain, query_weight, kv_weight, out_weight, lengths):
    core = lax.axis_index("core")
    chip = lax.axis_index(("zl", "x"))
    zl = lax.axis_index("zl")
    x = lax.axis_index("x")
    y = lax.axis_index("y")
    zh = lax.axis_index("zh")
    is_first = core == 0

    near_other = core_swap(query_weight)

    gain = lax.dynamic_slice_in_dim(norm_gain, (chip * 2 + core) * 512, 512, 0)
    wide = tokens.astype(jnp.float32)
    gained = (wide * gain[None, :]).astype(jnp.bfloat16)
    mine = send(half_of(gained, core), to_slice(0))
    theirs = send(half_of(gained, 1 - core), to_slice(1))
    block = ordered(is_first, mine, theirs, 1)

    kv_near = lax.dynamic_slice_in_dim(kv_weight, chip * 256, 256, 1)
    kv_own = lax.dynamic_slice_in_dim(kv_weight, chip * 256 + core * 128, 128, 1)
    near = jnp.concatenate([query_weight, kv_own], axis=1)
    slice_gain = 1.0 / lax.dynamic_slice_in_dim(norm_gain, y * 2048, 2048, 0)
    own_slots = core * HALF + jnp.arange(HALF, dtype=jnp.int32)
    slot_k = jnp.concatenate([own_slots, (1 - core) * HALF + jnp.arange(HALF, dtype=jnp.int32)])
    allowed = (slot_k[None, :] <= own_slots[:, None]) & (slot_k[None, :] < lengths[0])
    bias = jnp.where(allowed, 0.0, -jnp.inf).astype(jnp.float32)
    cosine, sine = rope_tables(own_slots)
    block, near_other, kv_near, near = lax.optimization_barrier((block, near_other, kv_near, near))
    block, slice_gain, bias, cosine, sine = lax.optimization_barrier(
        (block, slice_gain, bias, cosine, sine)
    )

    beside = zl_swap(block)
    left = x_shift(block, 1)
    right = x_shift(block, -1)
    left, right, beside = lax.optimization_barrier((left, right, beside))
    far = zh_swap(after(near, beside))
    beside_left = x_shift(beside, 1)
    beside_right = x_shift(beside, -1)
    opposite = jnp.concatenate([x_shift(left[:128], 1), x_shift(right[128:], -1)], 0)
    beside_opposite = jnp.concatenate(
        [x_shift(beside_left[:128], 1), x_shift(beside_right[128:], -1)], 0
    )
    weights = (query_weight, near_other, kv_near, far, core_swap(after(far, beside_opposite)))
    gathered = jnp.zeros((4, HALF, 2048), jnp.bfloat16)
    for dz, dx, part in (
        (0, 0, block),
        (0, 3, left),
        (0, 1, right),
        (1, 0, beside),
        (0, 2, opposite),
        (1, 3, beside_left),
        (1, 1, beside_right),
        (1, 2, beside_opposite),
    ):
        zs, xs = zl ^ dz, (x + dx) % 4
        gathered = lax.dynamic_update_slice(
            gathered, part[None], (zs * 2 + xs // 2, 0, (xs % 2) * 1024)
        )

    out_near = lax.all_gather(after(out_weight, block), "y", axis=0, tiled=False)

    squares = jnp.sum(jnp.square(gathered.astype(jnp.float32) * slice_gain), axis=-1)
    gathered, squares = lax.optimization_barrier((gathered, squares))
    low, high = project([(y + 2) % 4], zh, core, gathered, weights, True)
    from_below = y_shift(low, 1)
    from_above = y_shift(high, -1)
    a_top, a_bottom, b_top, b_bottom = project(
        [(y + 1) % 4, (y + 3) % 4], zh, core, gathered, weights, True
    )
    from_below, from_above, a_top, b_bottom = lax.optimization_barrier(
        (from_below, from_above, a_top, b_bottom)
    )
    a_bottom, b_top = y_shift(a_bottom, 1), y_shift(b_top, -1)
    a_top, b_bottom = two_sums(a_top, from_below, b_bottom, from_above)
    gathered = after(gathered, (a_top, b_bottom, a_bottom, b_top))
    (kept,) = project([y], zh, core, gathered, weights)
    sums = (kept, y_shift(a_top, 1), a_bottom, b_top, y_shift(b_bottom, -1))

    squares, a_top, b_bottom = lax.optimization_barrier((squares, a_top, b_bottom))
    total = lax.dynamic_index_in_dim(squares, y, 0, keepdims=False)
    for k in (1, 2, 3):
        total += y_shift(lax.dynamic_index_in_dim(squares, (y + k) % 4, 0, keepdims=False), k)
    scale = lax.rsqrt(total / 8192.0 + norm_eps)[:, None]

    kv_rows = key_value_rows(core, sums, scale, cosine, sine)
    kv_other = core_swap(kv_rows)
    out_other = core_swap(after(out_near, kv_other))
    own_a = attention(0, sums, scale, cosine, sine, bias, kv_rows, kv_other)
    far_a = zh_swap(own_a)
    own_b = attention(1, sums, scale, cosine, sine, bias, kv_rows, kv_other)
    far_b = zh_swap(own_b)
    attended = (own_a, own_b, far_a, far_b)

    def made(moves, form="whole"):
        targets = [(zl ^ dz, (x + dx) % 4) for dz, dx in moves]
        return products(targets, zh, attended, out_near, out_other, form)

    low, high = made([(1, 2), (0, 2)], "joined")
    from_left, from_right = x_shift(low, 1), x_shift(high, -1)
    a_top, a_bottom, b_top, b_bottom = made([(1, 1), (1, 3)], "halves")
    here_a, here_b, beside, mixed = made([(0, 1), (0, 3), (1, 0), (0, 0)])
    from_left, from_right, here_a, here_b = lax.optimization_barrier(
        (from_left, from_right, here_a, here_b)
    )
    a_bottom, b_top = x_shift(a_bottom, 1), x_shift(b_top, -1)
    a_top = x_shift(a_top + from_left[:128], 1)
    b_bottom = x_shift(b_bottom + from_right[:128], -1)
    here_a = x_shift(add_rows(here_a, from_left[128:], 0), 1)
    here_b = x_shift(add_rows(here_b, from_right[128:], 128), -1)

    across = zl_swap(summed_up(beside, a_top, a_bottom, b_top, b_bottom))
    keep, give = final_sums(core, mixed, here_a, here_b, across)
    keep, got = send(keep, to_home(0)), send(give, to_home(1))
    return (wide + ordered(is_first, keep, got, 0).astype(jnp.float32)).astype(jnp.bfloat16)


def solution(mesh):
    split = Mesh(mesh.devices.reshape(SIZES), AXES)
    gx, gy = ("zl", "x", "core"), ("y", "zh")
    placed = (P(gy, gx), P(), P(gy, gx), P(gy, None), P(gx, gy), P(gy))
    return jax.shard_map(
        local, mesh=split, in_specs=placed, out_specs=P(gy, gx), check_vma=False
    )
```

```python
import jax
import jax.numpy as jnp
from jax import lax
from jax.experimental import pallas as pl
from jax.experimental.pallas import tpu as pltpu
from jax.sharding import Mesh, PartitionSpec as P

HEAD_SIZE = 128
SLOTS = 512
HALF = 256
AXES = ("zl", "x", "core", "y", "zh")
SIZES = (2, 4, 2, 4, 2)

rope_base = 500000.0
norm_eps = 1e-05


def coords(i):
    out = {}
    for name, size in zip(AXES[::-1], SIZES[::-1]):
        i, out[name] = divmod(i, size)
    return out


def index(c):
    i = 0
    for name, size in zip(AXES, SIZES):
        i = i * size + c[name] % size
    return i


def pairs(change):
    out = []
    for i in range(128):
        c = coords(i)
        out.append((i, index({**c, **change(c)})))
    return out


def send(value, change):
    return lax.ppermute(value, AXES, pairs(change))


def core_swap(value):
    return send(value, lambda c: dict(core=1 - c["core"]))


def zh_swap(value):
    return send(value, lambda c: dict(zh=1 - c["zh"]))


def zl_swap(value):
    return send(value, lambda c: dict(zl=1 - c["zl"]))


def x_shift(value, k):
    return send(value, lambda c: dict(x=c["x"] + k))


def after(value, other):
    return lax.optimization_barrier((value, other))[0]


def y_shift(value, k):
    return send(value, lambda c: dict(y=c["y"] + k))


def to_slice(flip):
    def change(c):
        return dict(
            y=2 * c["zl"] + c["x"] // 2,
            zl=c["y"] // 2,
            x=(c["y"] % 2) * 2 + c["x"] % 2,
            core=c["core"] ^ flip,
        )

    return change


def to_home(flip):
    def change(c):
        moves = c["x"] % 2 != c["zh"]
        return dict(x=c["x"] ^ moves, zh=c["zh"] ^ moves, core=c["core"] ^ flip)

    return change


def rope_tables(positions):
    half_dim = HEAD_SIZE // 2
    steps_up = jnp.arange(0, half_dim, dtype=jnp.float32) * (2.0 / HEAD_SIZE)
    inverse = jnp.power(jnp.float32(rope_base), -steps_up)
    angles = positions.astype(jnp.float32)[:, None] * inverse[None, :]
    cosine, sine = jnp.cos(angles), jnp.sin(angles)
    return jnp.concatenate([cosine, cosine], 1), jnp.concatenate([-sine, sine], 1)


def rotated(vectors, cosine, sine):
    return vectors * cosine + pltpu.roll(vectors, HEAD_SIZE // 2, 1) * sine


WIDE = 640
GRANT = pltpu.CompilerParams(vmem_limit_bytes=24 * 1024 * 1024)


def total_of(refs, cols=slice(None)):
    whole, *halves = (ref[:, cols].astype(jnp.float32) for ref in refs)
    a_top, a_bottom, b_top, b_bottom = halves
    return whole + jnp.concatenate([a_top + b_top, a_bottom + b_bottom], axis=0)


def total_kernel(*refs):
    refs[-1][...] = total_of(refs[:-1]).astype(jnp.bfloat16)


def summed_up(*values):
    return pl.pallas_call(
        total_kernel, out_shape=jax.ShapeDtypeStruct(values[0].shape, jnp.bfloat16)
    )(*values)


def key_value_kernel(core_ref, *refs):
    scale_ref, cos_ref, sin_ref, out_ref = refs[10:]
    scale = scale_ref[...]
    keys = rotated(total_of(refs[:5]) * scale, cos_ref[...], sin_ref[...])
    out_ref[:, :HEAD_SIZE] = keys.astype(jnp.bfloat16)
    out_ref[:, HEAD_SIZE:] = (total_of(refs[5:10]) * scale).astype(jnp.bfloat16)


def key_value_rows(core, sums, scale, cosine, sine):
    keys = [
        pl.BlockSpec((v.shape[0], HEAD_SIZE), lambda i, c: (0, 4 + 5 * c[0])) for v in sums
    ]
    values = [
        pl.BlockSpec((v.shape[0], HEAD_SIZE), lambda i, c: (0, 9 - 5 * c[0])) for v in sums
    ]
    table = pl.BlockSpec((HALF, HEAD_SIZE), lambda i, c: (0, 0))
    return pl.pallas_call(
        key_value_kernel,
        grid_spec=pltpu.PrefetchScalarGridSpec(
            num_scalar_prefetch=1,
            grid=(1,),
            in_specs=keys
            + values
            + [pl.BlockSpec((HALF, 1), lambda i, c: (0, 0)), table, table],
            out_specs=pl.BlockSpec((HALF, 2 * HEAD_SIZE), lambda i, c: (0, 0)),
        ),
        out_shape=jax.ShapeDtypeStruct((HALF, 2 * HEAD_SIZE), jnp.bfloat16),
    )(core.reshape(1), *sums, *sums, scale, cosine, sine)


def attention_kernel(*refs):
    scale_ref, cos_ref, sin_ref, bias_ref, own_ref, other_ref, out_ref = refs[5:]
    contract = (((1,), (1,)), ((), ()))
    for head in range(4):
        cols = slice(head * HEAD_SIZE, (head + 1) * HEAD_SIZE)
        rows = total_of(refs[:5], cols) * scale_ref[...]
        queries = rotated(rows, cos_ref[...], sin_ref[...]).astype(jnp.bfloat16)

        def scores_of(ref, first):
            scores = lax.dot_general(
                queries, ref[:, :HEAD_SIZE], contract, preferred_element_type=jnp.float32
            )
            return scores * (HEAD_SIZE**-0.5) + bias_ref[:, first : first + HALF]

        own, other = scores_of(own_ref, 0), scores_of(other_ref, HALF)
        top = jnp.maximum(
            jnp.max(own, axis=-1, keepdims=True), jnp.max(other, axis=-1, keepdims=True)
        )
        own, other = jnp.exp(own - top), jnp.exp(other - top)
        total = jnp.sum(own, axis=-1, keepdims=True) + jnp.sum(other, axis=-1, keepdims=True)
        mixed = dot(own.astype(jnp.bfloat16), own_ref[:, HEAD_SIZE:]) + dot(
            other.astype(jnp.bfloat16), other_ref[:, HEAD_SIZE:]
        )
        out_ref[:, cols] = (mixed / total).astype(jnp.bfloat16)


def attention(part, sums, scale, cosine, sine, bias, own, other):
    def fixed(shape):
        return pl.BlockSpec(shape, lambda i: (0, 0))

    return pl.pallas_call(
        attention_kernel,
        grid=(1,),
        in_specs=[pl.BlockSpec((v.shape[0], WIDE), lambda i: (0, part)) for v in sums]
        + [
            fixed((HALF, 1)),
            fixed((HALF, HEAD_SIZE)),
            fixed((HALF, HEAD_SIZE)),
            fixed((HALF, SLOTS)),
            fixed((HALF, 2 * HEAD_SIZE)),
            fixed((HALF, 2 * HEAD_SIZE)),
        ],
        out_specs=fixed((HALF, 512)),
        out_shape=jax.ShapeDtypeStruct((HALF, 512), jnp.bfloat16),
        compiler_params=GRANT,
    )(*sums, scale, cosine, sine, bias, own, other)


def project_kernel(at_ref, rows_ref, near, near_other, near_kv, far, far_other, *outs):
    zh, core = at_ref[0], at_ref[1]
    step = pl.program_id(0)
    near_rows = rows_ref[0, :, pl.ds(pl.multiple_of(zh * 1024, 1024), 1024)]
    far_rows = rows_ref[0, :, pl.ds(pl.multiple_of((1 - zh) * 1024, 1024), 1024)]

    def put(start, near_part, far_part):
        cols = slice(start, start + near_part.shape[1])
        value = (dot(near_rows, near_part) + dot(far_rows, far_part)).astype(jnp.bfloat16)
        for i in range(len(outs) // 2):

            @pl.when(step == i)
            def _():
                outs[2 * i][:, cols] = value[:128]
                outs[2 * i + 1][:, cols] = value[128:]

        if len(outs) % 2:

            @pl.when(step == len(outs) // 2)
            def _():
                outs[-1][:, cols] = value

    def kv_cols(which):
        return near_kv[:, pl.ds(pl.multiple_of(which * HEAD_SIZE, HEAD_SIZE), HEAD_SIZE)]

    put(0, near[...], far[:, :512])
    put(512, kv_cols(core), far[:, 512:])
    put(WIDE, near_other[...], far_other[:, :512])
    put(WIDE + 512, kv_cols(1 - core), far_other[:, 512:])


def project(which, zh, core, gathered, weights, whole_last=False):
    steps = len(which)
    rows = [128] * 2 * steps if not whole_last else [128] * 2 * (steps - 1) + [HALF]
    return pl.pallas_call(
        project_kernel,
        grid_spec=pltpu.PrefetchScalarGridSpec(
            num_scalar_prefetch=1,
            grid=(steps,),
            in_specs=[pl.BlockSpec((1, HALF, 2048), lambda i, at: (at[2 + i], 0, 0))]
            + [pl.BlockSpec(w.shape, lambda i, at: (0, 0)) for w in weights],
            out_specs=[pl.BlockSpec((r, 2 * WIDE), lambda i, at: (0, 0)) for r in rows],
        ),
        out_shape=[jax.ShapeDtypeStruct((r, 2 * WIDE), jnp.bfloat16) for r in rows],
        compiler_params=GRANT,
    )(jnp.stack([zh, core, *which]).astype(jnp.int32), gathered, *weights)


def two_sums_kernel(a, b, c, d, first, second):
    for left, right, out in ((a, b, first), (c, d, second)):
        out[...] = (left[...].astype(jnp.float32) + right[...].astype(jnp.float32)).astype(
            jnp.bfloat16
        )


def two_sums(a, b, c, d):
    shape = jax.ShapeDtypeStruct(a.shape, jnp.bfloat16)
    return pl.pallas_call(two_sums_kernel, out_shape=[shape, shape])(a, b, c, d)


def products_kernel(form, steps, at_ref, own_a, own_b, far_a, far_b, near, other, *outs):
    step = pl.program_id(0)

    def put(left, right):
        product = dot(left[...], near[0]) + dot(right[...], other[0])
        product = product.astype(jnp.bfloat16)
        for i in range(steps):

            @pl.when(step == i)
            def _():
                if form == "joined":
                    outs[0][i * 128 : i * 128 + 128] = product[:128]
                    outs[1][i * 128 : i * 128 + 128] = product[128:]
                elif form == "halves":
                    outs[2 * i][...] = product[:128]
                    outs[2 * i + 1][...] = product[128:]
                else:
                    outs[i][...] = product

    @pl.when(at_ref[steps + step] == 1)
    def _():
        put(own_a, own_b)

    @pl.when(at_ref[steps + step] == 0)
    def _():
        put(far_a, far_b)


def products(targets, zh, attended, near, other, form="whole"):
    steps = len(targets)
    blocks = [zt * 2 + xt // 2 for zt, xt in targets]
    owns = [xt % 2 == zh for _, xt in targets]
    at = jnp.stack([v.astype(jnp.int32) for v in blocks + owns])
    rows = pl.BlockSpec((HALF, 512), lambda i, at: (0, 0))
    block = pl.BlockSpec((1, 512, 1024), lambda i, at: (at[i], 0, 0))
    count = {"joined": 2, "halves": 2 * steps, "whole": steps}[form]
    size = 128 if form == "halves" else HALF
    return pl.pallas_call(
        lambda *refs: products_kernel(form, steps, *refs),
        grid_spec=pltpu.PrefetchScalarGridSpec(
            num_scalar_prefetch=1,
            grid=(steps,),
            in_specs=[rows] * 4 + [block] * 2,
            out_specs=[pl.BlockSpec((size, 1024), lambda i, at: (0, 0))] * count,
        ),
        out_shape=[jax.ShapeDtypeStruct((size, 1024), jnp.bfloat16)] * count,
        compiler_params=GRANT,
    )(at, *attended, near, other)


def add_rows(value, arrived, start):
    rows = arrived.shape[0]
    return lax.dynamic_update_slice(value, value[start : start + rows] + arrived, (start, 0))


def half_of(value, which, dim=0):
    size = value.shape[dim] // 2
    return lax.dynamic_slice_in_dim(value, which * size, size, dim)


def ordered(first, own, other, dim=0):
    return jnp.where(
        first, jnp.concatenate([own, other], dim), jnp.concatenate([other, own], dim)
    )


def dot(a, b):
    return jnp.dot(a, b, preferred_element_type=jnp.float32)


def local(tokens, norm_gain, query_weight, kv_weight, out_weight, lengths):
    core = lax.axis_index("core")
    chip = lax.axis_index(("zl", "x"))
    zl = lax.axis_index("zl")
    x = lax.axis_index("x")
    y = lax.axis_index("y")
    zh = lax.axis_index("zh")
    is_first = core == 0

    near_other = core_swap(query_weight)

    gain = lax.dynamic_slice_in_dim(norm_gain, (chip * 2 + core) * 512, 512, 0)
    wide = tokens.astype(jnp.float32)
    gained = (wide * gain[None, :]).astype(jnp.bfloat16)
    mine = send(half_of(gained, core), to_slice(0))
    theirs = send(half_of(gained, 1 - core), to_slice(1))
    block = ordered(is_first, mine, theirs, 1)

    kv_near = lax.dynamic_slice_in_dim(kv_weight, chip * 256, 256, 1)
    kv_own = lax.dynamic_slice_in_dim(kv_weight, chip * 256 + core * 128, 128, 1)
    near = jnp.concatenate([query_weight, kv_own], axis=1)
    slice_gain = 1.0 / lax.dynamic_slice_in_dim(norm_gain, y * 2048, 2048, 0)
    own_slots = core * HALF + jnp.arange(HALF, dtype=jnp.int32)
    slot_k = jnp.concatenate([own_slots, (1 - core) * HALF + jnp.arange(HALF, dtype=jnp.int32)])
    allowed = (slot_k[None, :] <= own_slots[:, None]) & (slot_k[None, :] < lengths[0])
    bias = jnp.where(allowed, 0.0, -jnp.inf).astype(jnp.float32)
    cosine, sine = rope_tables(own_slots)
    block, near_other, kv_near, near = lax.optimization_barrier((block, near_other, kv_near, near))
    block, slice_gain, bias, cosine, sine = lax.optimization_barrier(
        (block, slice_gain, bias, cosine, sine)
    )

    beside = zl_swap(block)
    left = x_shift(block, 1)
    right = x_shift(block, -1)
    left, right, beside = lax.optimization_barrier((left, right, beside))
    far = zh_swap(after(near, beside))
    beside_left = x_shift(beside, 1)
    beside_right = x_shift(beside, -1)
    opposite = jnp.concatenate([x_shift(left[:128], 1), x_shift(right[128:], -1)], 0)
    beside_opposite = jnp.concatenate(
        [x_shift(beside_left[:128], 1), x_shift(beside_right[128:], -1)], 0
    )
    weights = (query_weight, near_other, kv_near, far, core_swap(after(far, beside_opposite)))
    gathered = jnp.zeros((4, HALF, 2048), jnp.bfloat16)
    for dz, dx, part in (
        (0, 0, block),
        (0, 3, left),
        (0, 1, right),
        (1, 0, beside),
        (0, 2, opposite),
        (1, 3, beside_left),
        (1, 1, beside_right),
        (1, 2, beside_opposite),
    ):
        zs, xs = zl ^ dz, (x + dx) % 4
        gathered = lax.dynamic_update_slice(
            gathered, part[None], (zs * 2 + xs // 2, 0, (xs % 2) * 1024)
        )

    out_near = lax.all_gather(after(out_weight, block), "y", axis=0, tiled=False)

    squares = jnp.sum(jnp.square(gathered.astype(jnp.float32) * slice_gain), axis=-1)
    low, high, kept = project([(y + 2) % 4, y], zh, core, gathered, weights, True)
    from_below = y_shift(low, 1)
    from_above = y_shift(high, -1)
    a_top, a_bottom, b_top, b_bottom = project(
        [(y + 1) % 4, (y + 3) % 4], zh, core, gathered, weights
    )

    squares, a_bottom, b_top = lax.optimization_barrier((squares, a_bottom, b_top))

    def squares_of(which):
        return lax.dynamic_index_in_dim(squares, which, 0, keepdims=False)

    squares_in = send(
        jnp.stack([squares_of(y ^ 1), squares_of(y ^ 3)]), lambda c: dict(y=c["y"] ^ 1)
    )
    from_below, from_above, a_top, b_bottom = lax.optimization_barrier(
        (from_below, from_above, a_top, b_bottom)
    )
    a_bottom, b_top = y_shift(a_bottom, 1), y_shift(b_top, -1)
    a_top, b_bottom = two_sums(a_top, from_below, b_bottom, from_above)
    squares_here, squares_beyond = squares_of(y) + squares_in[0], squares_of(y ^ 2) + squares_in[1]
    squares_here, squares_beyond, a_top, b_bottom = lax.optimization_barrier(
        (squares_here, squares_beyond, a_top, b_bottom)
    )
    sums = (kept, y_shift(a_top, 1), a_bottom, b_top, y_shift(b_bottom, -1))

    total = squares_here + y_shift(squares_beyond, 2)
    scale = lax.rsqrt(total / 8192.0 + norm_eps)[:, None]

    kv_rows = key_value_rows(core, sums, scale, cosine, sine)
    kv_other = core_swap(kv_rows)
    out_other = core_swap(after(out_near, kv_other))
    own_a = attention(0, sums, scale, cosine, sine, bias, kv_rows, kv_other)
    far_a = zh_swap(own_a)
    own_b = attention(1, sums, scale, cosine, sine, bias, kv_rows, kv_other)
    far_b = zh_swap(own_b)
    attended = (own_a, own_b, far_a, far_b)

    def made(moves, form="whole"):
        targets = [(zl ^ dz, (x + dx) % 4) for dz, dx in moves]
        return products(targets, zh, attended, out_near, out_other, form)

    low, high = made([(1, 2), (0, 2)], "joined")
    from_left, from_right = x_shift(low, 1), x_shift(high, -1)
    a_top, a_bottom, b_top, b_bottom = made([(1, 1), (1, 3)], "halves")
    here_a, here_b, beside, mixed = made([(0, 1), (0, 3), (1, 0), (0, 0)])
    from_left, from_right, here_a, here_b = lax.optimization_barrier(
        (from_left, from_right, here_a, here_b)
    )
    a_bottom, b_top = x_shift(a_bottom, 1), x_shift(b_top, -1)
    a_top = x_shift(a_top + from_left[:128], 1)
    b_bottom = x_shift(b_bottom + from_right[:128], -1)
    here_a = x_shift(add_rows(here_a, from_left[128:], 0), 1)
    here_b = x_shift(add_rows(here_b, from_right[128:], 128), -1)

    def sum_of(*values):
        return sum(v.astype(jnp.float32) for v in values).astype(jnp.bfloat16)

    across = zl_swap(summed_up(beside, a_top, a_bottom, b_top, b_bottom))
    mixed = sum_of(mixed, here_a, here_b, across)
    keep = send(half_of(mixed, core, 1), to_home(0))
    got = send(half_of(mixed, 1 - core, 1), to_home(1))
    return (wide + ordered(is_first, keep, got, 0).astype(jnp.float32)).astype(jnp.bfloat16)


def solution(mesh):
    split = Mesh(mesh.devices.reshape(SIZES), AXES)
    gx, gy = ("zl", "x", "core"), ("y", "zh")
    placed = (P(gy, gx), P(), P(gy, gx), P(gy, None), P(gx, gy), P(gy))
    return jax.shard_map(
        local, mesh=split, in_specs=placed, out_specs=P(gy, gx), check_vma=False
    )
```

```python
import jax
import jax.numpy as jnp
from jax import lax
from jax.experimental import pallas as pl
from jax.experimental.pallas import tpu as pltpu
from jax.sharding import Mesh, PartitionSpec as P

HEAD_SIZE = 128
SLOTS = 512
HALF = 256
AXES = ("zl", "x", "core", "y", "zh")
SIZES = (2, 4, 2, 4, 2)

rope_base = 500000.0
norm_eps = 1e-05


def coords(i):
    out = {}
    for name, size in zip(AXES[::-1], SIZES[::-1]):
        i, out[name] = divmod(i, size)
    return out


def index(c):
    i = 0
    for name, size in zip(AXES, SIZES):
        i = i * size + c[name] % size
    return i


def pairs(change):
    out = []
    for i in range(128):
        c = coords(i)
        out.append((i, index({**c, **change(c)})))
    return out


def send(value, change):
    return lax.ppermute(value, AXES, pairs(change))


def core_swap(value):
    return send(value, lambda c: dict(core=1 - c["core"]))


def zh_swap(value):
    return send(value, lambda c: dict(zh=1 - c["zh"]))


def zl_swap(value):
    return send(value, lambda c: dict(zl=1 - c["zl"]))


def x_shift(value, k):
    return send(value, lambda c: dict(x=c["x"] + k))


def after(value, other):
    return lax.optimization_barrier((value, other))[0]


def y_shift(value, k):
    return send(value, lambda c: dict(y=c["y"] + k))


def to_slice(flip):
    def change(c):
        return dict(
            y=2 * c["zl"] + c["x"] // 2,
            zl=c["y"] // 2,
            x=(c["y"] % 2) * 2 + c["x"] % 2,
            core=c["core"] ^ flip,
        )

    return change


def to_home(flip):
    def change(c):
        moves = c["x"] % 2 != c["zh"]
        return dict(x=c["x"] ^ moves, zh=c["zh"] ^ moves, core=c["core"] ^ flip)

    return change


def rope_tables(positions):
    half_dim = HEAD_SIZE // 2
    steps_up = jnp.arange(0, half_dim, dtype=jnp.float32) * (2.0 / HEAD_SIZE)
    inverse = jnp.power(jnp.float32(rope_base), -steps_up)
    angles = positions.astype(jnp.float32)[:, None] * inverse[None, :]
    cosine, sine = jnp.cos(angles), jnp.sin(angles)
    return jnp.concatenate([cosine, cosine], 1), jnp.concatenate([-sine, sine], 1)


def rotated(vectors, cosine, sine):
    return vectors * cosine + pltpu.roll(vectors, HEAD_SIZE // 2, 1) * sine


WIDE = 640
GRANT = pltpu.CompilerParams(vmem_limit_bytes=24 * 1024 * 1024)


def total_of(refs, cols=slice(None)):
    whole, *halves = (ref[:, cols].astype(jnp.float32) for ref in refs)
    a_top, a_bottom, b_top, b_bottom = halves
    return whole + jnp.concatenate([a_top + b_top, a_bottom + b_bottom], axis=0)


def total_kernel(*refs):
    refs[-1][...] = total_of(refs[:-1]).astype(jnp.bfloat16)


def summed_up(*values):
    return pl.pallas_call(
        total_kernel, out_shape=jax.ShapeDtypeStruct(values[0].shape, jnp.bfloat16)
    )(*values)


def key_value_kernel(core_ref, *refs):
    scale_ref, cos_ref, sin_ref, out_ref = refs[10:]
    scale = scale_ref[...]
    keys = rotated(total_of(refs[:5]) * scale, cos_ref[...], sin_ref[...])
    out_ref[:, :HEAD_SIZE] = keys.astype(jnp.bfloat16)
    out_ref[:, HEAD_SIZE:] = (total_of(refs[5:10]) * scale).astype(jnp.bfloat16)


def key_value_rows(core, sums, scale, cosine, sine):
    keys = [
        pl.BlockSpec((v.shape[0], HEAD_SIZE), lambda i, c: (0, 4 + 5 * c[0])) for v in sums
    ]
    values = [
        pl.BlockSpec((v.shape[0], HEAD_SIZE), lambda i, c: (0, 9 - 5 * c[0])) for v in sums
    ]
    table = pl.BlockSpec((HALF, HEAD_SIZE), lambda i, c: (0, 0))
    return pl.pallas_call(
        key_value_kernel,
        grid_spec=pltpu.PrefetchScalarGridSpec(
            num_scalar_prefetch=1,
            grid=(1,),
            in_specs=keys
            + values
            + [pl.BlockSpec((HALF, 1), lambda i, c: (0, 0)), table, table],
            out_specs=pl.BlockSpec((HALF, 2 * HEAD_SIZE), lambda i, c: (0, 0)),
        ),
        out_shape=jax.ShapeDtypeStruct((HALF, 2 * HEAD_SIZE), jnp.bfloat16),
    )(core.reshape(1), *sums, *sums, scale, cosine, sine)


def attention_kernel(*refs):
    scale_ref, cos_ref, sin_ref, bias_ref, own_ref, other_ref, out_ref = refs[5:]
    contract = (((1,), (1,)), ((), ()))
    for head in range(4):
        cols = slice(head * HEAD_SIZE, (head + 1) * HEAD_SIZE)
        rows = total_of(refs[:5], cols) * scale_ref[...]
        queries = rotated(rows, cos_ref[...], sin_ref[...]).astype(jnp.bfloat16)

        def scores_of(ref, first):
            scores = lax.dot_general(
                queries, ref[:, :HEAD_SIZE], contract, preferred_element_type=jnp.float32
            )
            return scores * (HEAD_SIZE**-0.5) + bias_ref[:, first : first + HALF]

        own, other = scores_of(own_ref, 0), scores_of(other_ref, HALF)
        top = jnp.maximum(
            jnp.max(own, axis=-1, keepdims=True), jnp.max(other, axis=-1, keepdims=True)
        )
        own, other = jnp.exp(own - top), jnp.exp(other - top)
        total = jnp.sum(own, axis=-1, keepdims=True) + jnp.sum(other, axis=-1, keepdims=True)
        mixed = dot(own.astype(jnp.bfloat16), own_ref[:, HEAD_SIZE:]) + dot(
            other.astype(jnp.bfloat16), other_ref[:, HEAD_SIZE:]
        )
        out_ref[:, cols] = (mixed / total).astype(jnp.bfloat16)


def attention(part, sums, scale, cosine, sine, bias, own, other):
    def fixed(shape):
        return pl.BlockSpec(shape, lambda i: (0, 0))

    return pl.pallas_call(
        attention_kernel,
        grid=(1,),
        in_specs=[pl.BlockSpec((v.shape[0], WIDE), lambda i: (0, part)) for v in sums]
        + [
            fixed((HALF, 1)),
            fixed((HALF, HEAD_SIZE)),
            fixed((HALF, HEAD_SIZE)),
            fixed((HALF, SLOTS)),
            fixed((HALF, 2 * HEAD_SIZE)),
            fixed((HALF, 2 * HEAD_SIZE)),
        ],
        out_specs=fixed((HALF, 512)),
        out_shape=jax.ShapeDtypeStruct((HALF, 512), jnp.bfloat16),
        compiler_params=GRANT,
    )(*sums, scale, cosine, sine, bias, own, other)


def project_kernel(at_ref, rows_ref, near, near_other, near_kv, far, far_other, *outs):
    zh, core = at_ref[0], at_ref[1]
    step = pl.program_id(0)
    near_rows = rows_ref[0, :, pl.ds(pl.multiple_of(zh * 1024, 1024), 1024)]
    far_rows = rows_ref[0, :, pl.ds(pl.multiple_of((1 - zh) * 1024, 1024), 1024)]

    def put(start, near_part, far_part):
        cols = slice(start, start + near_part.shape[1])
        value = (dot(near_rows, near_part) + dot(far_rows, far_part)).astype(jnp.bfloat16)
        if len(outs) == 1:
            outs[0][:, cols] = value
            return
        for i in range(len(outs) // 2):

            @pl.when(step == i)
            def _():
                outs[2 * i][:, cols] = value[:128]
                outs[2 * i + 1][:, cols] = value[128:]

    def kv_cols(which):
        return near_kv[:, pl.ds(pl.multiple_of(which * HEAD_SIZE, HEAD_SIZE), HEAD_SIZE)]

    put(0, near[...], far[:, :512])
    put(512, kv_cols(core), far[:, 512:])
    put(WIDE, near_other[...], far_other[:, :512])
    put(WIDE + 512, kv_cols(1 - core), far_other[:, 512:])


def project(which, zh, core, gathered, weights, halves=False):
    steps = len(which)
    rows, outs = (128, 2 * steps) if halves else (HALF, 1)
    return pl.pallas_call(
        project_kernel,
        grid_spec=pltpu.PrefetchScalarGridSpec(
            num_scalar_prefetch=1,
            grid=(steps,),
            in_specs=[pl.BlockSpec((1, HALF, 2048), lambda i, at: (at[2 + i], 0, 0))]
            + [pl.BlockSpec(w.shape, lambda i, at: (0, 0)) for w in weights],
            out_specs=[pl.BlockSpec((rows, 2 * WIDE), lambda i, at: (0, 0))] * outs,
        ),
        out_shape=[jax.ShapeDtypeStruct((rows, 2 * WIDE), jnp.bfloat16)] * outs,
        compiler_params=GRANT,
    )(jnp.stack([zh, core, *which]).astype(jnp.int32), gathered, *weights)


def products_kernel(form, steps, at_ref, own_a, own_b, far_a, far_b, near, other, *outs):
    step = pl.program_id(0)

    def put(left, right):
        product = dot(left[...], near[0]) + dot(right[...], other[0])
        product = product.astype(jnp.bfloat16)
        for i in range(steps):

            @pl.when(step == i)
            def _():
                if form == "joined":
                    outs[0][i * 128 : i * 128 + 128] = product[:128]
                    outs[1][i * 128 : i * 128 + 128] = product[128:]
                elif form == "halves":
                    outs[2 * i][...] = product[:128]
                    outs[2 * i + 1][...] = product[128:]
                else:
                    outs[i][...] = product

    @pl.when(at_ref[steps + step] == 1)
    def _():
        put(own_a, own_b)

    @pl.when(at_ref[steps + step] == 0)
    def _():
        put(far_a, far_b)


def products(targets, zh, attended, near, other, form="whole"):
    steps = len(targets)
    blocks = [zt * 2 + xt // 2 for zt, xt in targets]
    owns = [xt % 2 == zh for _, xt in targets]
    at = jnp.stack([v.astype(jnp.int32) for v in blocks + owns])
    rows = pl.BlockSpec((HALF, 512), lambda i, at: (0, 0))
    block = pl.BlockSpec((1, 512, 1024), lambda i, at: (at[i], 0, 0))
    count = {"joined": 2, "halves": 2 * steps, "whole": steps}[form]
    size = 128 if form == "halves" else HALF
    return pl.pallas_call(
        lambda *refs: products_kernel(form, steps, *refs),
        grid_spec=pltpu.PrefetchScalarGridSpec(
            num_scalar_prefetch=1,
            grid=(steps,),
            in_specs=[rows] * 4 + [block] * 2,
            out_specs=[pl.BlockSpec((size, 1024), lambda i, at: (0, 0))] * count,
        ),
        out_shape=[jax.ShapeDtypeStruct((size, 1024), jnp.bfloat16)] * count,
        compiler_params=GRANT,
    )(at, *attended, near, other)


def add_rows(value, arrived, start):
    rows = arrived.shape[0]
    return lax.dynamic_update_slice(value, value[start : start + rows] + arrived, (start, 0))


def half_of(value, which, dim=0):
    size = value.shape[dim] // 2
    return lax.dynamic_slice_in_dim(value, which * size, size, dim)


def ordered(first, own, other, dim=0):
    return jnp.where(
        first, jnp.concatenate([own, other], dim), jnp.concatenate([other, own], dim)
    )


def dot(a, b):
    return jnp.dot(a, b, preferred_element_type=jnp.float32)


def local(tokens, norm_gain, query_weight, kv_weight, out_weight, lengths):
    core = lax.axis_index("core")
    chip = lax.axis_index(("zl", "x"))
    zl = lax.axis_index("zl")
    x = lax.axis_index("x")
    y = lax.axis_index("y")
    zh = lax.axis_index("zh")
    is_first = core == 0

    near_other = core_swap(query_weight)

    gain = lax.dynamic_slice_in_dim(norm_gain, (chip * 2 + core) * 512, 512, 0)
    wide = tokens.astype(jnp.float32)
    gained = (wide * gain[None, :]).astype(jnp.bfloat16)
    mine = send(half_of(gained, core), to_slice(0))
    theirs = send(half_of(gained, 1 - core), to_slice(1))
    block = ordered(is_first, mine, theirs, 1)

    kv_near = lax.dynamic_slice_in_dim(kv_weight, chip * 256, 256, 1)
    kv_own = lax.dynamic_slice_in_dim(kv_weight, chip * 256 + core * 128, 128, 1)
    near = jnp.concatenate([query_weight, kv_own], axis=1)
    slice_gain = 1.0 / lax.dynamic_slice_in_dim(norm_gain, y * 2048, 2048, 0)
    own_slots = core * HALF + jnp.arange(HALF, dtype=jnp.int32)
    slot_k = jnp.concatenate([own_slots, (1 - core) * HALF + jnp.arange(HALF, dtype=jnp.int32)])
    allowed = (slot_k[None, :] <= own_slots[:, None]) & (slot_k[None, :] < lengths[0])
    bias = jnp.where(allowed, 0.0, -jnp.inf).astype(jnp.float32)
    cosine, sine = rope_tables(own_slots)
    block, near_other, kv_near, near = lax.optimization_barrier((block, near_other, kv_near, near))
    block, slice_gain, bias, cosine, sine = lax.optimization_barrier(
        (block, slice_gain, bias, cosine, sine)
    )

    beside = zl_swap(block)
    left = x_shift(block, 1)
    right = x_shift(block, -1)
    left, right, beside = lax.optimization_barrier((left, right, beside))
    far = zh_swap(after(near, beside))
    beside_left = x_shift(beside, 1)
    beside_right = x_shift(beside, -1)
    opposite = jnp.concatenate([x_shift(left[:128], 1), x_shift(right[128:], -1)], 0)
    beside_opposite = jnp.concatenate(
        [x_shift(beside_left[:128], 1), x_shift(beside_right[128:], -1)], 0
    )
    weights = (query_weight, near_other, kv_near, far, core_swap(after(far, beside_opposite)))
    gathered = jnp.zeros((4, HALF, 2048), jnp.bfloat16)
    for dz, dx, part in (
        (0, 0, block),
        (0, 3, left),
        (0, 1, right),
        (1, 0, beside),
        (0, 2, opposite),
        (1, 3, beside_left),
        (1, 1, beside_right),
        (1, 2, beside_opposite),
    ):
        zs, xs = zl ^ dz, (x + dx) % 4
        gathered = lax.dynamic_update_slice(
            gathered, part[None], (zs * 2 + xs // 2, 0, (xs % 2) * 1024)
        )

    out_near = lax.all_gather(after(out_weight, block), "y", axis=0, tiled=False)

    squares = jnp.sum(jnp.square(gathered.astype(jnp.float32) * slice_gain), axis=-1)
    low, high = project([(y + 2) % 4], zh, core, gathered, weights, True)
    from_below = y_shift(low, 1)
    from_above = y_shift(high, -1)
    a_top, a_bottom, b_top, b_bottom = project(
        [(y + 1) % 4, (y + 3) % 4], zh, core, gathered, weights, True
    )
    from_below, from_above, a_top, b_bottom = lax.optimization_barrier(
        (from_below, from_above, a_top, b_bottom)
    )
    a_bottom, b_top = y_shift(a_bottom, 1), y_shift(b_top, -1)
    a_top, b_bottom = a_top + from_below, b_bottom + from_above
    gathered = after(gathered, (a_top, b_bottom, a_bottom, b_top))
    (kept,) = project([y], zh, core, gathered, weights)
    sums = (kept, y_shift(a_top, 1), a_bottom, b_top, y_shift(b_bottom, -1))

    squares, a_top, b_bottom = lax.optimization_barrier((squares, a_top, b_bottom))
    total = lax.dynamic_index_in_dim(squares, y, 0, keepdims=False)
    for k in (1, 2, 3):
        total += y_shift(lax.dynamic_index_in_dim(squares, (y + k) % 4, 0, keepdims=False), k)
    scale = lax.rsqrt(total / 8192.0 + norm_eps)[:, None]

    kv_rows = key_value_rows(core, sums, scale, cosine, sine)
    kv_other = core_swap(kv_rows)
    out_other = core_swap(after(out_near, kv_other))
    own_a = attention(0, sums, scale, cosine, sine, bias, kv_rows, kv_other)
    far_a = zh_swap(own_a)
    own_b = attention(1, sums, scale, cosine, sine, bias, kv_rows, kv_other)
    far_b = zh_swap(own_b)
    attended = (own_a, own_b, far_a, far_b)

    def made(moves, form="whole"):
        targets = [(zl ^ dz, (x + dx) % 4) for dz, dx in moves]
        return products(targets, zh, attended, out_near, out_other, form)

    low, high = made([(1, 2), (0, 2)], "joined")
    from_left, from_right = x_shift(low, 1), x_shift(high, -1)
    a_top, a_bottom, b_top, b_bottom = made([(1, 1), (1, 3)], "halves")
    here_a, here_b, beside, mixed = made([(0, 1), (0, 3), (1, 0), (0, 0)])
    from_left, from_right, here_a, here_b = lax.optimization_barrier(
        (from_left, from_right, here_a, here_b)
    )
    a_bottom, b_top = x_shift(a_bottom, 1), x_shift(b_top, -1)
    a_top = x_shift(a_top + from_left[:128], 1)
    b_bottom = x_shift(b_bottom + from_right[:128], -1)
    here_a = x_shift(add_rows(here_a, from_left[128:], 0), 1)
    here_b = x_shift(add_rows(here_b, from_right[128:], 128), -1)

    def sum_of(*values):
        return sum(v.astype(jnp.float32) for v in values).astype(jnp.bfloat16)

    across = zl_swap(summed_up(beside, a_top, a_bottom, b_top, b_bottom))
    mixed = sum_of(mixed, here_a, here_b, across)
    keep = send(half_of(mixed, core, 1), to_home(0))
    got = send(half_of(mixed, 1 - core, 1), to_home(1))
    return (wide + ordered(is_first, keep, got, 0).astype(jnp.float32)).astype(jnp.bfloat16)


def solution(mesh):
    split = Mesh(mesh.devices.reshape(SIZES), AXES)
    gx, gy = ("zl", "x", "core"), ("y", "zh")
    placed = (P(gy, gx), P(), P(gy, gx), P(gy, None), P(gx, gy), P(gy))
    return jax.shard_map(
        local, mesh=split, in_specs=placed, out_specs=P(gy, gx), check_vma=False
    )
```

```python
import jax
import jax.numpy as jnp
from jax import lax
from jax.experimental import pallas as pl
from jax.experimental.pallas import tpu as pltpu
from jax.sharding import Mesh, PartitionSpec as P

HEAD_SIZE = 128
SLOTS = 512
HALF = 256
AXES = ("zl", "x", "core", "y", "zh")
SIZES = (2, 4, 2, 4, 2)

rope_base = 500000.0
norm_eps = 1e-05


def coords(i):
    out = {}
    for name, size in zip(AXES[::-1], SIZES[::-1]):
        i, out[name] = divmod(i, size)
    return out


def index(c):
    i = 0
    for name, size in zip(AXES, SIZES):
        i = i * size + c[name] % size
    return i


def pairs(change):
    out = []
    for i in range(128):
        c = coords(i)
        out.append((i, index({**c, **change(c)})))
    return out


def send(value, change):
    return lax.ppermute(value, AXES, pairs(change))


def core_swap(value):
    return send(value, lambda c: dict(core=1 - c["core"]))


def zh_swap(value):
    return send(value, lambda c: dict(zh=1 - c["zh"]))


def zl_swap(value):
    return send(value, lambda c: dict(zl=1 - c["zl"]))


def x_shift(value, k):
    return send(value, lambda c: dict(x=c["x"] + k))


def after(value, other):
    return lax.optimization_barrier((value, other))[0]


def y_shift(value, k):
    return send(value, lambda c: dict(y=c["y"] + k))


def to_slice(flip):
    def change(c):
        return dict(
            y=2 * c["zl"] + c["x"] // 2,
            zl=c["y"] // 2,
            x=(c["y"] % 2) * 2 + c["x"] % 2,
            core=c["core"] ^ flip,
        )

    return change


def to_home(flip):
    def change(c):
        moves = c["x"] % 2 != c["zh"]
        return dict(x=c["x"] ^ moves, zh=c["zh"] ^ moves, core=c["core"] ^ flip)

    return change


def rope_tables(positions):
    half_dim = HEAD_SIZE // 2
    steps_up = jnp.arange(0, half_dim, dtype=jnp.float32) * (2.0 / HEAD_SIZE)
    inverse = jnp.power(jnp.float32(rope_base), -steps_up)
    angles = positions.astype(jnp.float32)[:, None] * inverse[None, :]
    cosine, sine = jnp.cos(angles), jnp.sin(angles)
    return jnp.concatenate([cosine, cosine], 1), jnp.concatenate([-sine, sine], 1)


def rotated(vectors, cosine, sine):
    return vectors * cosine + pltpu.roll(vectors, HEAD_SIZE // 2, 1) * sine


WIDE = 640
GRANT = pltpu.CompilerParams(vmem_limit_bytes=24 * 1024 * 1024)
WIDE_GRANT = pltpu.CompilerParams(vmem_limit_bytes=52 * 1024 * 1024)


def total_of(refs, cols=slice(None)):
    whole, *halves = (ref[:, cols].astype(jnp.float32) for ref in refs)
    a_top, a_bottom, b_top, b_bottom = halves
    return whole + jnp.concatenate([a_top + b_top, a_bottom + b_bottom], axis=0)


def total_kernel(*refs):
    refs[-1][...] = total_of(refs[:-1]).astype(jnp.bfloat16)


def summed_up(*values):
    return pl.pallas_call(
        total_kernel, out_shape=jax.ShapeDtypeStruct(values[0].shape, jnp.bfloat16)
    )(*values)


def key_value_kernel(core_ref, *refs):
    scale_ref, cos_ref, sin_ref, out_ref = refs[10:]
    scale = scale_ref[...]
    keys = rotated(total_of(refs[:5]) * scale, cos_ref[...], sin_ref[...])
    out_ref[:, :HEAD_SIZE] = keys.astype(jnp.bfloat16)
    out_ref[:, HEAD_SIZE:] = (total_of(refs[5:10]) * scale).astype(jnp.bfloat16)


def key_value_rows(core, sums, scale, cosine, sine):
    keys = [
        pl.BlockSpec((v.shape[0], HEAD_SIZE), lambda i, c: (0, 4 + 5 * c[0])) for v in sums
    ]
    values = [
        pl.BlockSpec((v.shape[0], HEAD_SIZE), lambda i, c: (0, 9 - 5 * c[0])) for v in sums
    ]
    table = pl.BlockSpec((HALF, HEAD_SIZE), lambda i, c: (0, 0))
    return pl.pallas_call(
        key_value_kernel,
        grid_spec=pltpu.PrefetchScalarGridSpec(
            num_scalar_prefetch=1,
            grid=(1,),
            in_specs=keys
            + values
            + [pl.BlockSpec((HALF, 1), lambda i, c: (0, 0)), table, table],
            out_specs=pl.BlockSpec((HALF, 2 * HEAD_SIZE), lambda i, c: (0, 0)),
        ),
        out_shape=jax.ShapeDtypeStruct((HALF, 2 * HEAD_SIZE), jnp.bfloat16),
    )(core.reshape(1), *sums, *sums, scale, cosine, sine)


def attention_kernel(*refs):
    scale_ref, cos_ref, sin_ref, bias_ref, own_ref, other_ref, out_ref = refs[5:]
    contract = (((1,), (1,)), ((), ()))
    for head in range(4):
        cols = slice(head * HEAD_SIZE, (head + 1) * HEAD_SIZE)
        rows = total_of(refs[:5], cols) * scale_ref[...]
        queries = rotated(rows, cos_ref[...], sin_ref[...]).astype(jnp.bfloat16)

        def scores_of(ref, first):
            scores = lax.dot_general(
                queries, ref[:, :HEAD_SIZE], contract, preferred_element_type=jnp.float32
            )
            return scores * (HEAD_SIZE**-0.5) + bias_ref[:, first : first + HALF]

        own, other = scores_of(own_ref, 0), scores_of(other_ref, HALF)
        top = jnp.maximum(
            jnp.max(own, axis=-1, keepdims=True), jnp.max(other, axis=-1, keepdims=True)
        )
        own, other = jnp.exp(own - top), jnp.exp(other - top)
        total = jnp.sum(own, axis=-1, keepdims=True) + jnp.sum(other, axis=-1, keepdims=True)
        mixed = dot(own.astype(jnp.bfloat16), own_ref[:, HEAD_SIZE:]) + dot(
            other.astype(jnp.bfloat16), other_ref[:, HEAD_SIZE:]
        )
        out_ref[:, cols] = (mixed / total).astype(jnp.bfloat16)


def attention(part, sums, scale, cosine, sine, bias, own, other):
    def fixed(shape):
        return pl.BlockSpec(shape, lambda i: (0, 0))

    return pl.pallas_call(
        attention_kernel,
        grid=(1,),
        in_specs=[pl.BlockSpec((v.shape[0], WIDE), lambda i: (0, part)) for v in sums]
        + [
            fixed((HALF, 1)),
            fixed((HALF, HEAD_SIZE)),
            fixed((HALF, HEAD_SIZE)),
            fixed((HALF, SLOTS)),
            fixed((HALF, 2 * HEAD_SIZE)),
            fixed((HALF, 2 * HEAD_SIZE)),
        ],
        out_specs=fixed((HALF, 512)),
        out_shape=jax.ShapeDtypeStruct((HALF, 512), jnp.bfloat16),
        compiler_params=GRANT,
    )(*sums, scale, cosine, sine, bias, own, other)


def project_kernel(at_ref, rows_ref, near, near_other, near_kv, far, far_other, *outs):
    zh, core = at_ref[0], at_ref[1]
    step = pl.program_id(0)
    near_rows = rows_ref[0, :, pl.ds(pl.multiple_of(zh * 1024, 1024), 1024)]
    far_rows = rows_ref[0, :, pl.ds(pl.multiple_of((1 - zh) * 1024, 1024), 1024)]

    def put(start, near_part, far_part):
        cols = slice(start, start + near_part.shape[1])
        value = (dot(near_rows, near_part) + dot(far_rows, far_part)).astype(jnp.bfloat16)
        if len(outs) == 1:
            outs[0][:, cols] = value
            return
        for i in range(len(outs) // 2):

            @pl.when(step == i)
            def _():
                outs[2 * i][:, cols] = value[:128]
                outs[2 * i + 1][:, cols] = value[128:]

    def kv_cols(which):
        return near_kv[:, pl.ds(pl.multiple_of(which * HEAD_SIZE, HEAD_SIZE), HEAD_SIZE)]

    put(0, near[...], far[:, :512])
    put(512, kv_cols(core), far[:, 512:])
    put(WIDE, near_other[...], far_other[:, :512])
    put(WIDE + 512, kv_cols(1 - core), far_other[:, 512:])


def project(which, zh, core, gathered, weights, halves=False):
    steps = len(which)
    rows, outs = (128, 2 * steps) if halves else (HALF, 1)
    return pl.pallas_call(
        project_kernel,
        grid_spec=pltpu.PrefetchScalarGridSpec(
            num_scalar_prefetch=1,
            grid=(steps,),
            in_specs=[pl.BlockSpec((1, HALF, 2048), lambda i, at: (at[2 + i], 0, 0))]
            + [pl.BlockSpec(w.shape, lambda i, at: (0, 0)) for w in weights],
            out_specs=[pl.BlockSpec((rows, 2 * WIDE), lambda i, at: (0, 0))] * outs,
        ),
        out_shape=[jax.ShapeDtypeStruct((rows, 2 * WIDE), jnp.bfloat16)] * outs,
        compiler_params=GRANT,
    )(jnp.stack([zh, core, *which]).astype(jnp.int32), gathered, *weights)


def products_kernel(form, steps, at_ref, own_a, own_b, far_a, far_b, near, other, *outs):
    step = pl.program_id(0)

    def put(left, right):
        product = dot(left[...], near[0]) + dot(right[...], other[0])
        product = product.astype(jnp.bfloat16)
        for i in range(steps):

            @pl.when(step == i)
            def _():
                if form == "joined":
                    outs[0][i * 128 : i * 128 + 128] = product[:128]
                    outs[1][i * 128 : i * 128 + 128] = product[128:]
                elif form == "halves":
                    outs[2 * i][...] = product[:128]
                    outs[2 * i + 1][...] = product[128:]
                else:
                    outs[i][...] = product

    @pl.when(at_ref[steps + step] == 1)
    def _():
        put(own_a, own_b)

    @pl.when(at_ref[steps + step] == 0)
    def _():
        put(far_a, far_b)


def products(targets, zh, attended, near, other, form="whole"):
    steps = len(targets)
    blocks = [zt * 2 + xt // 2 for zt, xt in targets]
    owns = [xt % 2 == zh for _, xt in targets]
    at = jnp.stack([v.astype(jnp.int32) for v in blocks + owns])
    rows = pl.BlockSpec((HALF, 512), lambda i, at: (0, 0))
    block = pl.BlockSpec((1, 512, 1024), lambda i, at: (at[i], 0, 0))
    count = {"joined": 2, "halves": 2 * steps, "whole": steps}[form]
    size = 128 if form == "halves" else HALF
    return pl.pallas_call(
        lambda *refs: products_kernel(form, steps, *refs),
        grid_spec=pltpu.PrefetchScalarGridSpec(
            num_scalar_prefetch=1,
            grid=(steps,),
            in_specs=[rows] * 4 + [block] * 2,
            out_specs=[pl.BlockSpec((size, 1024), lambda i, at: (0, 0))] * count,
        ),
        out_shape=[jax.ShapeDtypeStruct((size, 1024), jnp.bfloat16)] * count,
        compiler_params=WIDE_GRANT if form == "joined" else GRANT,
    )(at, *attended, near, other)


def add_rows(value, arrived, start):
    rows = arrived.shape[0]
    return lax.dynamic_update_slice(value, value[start : start + rows] + arrived, (start, 0))


def half_of(value, which, dim=0):
    size = value.shape[dim] // 2
    return lax.dynamic_slice_in_dim(value, which * size, size, dim)


def ordered(first, own, other, dim=0):
    return jnp.where(
        first, jnp.concatenate([own, other], dim), jnp.concatenate([other, own], dim)
    )


def dot(a, b):
    return jnp.dot(a, b, preferred_element_type=jnp.float32)


def local(tokens, norm_gain, query_weight, kv_weight, out_weight, lengths):
    core = lax.axis_index("core")
    chip = lax.axis_index(("zl", "x"))
    zl = lax.axis_index("zl")
    x = lax.axis_index("x")
    y = lax.axis_index("y")
    zh = lax.axis_index("zh")
    is_first = core == 0

    near_other = core_swap(query_weight)

    gain = lax.dynamic_slice_in_dim(norm_gain, (chip * 2 + core) * 512, 512, 0)
    wide = tokens.astype(jnp.float32)
    gained = (wide * gain[None, :]).astype(jnp.bfloat16)
    mine = send(half_of(gained, core), to_slice(0))
    theirs = send(half_of(gained, 1 - core), to_slice(1))
    block = ordered(is_first, mine, theirs, 1)

    kv_near = lax.dynamic_slice_in_dim(kv_weight, chip * 256, 256, 1)
    kv_own = lax.dynamic_slice_in_dim(kv_weight, chip * 256 + core * 128, 128, 1)
    near = jnp.concatenate([query_weight, kv_own], axis=1)
    slice_gain = 1.0 / lax.dynamic_slice_in_dim(norm_gain, y * 2048, 2048, 0)
    own_slots = core * HALF + jnp.arange(HALF, dtype=jnp.int32)
    slot_k = jnp.concatenate([own_slots, (1 - core) * HALF + jnp.arange(HALF, dtype=jnp.int32)])
    allowed = (slot_k[None, :] <= own_slots[:, None]) & (slot_k[None, :] < lengths[0])
    bias = jnp.where(allowed, 0.0, -jnp.inf).astype(jnp.float32)
    cosine, sine = rope_tables(own_slots)
    block, near_other, kv_near, near = lax.optimization_barrier((block, near_other, kv_near, near))
    block, slice_gain, bias, cosine, sine = lax.optimization_barrier(
        (block, slice_gain, bias, cosine, sine)
    )

    beside = zl_swap(block)
    left = x_shift(block, 1)
    right = x_shift(block, -1)
    left, right, beside = lax.optimization_barrier((left, right, beside))
    far = zh_swap(after(near, beside))
    beside_left = x_shift(beside, 1)
    beside_right = x_shift(beside, -1)
    opposite = jnp.concatenate([x_shift(left[:128], 1), x_shift(right[128:], -1)], 0)
    beside_opposite = jnp.concatenate(
        [x_shift(beside_left[:128], 1), x_shift(beside_right[128:], -1)], 0
    )
    weights = (query_weight, near_other, kv_near, far, core_swap(after(far, beside_opposite)))
    gathered = jnp.zeros((4, HALF, 2048), jnp.bfloat16)
    for dz, dx, part in (
        (0, 0, block),
        (0, 3, left),
        (0, 1, right),
        (1, 0, beside),
        (0, 2, opposite),
        (1, 3, beside_left),
        (1, 1, beside_right),
        (1, 2, beside_opposite),
    ):
        zs, xs = zl ^ dz, (x + dx) % 4
        gathered = lax.dynamic_update_slice(
            gathered, part[None], (zs * 2 + xs // 2, 0, (xs % 2) * 1024)
        )

    out_near = lax.all_gather(after(out_weight, block), "y", axis=0, tiled=False)

    squares = jnp.sum(jnp.square(gathered.astype(jnp.float32) * slice_gain), axis=-1)
    low, high = project([(y + 2) % 4], zh, core, gathered, weights, True)
    from_below = y_shift(low, 1)
    from_above = y_shift(high, -1)
    a_top, a_bottom, b_top, b_bottom = project(
        [(y + 1) % 4, (y + 3) % 4], zh, core, gathered, weights, True
    )
    from_below, from_above, a_top, b_bottom = lax.optimization_barrier(
        (from_below, from_above, a_top, b_bottom)
    )
    a_bottom, b_top = y_shift(a_bottom, 1), y_shift(b_top, -1)
    a_top, b_bottom = a_top + from_below, b_bottom + from_above
    gathered = after(gathered, (a_top, b_bottom, a_bottom, b_top))
    (kept,) = project([y], zh, core, gathered, weights)
    sums = (kept, y_shift(a_top, 1), a_bottom, b_top, y_shift(b_bottom, -1))

    squares, a_top, b_bottom = lax.optimization_barrier((squares, a_top, b_bottom))
    total = lax.dynamic_index_in_dim(squares, y, 0, keepdims=False)
    for k in (1, 2, 3):
        total += y_shift(lax.dynamic_index_in_dim(squares, (y + k) % 4, 0, keepdims=False), k)
    scale = lax.rsqrt(total / 8192.0 + norm_eps)[:, None]

    kv_rows = key_value_rows(core, sums, scale, cosine, sine)
    kv_other = core_swap(kv_rows)
    out_other = core_swap(after(out_near, kv_other))
    own_a = attention(0, sums, scale, cosine, sine, bias, kv_rows, kv_other)
    far_a = zh_swap(own_a)
    own_b = attention(1, sums, scale, cosine, sine, bias, kv_rows, kv_other)
    far_b = zh_swap(own_b)
    attended = (own_a, own_b, far_a, far_b)

    def made(moves, form="whole"):
        targets = [(zl ^ dz, (x + dx) % 4) for dz, dx in moves]
        return products(targets, zh, attended, out_near, out_other, form)

    low, high = made([(1, 2), (0, 2)], "joined")
    from_left, from_right = x_shift(low, 1), x_shift(high, -1)
    a_top, a_bottom, b_top, b_bottom = made([(1, 1), (1, 3)], "halves")
    here_a, here_b, beside, mixed = made([(0, 1), (0, 3), (1, 0), (0, 0)])
    from_left, from_right, here_a, here_b = lax.optimization_barrier(
        (from_left, from_right, here_a, here_b)
    )
    a_bottom, b_top = x_shift(a_bottom, 1), x_shift(b_top, -1)
    a_top = x_shift(a_top + from_left[:128], 1)
    b_bottom = x_shift(b_bottom + from_right[:128], -1)
    here_a = x_shift(add_rows(here_a, from_left[128:], 0), 1)
    here_b = x_shift(add_rows(here_b, from_right[128:], 128), -1)

    def sum_of(*values):
        return sum(v.astype(jnp.float32) for v in values).astype(jnp.bfloat16)

    across = zl_swap(summed_up(beside, a_top, a_bottom, b_top, b_bottom))
    mixed = sum_of(mixed, here_a, here_b, across)
    keep = send(half_of(mixed, core, 1), to_home(0))
    got = send(half_of(mixed, 1 - core, 1), to_home(1))
    return (wide + ordered(is_first, keep, got, 0).astype(jnp.float32)).astype(jnp.bfloat16)


def solution(mesh):
    split = Mesh(mesh.devices.reshape(SIZES), AXES)
    gx, gy = ("zl", "x", "core"), ("y", "zh")
    placed = (P(gy, gx), P(), P(gy, gx), P(gy, None), P(gx, gy), P(gy))
    return jax.shard_map(
        local, mesh=split, in_specs=placed, out_specs=P(gy, gx), check_vma=False
    )
```

```python
import jax
import jax.numpy as jnp
from jax import lax
from jax.experimental import pallas as pl
from jax.experimental.pallas import tpu as pltpu
from jax.sharding import Mesh, PartitionSpec as P

HEAD_SIZE = 128
SLOTS = 512
HALF = 256
AXES = ("zl", "x", "core", "y", "zh")
SIZES = (2, 4, 2, 4, 2)

rope_base = 500000.0
norm_eps = 1e-05


def coords(i):
    out = {}
    for name, size in zip(AXES[::-1], SIZES[::-1]):
        i, out[name] = divmod(i, size)
    return out


def index(c):
    i = 0
    for name, size in zip(AXES, SIZES):
        i = i * size + c[name] % size
    return i


def pairs(change):
    out = []
    for i in range(128):
        c = coords(i)
        out.append((i, index({**c, **change(c)})))
    return out


def send(value, change):
    return lax.ppermute(value, AXES, pairs(change))


def core_swap(value):
    return send(value, lambda c: dict(core=1 - c["core"]))


def zh_swap(value):
    return send(value, lambda c: dict(zh=1 - c["zh"]))


def zl_swap(value):
    return send(value, lambda c: dict(zl=1 - c["zl"]))


def x_shift(value, k):
    return send(value, lambda c: dict(x=c["x"] + k))


def after(value, other):
    return lax.optimization_barrier((value, other))[0]


def y_shift(value, k):
    return send(value, lambda c: dict(y=c["y"] + k))


def to_slice(flip):
    def change(c):
        return dict(
            y=2 * c["zl"] + c["x"] // 2,
            zl=c["y"] // 2,
            x=(c["y"] % 2) * 2 + c["x"] % 2,
            core=c["core"] ^ flip,
        )

    return change


def to_home(flip):
    def change(c):
        moves = c["x"] % 2 != c["zh"]
        return dict(x=c["x"] ^ moves, zh=c["zh"] ^ moves, core=c["core"] ^ flip)

    return change


def rope_tables(positions):
    half_dim = HEAD_SIZE // 2
    steps_up = jnp.arange(0, half_dim, dtype=jnp.float32) * (2.0 / HEAD_SIZE)
    inverse = jnp.power(jnp.float32(rope_base), -steps_up)
    angles = positions.astype(jnp.float32)[:, None] * inverse[None, :]
    cosine, sine = jnp.cos(angles), jnp.sin(angles)
    return jnp.concatenate([cosine, cosine], 1), jnp.concatenate([-sine, sine], 1)


def rotated(vectors, cosine, sine):
    return vectors * cosine + pltpu.roll(vectors, HEAD_SIZE // 2, 1) * sine


WIDE = 640
GRANT = pltpu.CompilerParams(vmem_limit_bytes=24 * 1024 * 1024)
WIDE_GRANT = pltpu.CompilerParams(vmem_limit_bytes=52 * 1024 * 1024)


def total_of(refs, cols=slice(None)):
    whole, *halves = (ref[:, cols].astype(jnp.float32) for ref in refs)
    a_top, a_bottom, b_top, b_bottom = halves
    return whole + jnp.concatenate([a_top + b_top, a_bottom + b_bottom], axis=0)


def total_kernel(*refs):
    refs[-1][...] = total_of(refs[:-1]).astype(jnp.bfloat16)


def summed_up(*values):
    return pl.pallas_call(
        total_kernel,
        out_shape=jax.ShapeDtypeStruct(values[0].shape, jnp.bfloat16),
        compiler_params=WIDE_GRANT,
    )(*values)


def key_value_kernel(core_ref, *refs):
    scale_ref, cos_ref, sin_ref, out_ref = refs[10:]
    scale = scale_ref[...]
    keys = rotated(total_of(refs[:5]) * scale, cos_ref[...], sin_ref[...])
    out_ref[:, :HEAD_SIZE] = keys.astype(jnp.bfloat16)
    out_ref[:, HEAD_SIZE:] = (total_of(refs[5:10]) * scale).astype(jnp.bfloat16)


def key_value_rows(core, sums, scale, cosine, sine):
    keys = [
        pl.BlockSpec((v.shape[0], HEAD_SIZE), lambda i, c: (0, 4 + 5 * c[0])) for v in sums
    ]
    values = [
        pl.BlockSpec((v.shape[0], HEAD_SIZE), lambda i, c: (0, 9 - 5 * c[0])) for v in sums
    ]
    table = pl.BlockSpec((HALF, HEAD_SIZE), lambda i, c: (0, 0))
    return pl.pallas_call(
        key_value_kernel,
        grid_spec=pltpu.PrefetchScalarGridSpec(
            num_scalar_prefetch=1,
            grid=(1,),
            in_specs=keys
            + values
            + [pl.BlockSpec((HALF, 1), lambda i, c: (0, 0)), table, table],
            out_specs=pl.BlockSpec((HALF, 2 * HEAD_SIZE), lambda i, c: (0, 0)),
        ),
        out_shape=jax.ShapeDtypeStruct((HALF, 2 * HEAD_SIZE), jnp.bfloat16),
    )(core.reshape(1), *sums, *sums, scale, cosine, sine)


def attention_kernel(*refs):
    scale_ref, cos_ref, sin_ref, bias_ref, own_ref, other_ref, out_ref = refs[5:]
    contract = (((1,), (1,)), ((), ()))
    for head in range(4):
        cols = slice(head * HEAD_SIZE, (head + 1) * HEAD_SIZE)
        rows = total_of(refs[:5], cols) * scale_ref[...]
        queries = rotated(rows, cos_ref[...], sin_ref[...]).astype(jnp.bfloat16)

        def scores_of(ref, first):
            scores = lax.dot_general(
                queries, ref[:, :HEAD_SIZE], contract, preferred_element_type=jnp.float32
            )
            return scores * (HEAD_SIZE**-0.5) + bias_ref[:, first : first + HALF]

        own, other = scores_of(own_ref, 0), scores_of(other_ref, HALF)
        top = jnp.maximum(
            jnp.max(own, axis=-1, keepdims=True), jnp.max(other, axis=-1, keepdims=True)
        )
        own, other = jnp.exp(own - top), jnp.exp(other - top)
        total = jnp.sum(own, axis=-1, keepdims=True) + jnp.sum(other, axis=-1, keepdims=True)
        mixed = dot(own.astype(jnp.bfloat16), own_ref[:, HEAD_SIZE:]) + dot(
            other.astype(jnp.bfloat16), other_ref[:, HEAD_SIZE:]
        )
        out_ref[:, cols] = (mixed / total).astype(jnp.bfloat16)


def attention(part, sums, scale, cosine, sine, bias, own, other):
    def fixed(shape):
        return pl.BlockSpec(shape, lambda i: (0, 0))

    return pl.pallas_call(
        attention_kernel,
        grid=(1,),
        in_specs=[pl.BlockSpec((v.shape[0], WIDE), lambda i: (0, part)) for v in sums]
        + [
            fixed((HALF, 1)),
            fixed((HALF, HEAD_SIZE)),
            fixed((HALF, HEAD_SIZE)),
            fixed((HALF, SLOTS)),
            fixed((HALF, 2 * HEAD_SIZE)),
            fixed((HALF, 2 * HEAD_SIZE)),
        ],
        out_specs=fixed((HALF, 512)),
        out_shape=jax.ShapeDtypeStruct((HALF, 512), jnp.bfloat16),
        compiler_params=GRANT,
    )(*sums, scale, cosine, sine, bias, own, other)


def project_kernel(at_ref, rows_ref, near, near_other, near_kv, far, far_other, *outs):
    zh, core = at_ref[0], at_ref[1]
    step = pl.program_id(0)
    near_rows = rows_ref[0, :, pl.ds(pl.multiple_of(zh * 1024, 1024), 1024)]
    far_rows = rows_ref[0, :, pl.ds(pl.multiple_of((1 - zh) * 1024, 1024), 1024)]

    def put(start, near_part, far_part):
        cols = slice(start, start + near_part.shape[1])
        value = (dot(near_rows, near_part) + dot(far_rows, far_part)).astype(jnp.bfloat16)
        if len(outs) == 1:
            outs[0][:, cols] = value
            return
        for i in range(len(outs) // 2):

            @pl.when(step == i)
            def _():
                outs[2 * i][:, cols] = value[:128]
                outs[2 * i + 1][:, cols] = value[128:]

    def kv_cols(which):
        return near_kv[:, pl.ds(pl.multiple_of(which * HEAD_SIZE, HEAD_SIZE), HEAD_SIZE)]

    put(0, near[...], far[:, :512])
    put(512, kv_cols(core), far[:, 512:])
    put(WIDE, near_other[...], far_other[:, :512])
    put(WIDE + 512, kv_cols(1 - core), far_other[:, 512:])


def project(which, zh, core, gathered, weights, halves=False):
    steps = len(which)
    rows, outs = (128, 2 * steps) if halves else (HALF, 1)
    return pl.pallas_call(
        project_kernel,
        grid_spec=pltpu.PrefetchScalarGridSpec(
            num_scalar_prefetch=1,
            grid=(steps,),
            in_specs=[pl.BlockSpec((1, HALF, 2048), lambda i, at: (at[2 + i], 0, 0))]
            + [pl.BlockSpec(w.shape, lambda i, at: (0, 0)) for w in weights],
            out_specs=[pl.BlockSpec((rows, 2 * WIDE), lambda i, at: (0, 0))] * outs,
        ),
        out_shape=[jax.ShapeDtypeStruct((rows, 2 * WIDE), jnp.bfloat16)] * outs,
        compiler_params=GRANT,
    )(jnp.stack([zh, core, *which]).astype(jnp.int32), gathered, *weights)


def products_kernel(form, steps, at_ref, own_a, own_b, far_a, far_b, near, other, *outs):
    step = pl.program_id(0)

    def put(left, right):
        product = dot(left[...], near[0]) + dot(right[...], other[0])
        product = product.astype(jnp.bfloat16)
        for i in range(steps):

            @pl.when(step == i)
            def _():
                if form == "joined":
                    outs[0][i * 128 : i * 128 + 128] = product[:128]
                    outs[1][i * 128 : i * 128 + 128] = product[128:]
                elif form == "halves":
                    outs[2 * i][...] = product[:128]
                    outs[2 * i + 1][...] = product[128:]
                else:
                    outs[i][...] = product

    @pl.when(at_ref[steps + step] == 1)
    def _():
        put(own_a, own_b)

    @pl.when(at_ref[steps + step] == 0)
    def _():
        put(far_a, far_b)


def products(targets, zh, attended, near, other, form="whole"):
    steps = len(targets)
    blocks = [zt * 2 + xt // 2 for zt, xt in targets]
    owns = [xt % 2 == zh for _, xt in targets]
    at = jnp.stack([v.astype(jnp.int32) for v in blocks + owns])
    rows = pl.BlockSpec((HALF, 512), lambda i, at: (0, 0))
    block = pl.BlockSpec((1, 512, 1024), lambda i, at: (at[i], 0, 0))
    count = {"joined": 2, "halves": 2 * steps, "whole": steps}[form]
    size = 128 if form == "halves" else HALF
    return pl.pallas_call(
        lambda *refs: products_kernel(form, steps, *refs),
        grid_spec=pltpu.PrefetchScalarGridSpec(
            num_scalar_prefetch=1,
            grid=(steps,),
            in_specs=[rows] * 4 + [block] * 2,
            out_specs=[pl.BlockSpec((size, 1024), lambda i, at: (0, 0))] * count,
        ),
        out_shape=[jax.ShapeDtypeStruct((size, 1024), jnp.bfloat16)] * count,
        compiler_params=WIDE_GRANT if form == "joined" else GRANT,
    )(at, *attended, near, other)


def add_rows(value, arrived, start):
    rows = arrived.shape[0]
    return lax.dynamic_update_slice(value, value[start : start + rows] + arrived, (start, 0))


def half_of(value, which, dim=0):
    size = value.shape[dim] // 2
    return lax.dynamic_slice_in_dim(value, which * size, size, dim)


def ordered(first, own, other, dim=0):
    return jnp.where(
        first, jnp.concatenate([own, other], dim), jnp.concatenate([other, own], dim)
    )


def dot(a, b):
    return jnp.dot(a, b, preferred_element_type=jnp.float32)


def local(tokens, norm_gain, query_weight, kv_weight, out_weight, lengths):
    core = lax.axis_index("core")
    chip = lax.axis_index(("zl", "x"))
    zl = lax.axis_index("zl")
    x = lax.axis_index("x")
    y = lax.axis_index("y")
    zh = lax.axis_index("zh")
    is_first = core == 0

    near_other = core_swap(query_weight)

    gain = lax.dynamic_slice_in_dim(norm_gain, (chip * 2 + core) * 512, 512, 0)
    wide = tokens.astype(jnp.float32)
    gained = (wide * gain[None, :]).astype(jnp.bfloat16)
    mine = send(half_of(gained, core), to_slice(0))
    theirs = send(half_of(gained, 1 - core), to_slice(1))
    block = ordered(is_first, mine, theirs, 1)

    kv_near = lax.dynamic_slice_in_dim(kv_weight, chip * 256, 256, 1)
    kv_own = lax.dynamic_slice_in_dim(kv_weight, chip * 256 + core * 128, 128, 1)
    near = jnp.concatenate([query_weight, kv_own], axis=1)
    slice_gain = 1.0 / lax.dynamic_slice_in_dim(norm_gain, y * 2048, 2048, 0)
    own_slots = core * HALF + jnp.arange(HALF, dtype=jnp.int32)
    slot_k = jnp.concatenate([own_slots, (1 - core) * HALF + jnp.arange(HALF, dtype=jnp.int32)])
    allowed = (slot_k[None, :] <= own_slots[:, None]) & (slot_k[None, :] < lengths[0])
    bias = jnp.where(allowed, 0.0, -jnp.inf).astype(jnp.float32)
    cosine, sine = rope_tables(own_slots)
    block, near_other, kv_near, near = lax.optimization_barrier((block, near_other, kv_near, near))
    block, slice_gain, bias, cosine, sine = lax.optimization_barrier(
        (block, slice_gain, bias, cosine, sine)
    )

    beside = zl_swap(block)
    left = x_shift(block, 1)
    right = x_shift(block, -1)
    left, right, beside = lax.optimization_barrier((left, right, beside))
    far = zh_swap(after(near, beside))
    beside_left = x_shift(beside, 1)
    beside_right = x_shift(beside, -1)
    opposite = jnp.concatenate([x_shift(left[:128], 1), x_shift(right[128:], -1)], 0)
    beside_opposite = jnp.concatenate(
        [x_shift(beside_left[:128], 1), x_shift(beside_right[128:], -1)], 0
    )
    weights = (query_weight, near_other, kv_near, far, core_swap(after(far, beside_opposite)))
    gathered = jnp.zeros((4, HALF, 2048), jnp.bfloat16)
    for dz, dx, part in (
        (0, 0, block),
        (0, 3, left),
        (0, 1, right),
        (1, 0, beside),
        (0, 2, opposite),
        (1, 3, beside_left),
        (1, 1, beside_right),
        (1, 2, beside_opposite),
    ):
        zs, xs = zl ^ dz, (x + dx) % 4
        gathered = lax.dynamic_update_slice(
            gathered, part[None], (zs * 2 + xs // 2, 0, (xs % 2) * 1024)
        )

    out_near = lax.all_gather(after(out_weight, block), "y", axis=0, tiled=False)

    squares = jnp.sum(jnp.square(gathered.astype(jnp.float32) * slice_gain), axis=-1)
    low, high = project([(y + 2) % 4], zh, core, gathered, weights, True)
    from_below = y_shift(low, 1)
    from_above = y_shift(high, -1)
    a_top, a_bottom, b_top, b_bottom = project(
        [(y + 1) % 4, (y + 3) % 4], zh, core, gathered, weights, True
    )
    from_below, from_above, a_top, b_bottom = lax.optimization_barrier(
        (from_below, from_above, a_top, b_bottom)
    )
    a_bottom, b_top = y_shift(a_bottom, 1), y_shift(b_top, -1)
    a_top, b_bottom = a_top + from_below, b_bottom + from_above
    gathered = after(gathered, (a_top, b_bottom, a_bottom, b_top))
    (kept,) = project([y], zh, core, gathered, weights)
    sums = (kept, y_shift(a_top, 1), a_bottom, b_top, y_shift(b_bottom, -1))

    squares, a_top, b_bottom = lax.optimization_barrier((squares, a_top, b_bottom))
    total = lax.dynamic_index_in_dim(squares, y, 0, keepdims=False)
    for k in (1, 2, 3):
        total += y_shift(lax.dynamic_index_in_dim(squares, (y + k) % 4, 0, keepdims=False), k)
    scale = lax.rsqrt(total / 8192.0 + norm_eps)[:, None]

    kv_rows = key_value_rows(core, sums, scale, cosine, sine)
    kv_other = core_swap(kv_rows)
    out_other = core_swap(after(out_near, kv_other))
    own_a = attention(0, sums, scale, cosine, sine, bias, kv_rows, kv_other)
    far_a = zh_swap(own_a)
    own_b = attention(1, sums, scale, cosine, sine, bias, kv_rows, kv_other)
    far_b = zh_swap(own_b)
    attended = (own_a, own_b, far_a, far_b)

    def made(moves, form="whole"):
        targets = [(zl ^ dz, (x + dx) % 4) for dz, dx in moves]
        return products(targets, zh, attended, out_near, out_other, form)

    low, high = made([(1, 2), (0, 2)], "joined")
    from_left, from_right = x_shift(low, 1), x_shift(high, -1)
    a_top, a_bottom, b_top, b_bottom = made([(1, 1), (1, 3)], "halves")
    here_a, here_b, beside, mixed = made([(0, 1), (0, 3), (1, 0), (0, 0)])
    from_left, from_right, here_a, here_b = lax.optimization_barrier(
        (from_left, from_right, here_a, here_b)
    )
    a_bottom, b_top = x_shift(a_bottom, 1), x_shift(b_top, -1)
    a_top = x_shift(a_top + from_left[:128], 1)
    b_bottom = x_shift(b_bottom + from_right[:128], -1)
    here_a = x_shift(add_rows(here_a, from_left[128:], 0), 1)
    here_b = x_shift(add_rows(here_b, from_right[128:], 128), -1)

    def sum_of(*values):
        return sum(v.astype(jnp.float32) for v in values).astype(jnp.bfloat16)

    across = zl_swap(summed_up(beside, a_top, a_bottom, b_top, b_bottom))
    mixed = sum_of(mixed, here_a, here_b, across)
    keep = send(half_of(mixed, core, 1), to_home(0))
    got = send(half_of(mixed, 1 - core, 1), to_home(1))
    return (wide + ordered(is_first, keep, got, 0).astype(jnp.float32)).astype(jnp.bfloat16)


def solution(mesh):
    split = Mesh(mesh.devices.reshape(SIZES), AXES)
    gx, gy = ("zl", "x", "core"), ("y", "zh")
    placed = (P(gy, gx), P(), P(gy, gx), P(gy, None), P(gx, gy), P(gy))
    return jax.shard_map(
        local, mesh=split, in_specs=placed, out_specs=P(gy, gx), check_vma=False
    )
```

```python
import jax
import jax.numpy as jnp
from jax import lax
from jax.experimental import pallas as pl
from jax.experimental.pallas import tpu as pltpu
from jax.sharding import Mesh, PartitionSpec as P

HEAD_SIZE = 128
SLOTS = 512
HALF = 256
AXES = ("zl", "x", "core", "y", "zh")
SIZES = (2, 4, 2, 4, 2)

rope_base = 500000.0
norm_eps = 1e-05


def coords(i):
    out = {}
    for name, size in zip(AXES[::-1], SIZES[::-1]):
        i, out[name] = divmod(i, size)
    return out


def index(c):
    i = 0
    for name, size in zip(AXES, SIZES):
        i = i * size + c[name] % size
    return i


def pairs(change):
    out = []
    for i in range(128):
        c = coords(i)
        out.append((i, index({**c, **change(c)})))
    return out


def send(value, change):
    return lax.ppermute(value, AXES, pairs(change))


def core_swap(value):
    return send(value, lambda c: dict(core=1 - c["core"]))


def zh_swap(value):
    return send(value, lambda c: dict(zh=1 - c["zh"]))


def zl_swap(value):
    return send(value, lambda c: dict(zl=1 - c["zl"]))


def x_shift(value, k):
    return send(value, lambda c: dict(x=c["x"] + k))


def after(value, other):
    return lax.optimization_barrier((value, other))[0]


def y_shift(value, k):
    return send(value, lambda c: dict(y=c["y"] + k))


def to_slice(flip):
    def change(c):
        return dict(
            y=2 * c["zl"] + c["x"] // 2,
            zl=c["y"] // 2,
            x=(c["y"] % 2) * 2 + c["x"] % 2,
            core=c["core"] ^ flip,
        )

    return change


def to_home(flip):
    def change(c):
        moves = c["x"] % 2 != c["zh"]
        return dict(x=c["x"] ^ moves, zh=c["zh"] ^ moves, core=c["core"] ^ flip)

    return change


def rope_tables(positions):
    half_dim = HEAD_SIZE // 2
    steps_up = jnp.arange(0, half_dim, dtype=jnp.float32) * (2.0 / HEAD_SIZE)
    inverse = jnp.power(jnp.float32(rope_base), -steps_up)
    angles = positions.astype(jnp.float32)[:, None] * inverse[None, :]
    cosine, sine = jnp.cos(angles), jnp.sin(angles)
    return jnp.concatenate([cosine, cosine], 1), jnp.concatenate([-sine, sine], 1)


def rotated(vectors, cosine, sine):
    return vectors * cosine + pltpu.roll(vectors, HEAD_SIZE // 2, 1) * sine


WIDE = 640
GRANT = pltpu.CompilerParams(vmem_limit_bytes=24 * 1024 * 1024)
WIDE_GRANT = pltpu.CompilerParams(vmem_limit_bytes=52 * 1024 * 1024)


def total_of(refs, cols=slice(None)):
    whole, *halves = (ref[:, cols].astype(jnp.float32) for ref in refs)
    a_top, a_bottom, b_top, b_bottom = halves
    return whole + jnp.concatenate([a_top + b_top, a_bottom + b_bottom], axis=0)


def total_kernel(*refs):
    refs[-1][...] = total_of(refs[:-1]).astype(jnp.bfloat16)


def summed_up(*values):
    return pl.pallas_call(
        total_kernel,
        out_shape=jax.ShapeDtypeStruct(values[0].shape, jnp.bfloat16),
        compiler_params=WIDE_GRANT,
    )(*values)


def key_value_kernel(core_ref, *refs):
    scale_ref, cos_ref, sin_ref, out_ref = refs[10:]
    scale = scale_ref[...]
    keys = rotated(total_of(refs[:5]) * scale, cos_ref[...], sin_ref[...])
    out_ref[:, :HEAD_SIZE] = keys.astype(jnp.bfloat16)
    out_ref[:, HEAD_SIZE:] = (total_of(refs[5:10]) * scale).astype(jnp.bfloat16)


def key_value_rows(core, sums, scale, cosine, sine):
    keys = [
        pl.BlockSpec((v.shape[0], HEAD_SIZE), lambda i, c: (0, 4 + 5 * c[0])) for v in sums
    ]
    values = [
        pl.BlockSpec((v.shape[0], HEAD_SIZE), lambda i, c: (0, 9 - 5 * c[0])) for v in sums
    ]
    table = pl.BlockSpec((HALF, HEAD_SIZE), lambda i, c: (0, 0))
    return pl.pallas_call(
        key_value_kernel,
        grid_spec=pltpu.PrefetchScalarGridSpec(
            num_scalar_prefetch=1,
            grid=(1,),
            in_specs=keys
            + values
            + [pl.BlockSpec((HALF, 1), lambda i, c: (0, 0)), table, table],
            out_specs=pl.BlockSpec((HALF, 2 * HEAD_SIZE), lambda i, c: (0, 0)),
        ),
        out_shape=jax.ShapeDtypeStruct((HALF, 2 * HEAD_SIZE), jnp.bfloat16),
    )(core.reshape(1), *sums, *sums, scale, cosine, sine)


def attention_kernel(*refs):
    scale_ref, cos_ref, sin_ref, bias_ref, own_ref, other_ref, out_ref = refs[5:]
    contract = (((1,), (1,)), ((), ()))
    for head in range(4):
        cols = slice(head * HEAD_SIZE, (head + 1) * HEAD_SIZE)
        rows = total_of(refs[:5], cols) * scale_ref[...]
        queries = rotated(rows, cos_ref[...], sin_ref[...]).astype(jnp.bfloat16)

        def scores_of(ref, first):
            scores = lax.dot_general(
                queries, ref[:, :HEAD_SIZE], contract, preferred_element_type=jnp.float32
            )
            return scores * (HEAD_SIZE**-0.5) + bias_ref[:, first : first + HALF]

        own, other = scores_of(own_ref, 0), scores_of(other_ref, HALF)
        top = jnp.maximum(
            jnp.max(own, axis=-1, keepdims=True), jnp.max(other, axis=-1, keepdims=True)
        )
        own, other = jnp.exp(own - top), jnp.exp(other - top)
        total = jnp.sum(own, axis=-1, keepdims=True) + jnp.sum(other, axis=-1, keepdims=True)
        mixed = dot(own.astype(jnp.bfloat16), own_ref[:, HEAD_SIZE:]) + dot(
            other.astype(jnp.bfloat16), other_ref[:, HEAD_SIZE:]
        )
        out_ref[:, cols] = (mixed / total).astype(jnp.bfloat16)


def attention(part, sums, scale, cosine, sine, bias, own, other):
    def fixed(shape):
        return pl.BlockSpec(shape, lambda i: (0, 0))

    return pl.pallas_call(
        attention_kernel,
        grid=(1,),
        in_specs=[pl.BlockSpec((v.shape[0], WIDE), lambda i: (0, part)) for v in sums]
        + [
            fixed((HALF, 1)),
            fixed((HALF, HEAD_SIZE)),
            fixed((HALF, HEAD_SIZE)),
            fixed((HALF, SLOTS)),
            fixed((HALF, 2 * HEAD_SIZE)),
            fixed((HALF, 2 * HEAD_SIZE)),
        ],
        out_specs=fixed((HALF, 512)),
        out_shape=jax.ShapeDtypeStruct((HALF, 512), jnp.bfloat16),
        compiler_params=GRANT,
    )(*sums, scale, cosine, sine, bias, own, other)


def project_kernel(at_ref, rows_ref, near, near_other, near_kv, far, far_other, *outs):
    zh, core = at_ref[0], at_ref[1]
    step = pl.program_id(0)
    near_rows = rows_ref[0, :, pl.ds(pl.multiple_of(zh * 1024, 1024), 1024)]
    far_rows = rows_ref[0, :, pl.ds(pl.multiple_of((1 - zh) * 1024, 1024), 1024)]

    def put(start, near_part, far_part):
        cols = slice(start, start + near_part.shape[1])
        value = (dot(near_rows, near_part) + dot(far_rows, far_part)).astype(jnp.bfloat16)
        if len(outs) == 1:
            outs[0][:, cols] = value
            return
        for i in range(len(outs) // 2):

            @pl.when(step == i)
            def _():
                outs[2 * i][:, cols] = value[:128]
                outs[2 * i + 1][:, cols] = value[128:]

    def kv_cols(which):
        return near_kv[:, pl.ds(pl.multiple_of(which * HEAD_SIZE, HEAD_SIZE), HEAD_SIZE)]

    put(0, near[...], far[:, :512])
    put(512, kv_cols(core), far[:, 512:])
    put(WIDE, near_other[...], far_other[:, :512])
    put(WIDE + 512, kv_cols(1 - core), far_other[:, 512:])


def project(which, zh, core, gathered, weights, halves=False):
    steps = len(which)
    rows, outs = (128, 2 * steps) if halves else (HALF, 1)
    return pl.pallas_call(
        project_kernel,
        grid_spec=pltpu.PrefetchScalarGridSpec(
            num_scalar_prefetch=1,
            grid=(steps,),
            in_specs=[pl.BlockSpec((1, HALF, 2048), lambda i, at: (at[2 + i], 0, 0))]
            + [pl.BlockSpec(w.shape, lambda i, at: (0, 0)) for w in weights],
            out_specs=[pl.BlockSpec((rows, 2 * WIDE), lambda i, at: (0, 0))] * outs,
        ),
        out_shape=[jax.ShapeDtypeStruct((rows, 2 * WIDE), jnp.bfloat16)] * outs,
        compiler_params=GRANT,
    )(jnp.stack([zh, core, *which]).astype(jnp.int32), gathered, *weights)


def products_kernel(form, steps, at_ref, own_a, own_b, far_a, far_b, near, other, *outs):
    step = pl.program_id(0)

    def put(left, right):
        product = dot(left[...], near[0]) + dot(right[...], other[0])
        product = product.astype(jnp.bfloat16)
        for i in range(steps):

            @pl.when(step == i)
            def _():
                if form == "joined":
                    outs[0][i * 128 : i * 128 + 128] = product[:128]
                    outs[1][i * 128 : i * 128 + 128] = product[128:]
                elif form == "halves":
                    outs[2 * i][...] = product[:128]
                    outs[2 * i + 1][...] = product[128:]
                else:
                    outs[i][...] = product

    @pl.when(at_ref[steps + step] == 1)
    def _():
        put(own_a, own_b)

    @pl.when(at_ref[steps + step] == 0)
    def _():
        put(far_a, far_b)


def products(targets, zh, attended, near, other, form="whole"):
    steps = len(targets)
    blocks = [zt * 2 + xt // 2 for zt, xt in targets]
    owns = [xt % 2 == zh for _, xt in targets]
    at = jnp.stack([v.astype(jnp.int32) for v in blocks + owns])
    rows = pl.BlockSpec((HALF, 512), lambda i, at: (0, 0))
    block = pl.BlockSpec((1, 512, 1024), lambda i, at: (at[i], 0, 0))
    count = {"joined": 2, "halves": 2 * steps, "whole": steps}[form]
    size = 128 if form == "halves" else HALF
    return pl.pallas_call(
        lambda *refs: products_kernel(form, steps, *refs),
        grid_spec=pltpu.PrefetchScalarGridSpec(
            num_scalar_prefetch=1,
            grid=(steps,),
            in_specs=[rows] * 4 + [block] * 2,
            out_specs=[pl.BlockSpec((size, 1024), lambda i, at: (0, 0))] * count,
        ),
        out_shape=[jax.ShapeDtypeStruct((size, 1024), jnp.bfloat16)] * count,
        compiler_params=WIDE_GRANT if form == "joined" else GRANT,
    )(at, *attended, near, other)


def add_rows(value, arrived, start):
    rows = arrived.shape[0]
    return lax.dynamic_update_slice(value, value[start : start + rows] + arrived, (start, 0))


def half_of(value, which, dim=0):
    size = value.shape[dim] // 2
    return lax.dynamic_slice_in_dim(value, which * size, size, dim)


def ordered(first, own, other, dim=0):
    return jnp.where(
        first, jnp.concatenate([own, other], dim), jnp.concatenate([other, own], dim)
    )


def dot(a, b):
    return jnp.dot(a, b, preferred_element_type=jnp.float32)


def local(tokens, norm_gain, query_weight, kv_weight, out_weight, lengths):
    core = lax.axis_index("core")
    chip = lax.axis_index(("zl", "x"))
    zl = lax.axis_index("zl")
    x = lax.axis_index("x")
    y = lax.axis_index("y")
    zh = lax.axis_index("zh")
    is_first = core == 0

    near_other = core_swap(query_weight)

    gain = lax.dynamic_slice_in_dim(norm_gain, (chip * 2 + core) * 512, 512, 0)
    wide = tokens.astype(jnp.float32)
    gained = (wide * gain[None, :]).astype(jnp.bfloat16)
    mine = send(half_of(gained, core), to_slice(0))
    theirs = send(half_of(gained, 1 - core), to_slice(1))
    block = ordered(is_first, mine, theirs, 1)

    kv_near = lax.dynamic_slice_in_dim(kv_weight, chip * 256, 256, 1)
    kv_own = lax.dynamic_slice_in_dim(kv_weight, chip * 256 + core * 128, 128, 1)
    near = jnp.concatenate([query_weight, kv_own], axis=1)
    slice_gain = 1.0 / lax.dynamic_slice_in_dim(norm_gain, y * 2048, 2048, 0)
    own_slots = core * HALF + jnp.arange(HALF, dtype=jnp.int32)
    slot_k = jnp.concatenate([own_slots, (1 - core) * HALF + jnp.arange(HALF, dtype=jnp.int32)])
    allowed = (slot_k[None, :] <= own_slots[:, None]) & (slot_k[None, :] < lengths[0])
    bias = jnp.where(allowed, 0.0, -jnp.inf).astype(jnp.float32)
    cosine, sine = rope_tables(own_slots)
    block, near_other, kv_near, near = lax.optimization_barrier((block, near_other, kv_near, near))
    block, slice_gain, bias, cosine, sine = lax.optimization_barrier(
        (block, slice_gain, bias, cosine, sine)
    )

    beside = zl_swap(block)
    left = x_shift(block, 1)
    right = x_shift(block, -1)
    left, right, beside = lax.optimization_barrier((left, right, beside))
    far = zh_swap(after(near, beside))
    beside_left = x_shift(beside, 1)
    beside_right = x_shift(beside, -1)
    opposite = jnp.concatenate([x_shift(left[:128], 1), x_shift(right[128:], -1)], 0)
    beside_opposite = jnp.concatenate(
        [x_shift(beside_left[:128], 1), x_shift(beside_right[128:], -1)], 0
    )
    weights = (query_weight, near_other, kv_near, far, core_swap(after(far, beside_opposite)))
    gathered = jnp.zeros((4, HALF, 2048), jnp.bfloat16)
    for dz, dx, part in (
        (0, 0, block),
        (0, 3, left),
        (0, 1, right),
        (1, 0, beside),
        (0, 2, opposite),
        (1, 3, beside_left),
        (1, 1, beside_right),
        (1, 2, beside_opposite),
    ):
        zs, xs = zl ^ dz, (x + dx) % 4
        gathered = lax.dynamic_update_slice(
            gathered, part[None], (zs * 2 + xs // 2, 0, (xs % 2) * 1024)
        )

    out_near = lax.all_gather(after(out_weight, block), "y", axis=0, tiled=False)

    squares = jnp.sum(jnp.square(gathered.astype(jnp.float32) * slice_gain), axis=-1)
    low, high = project([(y + 2) % 4], zh, core, gathered, weights, True)
    from_below = y_shift(low, 1)
    from_above = y_shift(high, -1)
    a_top, a_bottom, b_top, b_bottom = project(
        [(y + 1) % 4, (y + 3) % 4], zh, core, gathered, weights, True
    )
    from_below, from_above, a_top, b_bottom = lax.optimization_barrier(
        (from_below, from_above, a_top, b_bottom)
    )
    a_bottom, b_top = y_shift(a_bottom, 1), y_shift(b_top, -1)
    a_top, b_bottom = a_top + from_below, b_bottom + from_above
    gathered = after(gathered, (a_top, b_bottom, a_bottom, b_top))
    (kept,) = project([y], zh, core, gathered, weights)
    sums = (kept, y_shift(a_top, 1), a_bottom, b_top, y_shift(b_bottom, -1))

    squares, a_top, b_bottom = lax.optimization_barrier((squares, a_top, b_bottom))
    total = lax.dynamic_index_in_dim(squares, y, 0, keepdims=False)
    for k in (1, 2, 3):
        total += y_shift(lax.dynamic_index_in_dim(squares, (y + k) % 4, 0, keepdims=False), k)
    scale = lax.rsqrt(total / 8192.0 + norm_eps)[:, None]

    kv_rows = key_value_rows(core, sums, scale, cosine, sine)
    kv_other = core_swap(kv_rows)
    out_other = core_swap(after(out_near, kv_other))
    own_a = attention(0, sums, scale, cosine, sine, bias, kv_rows, kv_other)
    far_a = zh_swap(own_a)
    own_b = attention(1, sums, scale, cosine, sine, bias, kv_rows, kv_other)
    far_b = zh_swap(own_b)
    attended = (own_a, own_b, far_a, far_b)

    def made(moves, form="whole"):
        targets = [(zl ^ dz, (x + dx) % 4) for dz, dx in moves]
        return products(targets, zh, attended, out_near, out_other, form)

    low, high = made([(1, 2), (0, 2)], "joined")
    from_left, from_right = x_shift(low, 1), x_shift(high, -1)
    a_top, a_bottom, b_top, b_bottom = made([(1, 1), (1, 3)], "halves")
    here_a, here_b, beside, mixed = made([(0, 1), (0, 3), (1, 0), (0, 0)])
    from_left, from_right, here_a, here_b = lax.optimization_barrier(
        (from_left, from_right, here_a, here_b)
    )
    a_bottom, b_top = x_shift(a_bottom, 1), x_shift(b_top, -1)
    a_top, b_bottom = a_top + from_left[:128], b_bottom + from_right[:128]
    here_a, here_b, a_top, b_bottom = lax.optimization_barrier((here_a, here_b, a_top, b_bottom))
    a_top, b_bottom = x_shift(a_top, 1), x_shift(b_bottom, -1)
    here_a = x_shift(add_rows(here_a, from_left[128:], 0), 1)
    here_b = x_shift(add_rows(here_b, from_right[128:], 128), -1)

    def sum_of(*values):
        return sum(v.astype(jnp.float32) for v in values).astype(jnp.bfloat16)

    across = zl_swap(summed_up(beside, a_top, a_bottom, b_top, b_bottom))
    mixed = sum_of(mixed, here_a, here_b, across)
    keep = send(half_of(mixed, core, 1), to_home(0))
    got = send(half_of(mixed, 1 - core, 1), to_home(1))
    return (wide + ordered(is_first, keep, got, 0).astype(jnp.float32)).astype(jnp.bfloat16)


def solution(mesh):
    split = Mesh(mesh.devices.reshape(SIZES), AXES)
    gx, gy = ("zl", "x", "core"), ("y", "zh")
    placed = (P(gy, gx), P(), P(gy, gx), P(gy, None), P(gx, gy), P(gy))
    return jax.shard_map(
        local, mesh=split, in_specs=placed, out_specs=P(gy, gx), check_vma=False
    )
```

```python
import jax
import jax.numpy as jnp
from jax import lax
from jax.experimental import pallas as pl
from jax.experimental.pallas import tpu as pltpu
from jax.sharding import Mesh, PartitionSpec as P

HEAD_SIZE = 128
SLOTS = 512
HALF = 256
AXES = ("zl", "x", "core", "y", "zh")
SIZES = (2, 4, 2, 4, 2)

rope_base = 500000.0
norm_eps = 1e-05


def coords(i):
    out = {}
    for name, size in zip(AXES[::-1], SIZES[::-1]):
        i, out[name] = divmod(i, size)
    return out


def index(c):
    i = 0
    for name, size in zip(AXES, SIZES):
        i = i * size + c[name] % size
    return i


def pairs(change):
    out = []
    for i in range(128):
        c = coords(i)
        out.append((i, index({**c, **change(c)})))
    return out


def send(value, change):
    return lax.ppermute(value, AXES, pairs(change))


def core_swap(value):
    return send(value, lambda c: dict(core=1 - c["core"]))


def zh_swap(value):
    return send(value, lambda c: dict(zh=1 - c["zh"]))


def zl_swap(value):
    return send(value, lambda c: dict(zl=1 - c["zl"]))


def x_shift(value, k):
    return send(value, lambda c: dict(x=c["x"] + k))


def after(value, other):
    return lax.optimization_barrier((value, other))[0]


def y_shift(value, k):
    return send(value, lambda c: dict(y=c["y"] + k))


def to_slice(flip):
    def change(c):
        return dict(
            y=2 * c["zl"] + c["x"] // 2,
            zl=c["y"] // 2,
            x=(c["y"] % 2) * 2 + c["x"] % 2,
            core=c["core"] ^ flip,
        )

    return change


def to_home(flip):
    def change(c):
        moves = c["x"] % 2 != c["zh"]
        return dict(x=c["x"] ^ moves, zh=c["zh"] ^ moves, core=c["core"] ^ flip)

    return change


def rope_tables(positions):
    half_dim = HEAD_SIZE // 2
    steps_up = jnp.arange(0, half_dim, dtype=jnp.float32) * (2.0 / HEAD_SIZE)
    inverse = jnp.power(jnp.float32(rope_base), -steps_up)
    angles = positions.astype(jnp.float32)[:, None] * inverse[None, :]
    cosine, sine = jnp.cos(angles), jnp.sin(angles)
    return jnp.concatenate([cosine, cosine], 1), jnp.concatenate([-sine, sine], 1)


def rotated(vectors, cosine, sine):
    return vectors * cosine + pltpu.roll(vectors, HEAD_SIZE // 2, 1) * sine


WIDE = 640
GRANT = pltpu.CompilerParams(vmem_limit_bytes=24 * 1024 * 1024)
WIDE_GRANT = pltpu.CompilerParams(vmem_limit_bytes=52 * 1024 * 1024)


def total_of(refs, cols=slice(None)):
    whole, *halves = (ref[:, cols].astype(jnp.float32) for ref in refs)
    a_top, a_bottom, b_top, b_bottom = halves
    return whole + jnp.concatenate([a_top + b_top, a_bottom + b_bottom], axis=0)


def total_kernel(*refs):
    refs[-1][...] = total_of(refs[:-1]).astype(jnp.bfloat16)


def summed_up(*values):
    return pl.pallas_call(
        total_kernel,
        out_shape=jax.ShapeDtypeStruct(values[0].shape, jnp.bfloat16),
        compiler_params=WIDE_GRANT,
    )(*values)


def key_value_kernel(core_ref, *refs):
    scale_ref, cos_ref, sin_ref, out_ref = refs[10:]
    scale = scale_ref[...]
    keys = rotated(total_of(refs[:5]) * scale, cos_ref[...], sin_ref[...])
    out_ref[:, :HEAD_SIZE] = keys.astype(jnp.bfloat16)
    out_ref[:, HEAD_SIZE:] = (total_of(refs[5:10]) * scale).astype(jnp.bfloat16)


def key_value_rows(core, sums, scale, cosine, sine):
    keys = [
        pl.BlockSpec((v.shape[0], HEAD_SIZE), lambda i, c: (0, 4 + 5 * c[0])) for v in sums
    ]
    values = [
        pl.BlockSpec((v.shape[0], HEAD_SIZE), lambda i, c: (0, 9 - 5 * c[0])) for v in sums
    ]
    table = pl.BlockSpec((HALF, HEAD_SIZE), lambda i, c: (0, 0))
    return pl.pallas_call(
        key_value_kernel,
        grid_spec=pltpu.PrefetchScalarGridSpec(
            num_scalar_prefetch=1,
            grid=(1,),
            in_specs=keys
            + values
            + [pl.BlockSpec((HALF, 1), lambda i, c: (0, 0)), table, table],
            out_specs=pl.BlockSpec((HALF, 2 * HEAD_SIZE), lambda i, c: (0, 0)),
        ),
        out_shape=jax.ShapeDtypeStruct((HALF, 2 * HEAD_SIZE), jnp.bfloat16),
    )(core.reshape(1), *sums, *sums, scale, cosine, sine)


def attention_kernel(*refs):
    scale_ref, cos_ref, sin_ref, bias_ref, own_ref, other_ref, out_ref = refs[5:]
    contract = (((1,), (1,)), ((), ()))
    for head in range(4):
        cols = slice(head * HEAD_SIZE, (head + 1) * HEAD_SIZE)
        rows = total_of(refs[:5], cols) * scale_ref[...]
        queries = rotated(rows, cos_ref[...], sin_ref[...]).astype(jnp.bfloat16)

        def scores_of(ref, first):
            scores = lax.dot_general(
                queries, ref[:, :HEAD_SIZE], contract, preferred_element_type=jnp.float32
            )
            return scores * (HEAD_SIZE**-0.5) + bias_ref[:, first : first + HALF]

        own, other = scores_of(own_ref, 0), scores_of(other_ref, HALF)
        top = jnp.maximum(
            jnp.max(own, axis=-1, keepdims=True), jnp.max(other, axis=-1, keepdims=True)
        )
        own, other = jnp.exp(own - top), jnp.exp(other - top)
        total = jnp.sum(own, axis=-1, keepdims=True) + jnp.sum(other, axis=-1, keepdims=True)
        mixed = dot(own.astype(jnp.bfloat16), own_ref[:, HEAD_SIZE:]) + dot(
            other.astype(jnp.bfloat16), other_ref[:, HEAD_SIZE:]
        )
        out_ref[:, cols] = (mixed / total).astype(jnp.bfloat16)


def attention(part, sums, scale, cosine, sine, bias, own, other):
    def fixed(shape):
        return pl.BlockSpec(shape, lambda i: (0, 0))

    return pl.pallas_call(
        attention_kernel,
        grid=(1,),
        in_specs=[pl.BlockSpec((v.shape[0], WIDE), lambda i: (0, part)) for v in sums]
        + [
            fixed((HALF, 1)),
            fixed((HALF, HEAD_SIZE)),
            fixed((HALF, HEAD_SIZE)),
            fixed((HALF, SLOTS)),
            fixed((HALF, 2 * HEAD_SIZE)),
            fixed((HALF, 2 * HEAD_SIZE)),
        ],
        out_specs=fixed((HALF, 512)),
        out_shape=jax.ShapeDtypeStruct((HALF, 512), jnp.bfloat16),
        compiler_params=GRANT,
    )(*sums, scale, cosine, sine, bias, own, other)


def project_kernel(at_ref, rows_ref, near, near_other, near_kv, far, far_other, *outs):
    zh, core = at_ref[0], at_ref[1]
    step = pl.program_id(0)
    near_rows = rows_ref[0, :, pl.ds(pl.multiple_of(zh * 1024, 1024), 1024)]
    far_rows = rows_ref[0, :, pl.ds(pl.multiple_of((1 - zh) * 1024, 1024), 1024)]

    def put(start, near_part, far_part):
        cols = slice(start, start + near_part.shape[1])
        value = (dot(near_rows, near_part) + dot(far_rows, far_part)).astype(jnp.bfloat16)
        if len(outs) == 1:
            outs[0][:, cols] = value
            return
        for i in range(len(outs) // 2):

            @pl.when(step == i)
            def _():
                outs[2 * i][:, cols] = value[:128]
                outs[2 * i + 1][:, cols] = value[128:]

    def kv_cols(which):
        return near_kv[:, pl.ds(pl.multiple_of(which * HEAD_SIZE, HEAD_SIZE), HEAD_SIZE)]

    put(0, near[...], far[:, :512])
    put(512, kv_cols(core), far[:, 512:])
    put(WIDE, near_other[...], far_other[:, :512])
    put(WIDE + 512, kv_cols(1 - core), far_other[:, 512:])


def project(which, zh, core, gathered, weights, halves=False):
    steps = len(which)
    rows, outs = (128, 2 * steps) if halves else (HALF, 1)
    return pl.pallas_call(
        project_kernel,
        grid_spec=pltpu.PrefetchScalarGridSpec(
            num_scalar_prefetch=1,
            grid=(steps,),
            in_specs=[pl.BlockSpec((1, HALF, 2048), lambda i, at: (at[2 + i], 0, 0))]
            + [pl.BlockSpec(w.shape, lambda i, at: (0, 0)) for w in weights],
            out_specs=[pl.BlockSpec((rows, 2 * WIDE), lambda i, at: (0, 0))] * outs,
        ),
        out_shape=[jax.ShapeDtypeStruct((rows, 2 * WIDE), jnp.bfloat16)] * outs,
        compiler_params=GRANT,
    )(jnp.stack([zh, core, *which]).astype(jnp.int32), gathered, *weights)


def products_kernel(form, steps, at_ref, own_a, own_b, far_a, far_b, near, other, *outs):
    step = pl.program_id(0)

    def put(left, right):
        product = dot(left[...], near[0]) + dot(right[...], other[0])
        product = product.astype(jnp.bfloat16)
        for i in range(steps):

            @pl.when(step == i)
            def _():
                if form == "joined":
                    outs[0][i * 128 : i * 128 + 128] = product[:128]
                    outs[1][i * 128 : i * 128 + 128] = product[128:]
                elif form == "halves":
                    outs[2 * i][...] = product[:128]
                    outs[2 * i + 1][...] = product[128:]
                else:
                    outs[i][...] = product

    @pl.when(at_ref[steps + step] == 1)
    def _():
        put(own_a, own_b)

    @pl.when(at_ref[steps + step] == 0)
    def _():
        put(far_a, far_b)


def products(targets, zh, attended, near, other, form="whole"):
    steps = len(targets)
    blocks = [zt * 2 + xt // 2 for zt, xt in targets]
    owns = [xt % 2 == zh for _, xt in targets]
    at = jnp.stack([v.astype(jnp.int32) for v in blocks + owns])
    rows = pl.BlockSpec((HALF, 512), lambda i, at: (0, 0))
    block = pl.BlockSpec((1, 512, 1024), lambda i, at: (at[i], 0, 0))
    count = {"joined": 2, "halves": 2 * steps, "whole": steps}[form]
    size = 128 if form == "halves" else HALF
    return pl.pallas_call(
        lambda *refs: products_kernel(form, steps, *refs),
        grid_spec=pltpu.PrefetchScalarGridSpec(
            num_scalar_prefetch=1,
            grid=(steps,),
            in_specs=[rows] * 4 + [block] * 2,
            out_specs=[pl.BlockSpec((size, 1024), lambda i, at: (0, 0))] * count,
        ),
        out_shape=[jax.ShapeDtypeStruct((size, 1024), jnp.bfloat16)] * count,
        compiler_params=WIDE_GRANT,
    )(at, *attended, near, other)


def add_rows(value, arrived, start):
    rows = arrived.shape[0]
    return lax.dynamic_update_slice(value, value[start : start + rows] + arrived, (start, 0))


def half_of(value, which, dim=0):
    size = value.shape[dim] // 2
    return lax.dynamic_slice_in_dim(value, which * size, size, dim)


def ordered(first, own, other, dim=0):
    return jnp.where(
        first, jnp.concatenate([own, other], dim), jnp.concatenate([other, own], dim)
    )


def dot(a, b):
    return jnp.dot(a, b, preferred_element_type=jnp.float32)


def local(tokens, norm_gain, query_weight, kv_weight, out_weight, lengths):
    core = lax.axis_index("core")
    chip = lax.axis_index(("zl", "x"))
    zl = lax.axis_index("zl")
    x = lax.axis_index("x")
    y = lax.axis_index("y")
    zh = lax.axis_index("zh")
    is_first = core == 0

    near_other = core_swap(query_weight)

    gain = lax.dynamic_slice_in_dim(norm_gain, (chip * 2 + core) * 512, 512, 0)
    wide = tokens.astype(jnp.float32)
    gained = (wide * gain[None, :]).astype(jnp.bfloat16)
    mine = send(half_of(gained, core), to_slice(0))
    theirs = send(half_of(gained, 1 - core), to_slice(1))
    block = ordered(is_first, mine, theirs, 1)

    kv_near = lax.dynamic_slice_in_dim(kv_weight, chip * 256, 256, 1)
    kv_own = lax.dynamic_slice_in_dim(kv_weight, chip * 256 + core * 128, 128, 1)
    near = jnp.concatenate([query_weight, kv_own], axis=1)
    slice_gain = 1.0 / lax.dynamic_slice_in_dim(norm_gain, y * 2048, 2048, 0)
    own_slots = core * HALF + jnp.arange(HALF, dtype=jnp.int32)
    slot_k = jnp.concatenate([own_slots, (1 - core) * HALF + jnp.arange(HALF, dtype=jnp.int32)])
    allowed = (slot_k[None, :] <= own_slots[:, None]) & (slot_k[None, :] < lengths[0])
    bias = jnp.where(allowed, 0.0, -jnp.inf).astype(jnp.float32)
    cosine, sine = rope_tables(own_slots)
    block, near_other, kv_near, near = lax.optimization_barrier((block, near_other, kv_near, near))
    block, slice_gain, bias, cosine, sine = lax.optimization_barrier(
        (block, slice_gain, bias, cosine, sine)
    )

    beside = zl_swap(block)
    left = x_shift(block, 1)
    right = x_shift(block, -1)
    left, right, beside = lax.optimization_barrier((left, right, beside))
    far = zh_swap(after(near, beside))
    beside_left = x_shift(beside, 1)
    beside_right = x_shift(beside, -1)
    opposite = jnp.concatenate([x_shift(left[:128], 1), x_shift(right[128:], -1)], 0)
    beside_opposite = jnp.concatenate(
        [x_shift(beside_left[:128], 1), x_shift(beside_right[128:], -1)], 0
    )
    weights = (query_weight, near_other, kv_near, far, core_swap(after(far, beside_opposite)))
    gathered = jnp.zeros((4, HALF, 2048), jnp.bfloat16)
    for dz, dx, part in (
        (0, 0, block),
        (0, 3, left),
        (0, 1, right),
        (1, 0, beside),
        (0, 2, opposite),
        (1, 3, beside_left),
        (1, 1, beside_right),
        (1, 2, beside_opposite),
    ):
        zs, xs = zl ^ dz, (x + dx) % 4
        gathered = lax.dynamic_update_slice(
            gathered, part[None], (zs * 2 + xs // 2, 0, (xs % 2) * 1024)
        )

    out_near = lax.all_gather(after(out_weight, block), "y", axis=0, tiled=False)

    squares = jnp.sum(jnp.square(gathered.astype(jnp.float32) * slice_gain), axis=-1)
    low, high = project([(y + 2) % 4], zh, core, gathered, weights, True)
    from_below = y_shift(low, 1)
    from_above = y_shift(high, -1)
    a_top, a_bottom, b_top, b_bottom = project(
        [(y + 1) % 4, (y + 3) % 4], zh, core, gathered, weights, True
    )
    from_below, from_above, a_top, b_bottom = lax.optimization_barrier(
        (from_below, from_above, a_top, b_bottom)
    )
    a_bottom, b_top = y_shift(a_bottom, 1), y_shift(b_top, -1)
    a_top, b_bottom = a_top + from_below, b_bottom + from_above
    gathered = after(gathered, (a_top, b_bottom, a_bottom, b_top))
    (kept,) = project([y], zh, core, gathered, weights)
    sums = (kept, y_shift(a_top, 1), a_bottom, b_top, y_shift(b_bottom, -1))

    squares, a_top, b_bottom = lax.optimization_barrier((squares, a_top, b_bottom))
    total = lax.dynamic_index_in_dim(squares, y, 0, keepdims=False)
    for k in (1, 2, 3):
        total += y_shift(lax.dynamic_index_in_dim(squares, (y + k) % 4, 0, keepdims=False), k)
    scale = lax.rsqrt(total / 8192.0 + norm_eps)[:, None]

    kv_rows = key_value_rows(core, sums, scale, cosine, sine)
    kv_other = core_swap(kv_rows)
    out_other = core_swap(after(out_near, kv_other))
    own_a = attention(0, sums, scale, cosine, sine, bias, kv_rows, kv_other)
    far_a = zh_swap(own_a)
    own_b = attention(1, sums, scale, cosine, sine, bias, kv_rows, kv_other)
    far_b = zh_swap(own_b)
    attended = (own_a, own_b, far_a, far_b)

    def made(moves, form="whole"):
        targets = [(zl ^ dz, (x + dx) % 4) for dz, dx in moves]
        return products(targets, zh, attended, out_near, out_other, form)

    low, high = made([(1, 2), (0, 2)], "joined")
    from_left, from_right = x_shift(low, 1), x_shift(high, -1)
    a_top, a_bottom, b_top, b_bottom = made([(1, 1), (1, 3)], "halves")
    here_a, here_b, beside, mixed = made([(0, 1), (0, 3), (1, 0), (0, 0)])
    from_left, from_right, here_a, here_b = lax.optimization_barrier(
        (from_left, from_right, here_a, here_b)
    )
    a_bottom, b_top = x_shift(a_bottom, 1), x_shift(b_top, -1)
    a_top, b_bottom = a_top + from_left[:128], b_bottom + from_right[:128]
    here_a, here_b, a_top, b_bottom = lax.optimization_barrier((here_a, here_b, a_top, b_bottom))
    a_top, b_bottom = x_shift(a_top, 1), x_shift(b_bottom, -1)
    here_a = x_shift(add_rows(here_a, from_left[128:], 0), 1)
    here_b = x_shift(add_rows(here_b, from_right[128:], 128), -1)

    def sum_of(*values):
        return sum(v.astype(jnp.float32) for v in values).astype(jnp.bfloat16)

    across = zl_swap(summed_up(beside, a_top, a_bottom, b_top, b_bottom))
    mixed = sum_of(mixed, here_a, here_b, across)
    keep = send(half_of(mixed, core, 1), to_home(0))
    got = send(half_of(mixed, 1 - core, 1), to_home(1))
    return (wide + ordered(is_first, keep, got, 0).astype(jnp.float32)).astype(jnp.bfloat16)


def solution(mesh):
    split = Mesh(mesh.devices.reshape(SIZES), AXES)
    gx, gy = ("zl", "x", "core"), ("y", "zh")
    placed = (P(gy, gx), P(), P(gy, gx), P(gy, None), P(gx, gy), P(gy))
    return jax.shard_map(
        local, mesh=split, in_specs=placed, out_specs=P(gy, gx), check_vma=False
    )
```
